128 devices in a mesh: bx: 8 (over y, z_hi), by: 16 (over x, z_lo, core).
Axes of the slice: x: 4, y: 4, z: 4 (z_hi: 2, z_lo: 2; z = z_hi * 2 + z_lo), core: 2. Of those that a mesh axis runs over, the one named last changes fastest.
Arguments:
- populations: float32 [27, 128, 256, 128], P(None, 'bx', 'by'), as said below
- block_level: int32 [1024], replicated, may hold values 0 or 1
- new_slot: int32 [1024], P(('bx', 'by')), may hold values from 0 to 1023, as said below
Outputs:
- density: float32 [1024, 4096], P(('bx', 'by'))
- velocity: float32 [3, 1024, 4096], P(None, ('bx', 'by'))
The draws below stay inside these ranges and needn't reach their ends.
Inputs may be any that keep to these rules, and one draw needn't show every extreme that they name: `populations`: every population is positive. new_slot is a permutation; slot s belongs to device s // 8 in the curve order, which is the order of bx+by. Every block stays at its slot or moves to the next or the previous device in that order; at most one block of a device goes to each of those two devices, and it takes the slot of the block that crosses the same cut the other way. Some cut is crossed in every draw.
All inputs are finite; a program needn't handle non-finite values.
Results may differ from the reference program's by a relative error of at most 0.0003.
Values sent between devices are 32-bit elements; how exact they have to be, the bound alone decides.
No kernel may reach another device: no remote copies, remote signals or barrier semaphores. Data moves between devices by JAX's collectives and lax.ppermute only.
A program may use at most 192 MiB of HBM per device.

```python
import math
import jax
import jax.numpy as jnp
import numpy as np
from jax import lax

BLK_EDGE = 16
BLK_DEV = 8
STEPS = 1
NX = 128
NY = 256
NZ = 128
NBLK = 1024
CELLS = 4096
N_BX = 8
N_BY = 16


def draw_populations(key, part):
    key = jax.random.fold_in(key, 5)
    key_rho, key_vel, key_noise = jax.random.split(key, 3)
    shape = (NX, NY, NZ)
    density = jax.random.uniform(key_rho, shape, jnp.float32, 0.8, 1.2)
    velocity = 0.04 * jnp.clip(jax.random.normal(key_vel, (3,) + shape, jnp.float32), -3.0, 3.0)
    table = np.array([[first, second, third] for first in (-1, 0, 1) for second in (-1, 0, 1) for third in (-1, 0, 1)], dtype=np.float32)
    squares = np.sum(table * table, axis=1)
    weights = np.where(squares == 0, 8.0 / 27, np.where(squares == 1, 2.0 / 27, np.where(squares == 2, 1.0 / 54, 1.0 / 216))).astype(np.float32)
    comp_x = jnp.asarray(table[:, 0]).reshape(27, 1, 1, 1)
    comp_y = jnp.asarray(table[:, 1]).reshape(27, 1, 1, 1)
    comp_z = jnp.asarray(table[:, 2]).reshape(27, 1, 1, 1)
    projected = comp_x * velocity[0] + comp_y * velocity[1] + comp_z * velocity[2]
    speed_sq = velocity[0] * velocity[0] + velocity[1] * velocity[1] + velocity[2] * velocity[2]
    balance = jnp.asarray(weights).reshape(27, 1, 1, 1) * density * (1.0 + 3.0 * projected + 4.5 * projected * projected - 1.5 * speed_sq)
    noise = jax.random.uniform(key_noise, (27,) + shape, jnp.float32, -0.15, 0.15)
    return (balance * (1.0 + noise)).astype(jnp.float32)


def draw_new_slot(key, part):
    key = jax.random.fold_in(key, 11)
    key_cut, key_slots, key_force = jax.random.split(key, 3)
    devices = NBLK // BLK_DEV
    cut_on = jax.random.randint(key_cut, (devices - 1,), 0, 2)
    forced = jax.random.randint(key_force, (), 0, devices - 1)
    cut_on = jnp.where(jnp.arange(devices - 1) == forced, 1, cut_on)
    orders = jax.vmap(lambda single: jax.random.permutation(single, BLK_DEV))(jax.random.split(key_slots, devices))
    left_slot = orders[:, 0]
    right_slot = orders[:, 1]
    cuts = jnp.arange(devices - 1, dtype=jnp.int32)
    lower = cuts * BLK_DEV + right_slot[:-1]
    upper = (cuts + 1) * BLK_DEV + left_slot[1:]
    base = jnp.arange(NBLK, dtype=jnp.int32)
    moved = base.at[lower].set(jnp.where(cut_on == 1, upper, lower))
    moved = moved.at[upper].set(jnp.where(cut_on == 1, lower, upper))
    return moved.astype(jnp.int32)


def touch_ends(result, stream_key, low, top_value):
    longest = result.shape.index(max(result.shape))
    spots = []
    for shift in (0, 1):
        where = [jax.random.randint(jax.random.fold_in(stream_key, axis), (), 0, length) for axis, length in enumerate(result.shape)]
        where[longest] = (where[longest] + shift) % result.shape[longest]
        spots.append(tuple(where))
    return result.at[spots[0]].set(low).at[spots[1]].set(top_value)


def setup_inputs(seed: int = 0) -> dict:
    seeds = jax.random.split(jax.random.key(seed), 4)
    return {
        "populations": draw_populations(jax.random.fold_in(seeds[3], 71), 0),
        "block_level": touch_ends((jax.random.randint(seeds[1], (NBLK,), 0, 5) < 1).astype(jnp.int32), jax.random.fold_in(seeds[1], 1), 0, 1),
        "new_slot": draw_new_slot(jax.random.fold_in(seeds[3], 71), 0),
    }


lattice_vel = np.array([[first, second, third] for first in (-1, 0, 1) for second in (-1, 0, 1) for third in (-1, 0, 1)], dtype=np.float32)
lattice_sq = np.sum(lattice_vel * lattice_vel, axis=1)
lattice_wts = np.where(lattice_sq == 0, 8.0 / 27, np.where(lattice_sq == 1, 2.0 / 27, np.where(lattice_sq == 2, 1.0 / 54, 1.0 / 216))).astype(np.float32)
stress_table = np.stack([lattice_vel[:, first] * lattice_vel[:, second] for first in range(3) for second in range(3)]).astype(np.float32)
tau_coarse = 0.56
tau_fine = 0.62
scale_to_fine = tau_fine / (2.0 * tau_coarse)
scale_to_coarse = 2.0 * tau_coarse / tau_fine
smagorinsky = 18.0 * math.sqrt(2.0) * 0.17 * 0.17

def cell_moments(states):
    density = lax.optimization_barrier(jnp.sum(states, axis=0))
    momentum = jnp.einsum('ia,i...->a...', jnp.asarray(lattice_vel), states, precision=lax.Precision.HIGHEST)
    return (density, momentum / density)

def equilibrium(density, velocity):
    projected = jnp.einsum('ia,a...->i...', jnp.asarray(lattice_vel), velocity, precision=lax.Precision.HIGHEST)
    speed_sq = lax.optimization_barrier(jnp.sum(velocity * velocity, axis=0))
    weights = jnp.asarray(lattice_wts).reshape((27,) + (1,) * density.ndim)
    return weights * density * (1.0 + 3.0 * projected + 4.5 * projected * projected - 1.5 * speed_sq)

def relax_cells(states, fine_cells, active_cells):
    density, velocity = cell_moments(states)
    balance = equilibrium(density, velocity)
    departure = states - balance
    stress = jnp.einsum('ki,i...->k...', jnp.asarray(stress_table), departure, precision=lax.Precision.HIGHEST)
    stress_norm = jnp.sqrt(lax.optimization_barrier(jnp.sum(stress * stress, axis=0)))
    base_time = jnp.where(fine_cells, tau_fine, tau_coarse)
    relax_time = 0.5 * (base_time + jnp.sqrt(base_time * base_time + smagorinsky * stress_norm / density))
    relaxed = jnp.where(active_cells, states - departure / relax_time, states)
    factor = jnp.where(fine_cells, scale_to_coarse, scale_to_fine)
    rescaled = balance + factor * (relaxed - balance)
    return (relaxed, rescaled)

def reference(populations, block_level, new_slot):
    levels = block_level.reshape(N_BX, N_BY, BLK_DEV)
    cell_level = jnp.repeat(jnp.repeat(jnp.repeat(levels, BLK_EDGE, 0), BLK_EDGE, 1), BLK_EDGE, 2)
    fine_cells = cell_level == 1
    crossing = jnp.stack([jnp.roll(cell_level, (-int(offset[0]), -int(offset[1]), -int(offset[2])), axis=(0, 1, 2)) != cell_level for offset in lattice_vel])
    every = jnp.ones_like(fine_cells)
    state = populations
    for step in range(STEPS):
        for substep in range(2):
            active_cells = fine_cells if substep == 0 else every
            relaxed, rescaled = relax_cells(state, fine_cells, active_cells)
            outgoing = jnp.where(crossing, rescaled, relaxed)
            read = jnp.stack([jnp.roll(outgoing[direction], (int(lattice_vel[direction][0]), int(lattice_vel[direction][1]), int(lattice_vel[direction][2])), axis=(0, 1, 2)) for direction in range(27)])
            state = jnp.where(active_cells, read, state)
    density, velocity = cell_moments(state)
    fields = jnp.concatenate([density[None], velocity], axis=0)
    fields = fields.reshape(4, N_BX, BLK_EDGE, N_BY, BLK_EDGE, BLK_DEV, BLK_EDGE)
    fields = fields.transpose(0, 1, 3, 5, 2, 4, 6).reshape(4, NBLK, CELLS)
    placed = jnp.zeros_like(fields).at[:, new_slot].set(fields)
    return (placed[0], placed[1:4])
```

```python
import math

import jax
import jax.numpy as jnp
import numpy as np
from jax import lax
from jax.experimental import pallas as pl
from jax.experimental.pallas import tpu as pltpu
from jax.sharding import PartitionSpec as P

tau_coarse = 0.56
tau_fine = 0.62
scale_to_fine = tau_fine / (2.0 * tau_coarse)
scale_to_coarse = 2.0 * tau_coarse / tau_fine
smagorinsky = 18.0 * math.sqrt(2.0) * 0.17 * 0.17
weights = (8.0 / 27, 2.0 / 27, 1.0 / 54, 1.0 / 216)
ROWS = 8
LANES = 128
VMEM_BYTES = 56 * 1024 * 1024


def comp(a, b, e):
    return 9 * (a + 1) + 3 * (b + 1) + (e + 1)


def face(b, e):
    return 3 * (b + 1) + (e + 1)


DIRS = [(a, b, e) for a in (-1, 0, 1) for b in (-1, 0, 1) for e in (-1, 0, 1)]
HALF = [c for c in DIRS if c > (0, 0, 0)]


def lane_block(edge):
    return lax.broadcasted_iota(jnp.int32, (ROWS, LANES), 1) // edge


def sublane():
    return lax.broadcasted_iota(jnp.int32, (ROWS, LANES), 0)


def column_level(levels, shape, blocks, dx, dy):
    count_x, count_y = shape
    ix = lax.rem(lax.axis_index("bx") + (dx + count_x), count_x)
    iy = lax.rem(lax.axis_index("by") + (dy + count_y), count_y)
    base = (ix * count_y + iy) * blocks
    block = lane_block(LANES // blocks)
    value = jnp.full((ROWS, LANES), levels[base], jnp.int32)
    for k in range(1, blocks):
        value = jnp.where(block == k, levels[base + k], value)
    return value


def lane_roll(tile, by):
    return tile if by == 0 else pltpu.roll(tile, by % LANES, 1)


def collide(get, fine, everywhere, factor, put, dirs=None):
    total, diff, quad = {}, {}, {}
    for a in (-1, 0, 1):
        for b in (-1, 0, 1):
            low, mid, high = (get((a, b, e)) for e in (-1, 0, 1))
            both = low + high
            total[a, b] = both + mid
            diff[a, b] = high - low
            quad[a, b] = both
    ta, tb, tbb, da, db, qa = {}, {}, {}, {}, {}, {}
    for a in (-1, 0, 1):
        both = total[a, -1] + total[a, 1]
        tbb[a] = both
        ta[a] = both + total[a, 0]
        tb[a] = total[a, 1] - total[a, -1]
        da[a] = diff[a, -1] + diff[a, 0] + diff[a, 1]
        db[a] = diff[a, 1] - diff[a, -1]
        qa[a] = quad[a, -1] + quad[a, 0] + quad[a, 1]
    pxx = ta[-1] + ta[1]
    rho = pxx + ta[0]
    jx = ta[1] - ta[-1]
    jy = tb[-1] + tb[0] + tb[1]
    jz = da[-1] + da[0] + da[1]
    pyy = tbb[-1] + tbb[0] + tbb[1]
    pzz = qa[-1] + qa[0] + qa[1]
    pxy = tb[1] - tb[-1]
    pxz = da[1] - da[-1]
    pyz = db[-1] + db[0] + db[1]
    inv = 1.0 / rho
    ux, uy, uz = jx * inv, jy * inv, jz * inv
    third = rho * (1.0 / 3.0)
    pxx = pxx - third - jx * ux
    pyy = pyy - third - jy * uy
    pzz = pzz - third - jz * uz
    pxy = pxy - jx * uy
    pxz = pxz - jx * uz
    pyz = pyz - jy * uz
    norm = jnp.sqrt(
        pxx * pxx + pyy * pyy + pzz * pzz + 2.0 * (pxy * pxy + pxz * pxz + pyz * pyz)
    )
    base_time = jnp.where(fine, tau_fine, tau_coarse)
    tau = 0.5 * (base_time + jnp.sqrt(base_time * base_time + smagorinsky * norm * inv))
    keep = 1.0 - 1.0 / tau
    if not everywhere:
        keep = jnp.where(fine, keep, 1.0)
    base = 1.0 - 1.5 * (ux * ux + uy * uy + uz * uz)
    scaled = [rho * w for w in weights]
    rest = [s * base for s in scaled]
    vx, vy, vz = 3.0 * ux, 3.0 * uy, 3.0 * uz
    vel = {(0, 0, 1): vz, (0, 1, 0): vy, (1, 0, 0): vx}
    vel[0, 1, 1], vel[0, 1, -1] = vy + vz, vy - vz
    vel[1, 0, 1], vel[1, 0, -1] = vx + vz, vx - vz
    vel[1, 1, 0], vel[1, -1, 0] = vx + vy, vx - vy
    for b in (-1, 1):
        for e in (-1, 1):
            vel[1, b, e] = vel[1, b, 0] + (vz if e > 0 else -vz)

    def emit(c, balance):
        if dirs is not None and c not in dirs:
            return
        gain = keep if c == (0, 0, 0) else keep * factor(c)
        put(c, balance + gain * (get(c) - balance))

    emit((0, 0, 0), rest[0])
    for c in HALF:
        n = sum(abs(k) for k in c)
        odd = scaled[n] * vel[c]
        even = rest[n] + 0.5 * odd * vel[c]
        emit(c, even + odd)
        emit(tuple(-k for k in c), even - odd)


def level_factor(here, there_rows, e):
    scale = jnp.where(here == 1, scale_to_coarse, scale_to_fine)
    return jnp.where(lane_roll(there_rows, -e) != here, scale, 1.0)


def fill_factors(levels, shape, blocks, table):
    lev = {
        (dx, dy): column_level(levels, shape, blocks, dx, dy)
        for dx in (-1, 0, 1)
        for dy in (-1, 0, 1)
    }
    row = sublane()
    for k, (own, dx) in enumerate(((0, -1), (0, 0), (0, 1), (-1, 0), (1, 0))):
        here = lev[own, 0]
        for e in (-1, 0, 1):
            plain = level_factor(here, lev[dx, 0], e)
            for b in (-1, 0, 1):
                low, high = plain, plain
                if b == -1:
                    low = jnp.where(row == 0, level_factor(here, lev[dx, -1], e), plain)
                if b == 1:
                    high = jnp.where(row == ROWS - 1, level_factor(here, lev[dx, 1], e), plain)
                table[k, b + 1, e + 1, 0:8, :] = low
                table[k, b + 1, e + 1, 8:16, :] = high


def x_side(a, x, last):
    if a == 0:
        return 1
    return jnp.where(x == (0 if a < 0 else last), 1 + a, 1)


def store_by_parity(odd, first, second, up, down):
    @pl.when(odd == 0)
    def _():
        first[...] = up[...]
        second[...] = down[...]

    @pl.when(odd == 1)
    def _():
        first[...] = down[...]
        second[...] = up[...]


def start_kernel(shape, blocks, levels, f, out, table, pay_a, pay_b, up, down):
    fill_factors(levels, shape, blocks, table)
    fine = column_level(levels, shape, blocks, 0, 0) == 1
    last = f.shape[1] - 1

    def layer(x, carry):
        for h in (0, 1):
            rows = slice(8 * h, 8 * h + 8)

            def put(c, value):
                a, b, e = c
                out[comp(*c), x, rows, :] = value
                if b == 1 and h == 1:
                    up[face(a, e), pl.ds(x, 1), :] = value[7:8]
                if b == -1 and h == 0:
                    down[face(a, e), pl.ds(x, 1), :] = value[0:1]

            collide(
                lambda c: f[comp(*c), x, rows, :],
                fine,
                False,
                lambda c: table[x_side(c[0], x, last), c[1] + 1, c[2] + 1, rows, :],
                put,
            )
        return carry

    lax.fori_loop(0, f.shape[1], layer, 0)
    store_by_parity(lax.rem(lax.axis_index("by"), 2), pay_a, pay_b, up, down)


def shifted_read(g, above, below, row, c, x, h):
    a, b, e = c
    i = comp(a, b, e)
    if b == 0:
        tile = g[i, x, 8 * h : 8 * h + 8, :]
    elif b == 1:
        if h == 1:
            tile = g[i, x, 7:15, :]
        else:
            tile = pltpu.roll(g[i, x, 0:8, :], 1, 0)
            tile = jnp.where(row == 0, below[face(a, e), pl.ds(x, 1), :], tile)
    else:
        if h == 0:
            tile = g[i, x, 1:9, :]
        else:
            tile = pltpu.roll(g[i, x, 8:16, :], 7, 0)
            tile = jnp.where(row == 7, above[face(a, e), pl.ds(x, 1), :], tile)
    return lane_roll(tile, e)


def load_by_parity(odd, first, second, above, below):
    @pl.when(odd == 0)
    def _():
        above[...] = first[...]
        below[...] = second[...]

    @pl.when(odd == 1)
    def _():
        above[...] = second[...]
        below[...] = first[...]


def side_kernel(shape, blocks, levels, f, g, got_a, got_b, pay_a, pay_b, above, below, up, down):
    load_by_parity(lax.rem(lax.axis_index("by"), 2), got_a, got_b, above, below)
    fine = column_level(levels, shape, blocks, 0, 0) == 1
    row = sublane()
    last = f.shape[1] - 1
    for ad, edge, inner, pay in ((1, last, last - 1, up), (-1, 0, 1, down)):
        for h in (0, 1):
            rows = slice(8 * h, 8 * h + 8)
            for b in (-1, 0, 1):
                for e in (-1, 0, 1):
                    j = face(b, e)
                    same, flat, back = (ad, b, e), (0, b, e), (-ad, b, e)
                    pay[j, rows, :] = shifted_read(g, above, below, row, same, edge, h)
                    pay[9 + j, rows, :] = jnp.where(
                        fine,
                        shifted_read(g, above, below, row, same, inner, h),
                        f[comp(*same), edge, rows, :],
                    )
                    pay[18 + j, rows, :] = jnp.where(
                        fine,
                        shifted_read(g, above, below, row, flat, edge, h),
                        f[comp(*flat), edge, rows, :],
                    )
                    pay[27 + j, rows, :] = f[comp(*back), edge, rows, :]
    store_by_parity(lax.rem(lax.axis_index("bx"), 2), pay_a, pay_b, up, down)


def body_kernel(
    shape, blocks, levels, f, g, table, ya, yb, xa, xb, out, pay_a, pay_b,
    above, below, right, left, state, sums, up, down,
):
    odd_x = lax.rem(lax.axis_index("bx"), 2)
    odd_y = lax.rem(lax.axis_index("by"), 2)
    load_by_parity(odd_y, ya, yb, above, below)
    load_by_parity(odd_x, xa, xb, right, left)
    fine = {dx: column_level(levels, shape, blocks, dx, 0) == 1 for dx in (-1, 0, 1)}
    row = sublane()
    last = f.shape[1] - 1

    def read(c, x, h):
        return shifted_read(g, above, below, row, c, x, h)

    def finish(x, h, mask, factor, dirs, slot):
        rows = slice(8 * h, 8 * h + 8)
        made = {}

        def put(c, value):
            made[c] = value

        collide(lambda c: state[comp(*c), rows, :], mask, True, factor, put, dirs)
        for a in (-1, 0, 1):
            if dirs is not None and (a, 0, 0) not in dirs:
                continue
            for b in (-1, 0, 1):
                plus = lane_roll(made[a, b, 1], 1)
                minus = lane_roll(made[a, b, -1], -1)
                sums[a + 1, b + 1, 0, slot, rows, :] = made[a, b, 0] + (plus + minus)
                sums[a + 1, b + 1, 1, slot, rows, :] = plus - minus

    def own(x, skip):
        for h in (0, 1):
            rows = slice(8 * h, 8 * h + 8)
            for c in DIRS:
                a, b, e = c
                if a == skip == 1:
                    tile = left[face(b, e), rows, :]
                elif a == skip == -1:
                    tile = right[face(b, e), rows, :]
                else:
                    tile = read(c, x - a, h)
                state[comp(*c), rows, :] = jnp.where(fine[0], tile, f[comp(*c), x, rows, :])
            dirs = None if skip == 0 else [c for c in DIRS if c[0] != -skip]
            finish(
                x, h, fine[0],
                lambda c: table[
                    1 + (c[0] if skip == -c[0] else 0), c[1] + 1, c[2] + 1, rows, :
                ],
                dirs, x + 1,
            )

    def halo(side, slot, pay, edge, k):
        for h in (0, 1):
            rows = slice(8 * h, 8 * h + 8)
            for b in (-1, 0, 1):
                for e in (-1, 0, 1):
                    j = face(b, e)
                    state[comp(-side, b, e), rows, :] = pay[9 + j, rows, :]
                    state[comp(0, b, e), rows, :] = pay[18 + j, rows, :]
                    state[comp(side, b, e), rows, :] = jnp.where(
                        fine[side], read((side, b, e), edge, h), pay[27 + j, rows, :]
                    )
            finish(
                0, h, fine[side],
                lambda c: table[k, c[1] + 1, c[2] + 1, rows, :],
                [c for c in DIRS if c[0] == -side], slot,
            )

    def layer(x, carry):
        own(x, 0)
        return carry

    lax.fori_loop(1, last, layer, 0)
    own(0, 1)
    own(last, -1)
    halo(-1, 0, left, 0, 3)
    halo(1, last + 2, right, last, 4)

    def gather(x, carry):
        for h in (0, 1):
            rows = slice(8 * h, 8 * h + 8)
        total, cross, along = {}, {}, {}
        for b in (-1, 0, 1):
            for h in (0, 1):
                rows = slice(8 * h, 8 * h + 8)
                low = sums[2, b + 1, 0, x, rows, :]
                mid = sums[1, b + 1, 0, x + 1, rows, :]
                high = sums[0, b + 1, 0, x + 2, rows, :]
                total[b, h] = low + mid + high
                cross[b, h] = low - high
                along[b, h] = (
                    sums[2, b + 1, 1, x, rows, :]
                    + sums[1, b + 1, 1, x + 1, rows, :]
                    + sums[0, b + 1, 1, x + 2, rows, :]
                )
        for n, part in enumerate((total, cross, along)):
            up[n, pl.ds(x, 1), :] = part[1, 1][7:8]
            down[n, pl.ds(x, 1), :] = part[-1, 0][0:1]
            rise = [pltpu.roll(part[1, h], 1, 0) for h in (0, 1)]
            fall = [pltpu.roll(part[-1, h], 7, 0) for h in (0, 1)]
            rise = [jnp.where(row == 0, 0.0, rise[0]), jnp.where(row == 0, rise[0], rise[1])]
            fall = [jnp.where(row == 7, fall[1], fall[0]), jnp.where(row == 7, 0.0, fall[1])]
            for h in (0, 1):
                rows = slice(8 * h, 8 * h + 8)
                out[(0, 1, 3)[n], x, rows, :] = part[0, h] + rise[h] + fall[h]
                if n == 0:
                    out[2, x, rows, :] = rise[h] - fall[h]
        return carry

    lax.fori_loop(0, last + 1, gather, 0)
    store_by_parity(odd_y, pay_a, pay_b, up, down)


def block_rows(tile, reflect, turn):
    tile = pltpu.roll(tile, 0, 1, stride=LANES // 8, stride_axis=0)
    tile = jnp.take_along_axis(tile, reflect, axis=0)
    return jnp.take_along_axis(tile, turn, axis=1)


def leaving(slots, blocks, step):
    here = lax.axis_index("bx") * lax.axis_size("by") + lax.axis_index("by")
    which = jnp.int32(-1)
    for k in range(blocks):
        which = jnp.where(slots[k] // blocks == here + step, k, which)
    return which


def moments_kernel(
    blocks, slots, part, got_a, got_b, rho_out, vel_out, pay_a, pay_b,
    above, below, made, up, down,
):
    odd = lax.rem(lax.axis_index("by"), 2)
    load_by_parity(odd, got_a, got_b, above, below)
    row = sublane()
    group = lane_block(LANES // 8)
    reflect = (group - row) & 7
    turn = (lane_block(1) + row * (LANES // 8)) & (LANES - 1)

    def layer(x, carry):
        for h in (0, 1):
            rows = slice(8 * h, 8 * h + 8)
            edge, halo, sign = (0, below, 1.0) if h == 0 else (7, above, -1.0)
            total, cross, along = (halo[n, pl.ds(x, 1), :] for n in range(3))
            values = []
            for n, extra in enumerate((total, cross, sign * total, along)):
                values.append(part[n, x, rows, :] + jnp.where(row == edge, extra, 0.0))
            inv = 1.0 / values[0]
            for n in range(4):
                tile = values[0] if n == 0 else values[n] * inv
                tile = block_rows(tile, reflect, turn)
                made[2 * n + h, pl.ds(x * 8, 8), :] = tile
        return carry

    lax.fori_loop(0, part.shape[1], layer, 0)
    for x in range(part.shape[1]):
        for h in (0, 1):
            lanes = slice((2 * x + h) * LANES, (2 * x + h + 1) * LANES)
            rho_out[:, lanes] = made[h, 8 * x : 8 * x + 8, :]
            for n in range(3):
                vel_out[n, :, lanes] = made[2 * n + 2 + h, 8 * x : 8 * x + 8, :]
    for step, pay in ((1, up), (-1, down)):
        which = jnp.maximum(leaving(slots, blocks, step), 0)
        for n in range(8):
            pay[n, :, :] = made[n, pl.ds(which, part.shape[1], stride=8), :]
    store_by_parity(odd, pay_a, pay_b, up, down)


def place_kernel(blocks, slots, rho, vel, got_a, got_b, rho_out, vel_out, after, before):
    odd = lax.rem(lax.axis_index("by"), 2)
    load_by_parity(odd, got_a, got_b, after, before)
    row = sublane()
    to_next = row == leaving(slots, blocks, 1)
    to_prev = row == leaving(slots, blocks, -1)
    for x in range(after.shape[1]):
        for h in (0, 1):
            lanes = slice((2 * x + h) * LANES, (2 * x + h + 1) * LANES)
            for n in range(4):
                k = 2 * n + h
                tile = rho[:, lanes] if n == 0 else vel[n - 1, :, lanes]
                tile = jnp.where(to_next, after[k, x : x + 1, :], tile)
                tile = jnp.where(to_prev, before[k, x : x + 1, :], tile)
                if n == 0:
                    rho_out[:, lanes] = tile
                else:
                    vel_out[n - 1, :, lanes] = tile


def swap(value, axis, odd, curve=False):
    count_x, count_y = lax.axis_size("bx"), lax.axis_size("by")
    pairs = []
    if curve:
        pairs = [(j, j + 1) for j in range(odd, count_x * count_y - 1, 2)]
    elif axis == "by":
        for x in range(count_x):
            for y in range(odd, count_y, 2):
                pairs.append((x * count_y + y, x * count_y + (y + 1) % count_y))
    else:
        for y in range(count_y):
            for x in range(odd, count_x, 2):
                pairs.append((x * count_y + y, (x + 1) % count_x * count_y + y))
    pairs = pairs + [(b, a) for a, b in pairs]
    return lax.ppermute(value, ("bx", "by"), pairs)


def call(kernel, outs, specs, scratch, name):
    space = {"v": pltpu.VMEM, "s": pltpu.SMEM}
    return pl.pallas_call(
        kernel,
        out_shape=[jax.ShapeDtypeStruct(s, jnp.float32) for s in outs],
        in_specs=[pl.BlockSpec(memory_space=space[k]) for k in specs],
        out_specs=[pl.BlockSpec(memory_space=pltpu.VMEM)] * len(outs),
        scratch_shapes=[pltpu.VMEM(s, jnp.float32) for s in scratch],
        compiler_params=pltpu.CompilerParams(vmem_limit_bytes=VMEM_BYTES),
        name=name,
    )


def on_device(populations, block_level, new_slot):
    shape = (lax.axis_size("bx"), lax.axis_size("by"))
    blocks = new_slot.shape[0]
    _, nx, ny, nz = populations.shape
    yface, xface, yedge, block = (9, nx, nz), (36, ny, nz), (3, nx, nz), (8, nx, nz)

    def start(*refs):
        start_kernel(shape, blocks, *refs)

    out, table, pay_a, pay_b = call(
        start,
        [populations.shape, (5, 3, 3, ny, nz), yface, yface],
        "sv",
        [yface, yface],
        "start",
    )(block_level, populations)
    ya, yb = swap(pay_a, "by", 0), swap(pay_b, "by", 1)

    def side(*refs):
        side_kernel(shape, blocks, *refs)

    pay_a, pay_b = call(
        side, [xface, xface], "svvvv", [yface, yface, xface, xface], "side"
    )(block_level, populations, out, ya, yb)
    xa, xb = swap(pay_a, "bx", 0), swap(pay_b, "bx", 1)

    def body(*refs):
        body_kernel(shape, blocks, *refs)

    part, pay_a, pay_b = call(
        body,
        [(4, nx, ny, nz), yedge, yedge],
        "svvvvvvv",
        [yface, yface, xface, xface, (27, ny, nz), (3, 3, 2, nx + 2, ny, nz), yedge, yedge],
        "body",
    )(block_level, populations, out, table, ya, yb, xa, xb)
    ya, yb = swap(pay_a, "by", 0), swap(pay_b, "by", 1)

    def moments(*refs):
        moments_kernel(blocks, *refs)

    cells = nx * ny * nz // blocks
    rho, vel, pay_a, pay_b = call(
        moments,
        [(blocks, cells), (3, blocks, cells), block, block],
        "svvv",
        [yedge, yedge, (8, nx * 8, nz), block, block],
        "moments",
    )(new_slot, part, ya, yb)
    ma, mb = swap(pay_a, "by", 0, True), swap(pay_b, "by", 1, True)

    def place(*refs):
        place_kernel(blocks, *refs)

    return tuple(
        call(place, [(blocks, cells), (3, blocks, cells)], "svvvv", [block, block], "place")(
            new_slot, rho, vel, ma, mb
        )
    )


def solution(mesh):
    in_specs = (P(None, "bx", "by", None), P(), P(("bx", "by")))
    out_specs = (P(("bx", "by"), None), P(None, ("bx", "by"), None))
    return jax.shard_map(
        on_device, mesh=mesh, in_specs=in_specs, out_specs=out_specs, check_vma=False
    )
```

```python
import math

import jax
import jax.numpy as jnp
import numpy as np
from jax import lax
from jax.experimental import pallas as pl
from jax.experimental.pallas import tpu as pltpu
from jax.sharding import PartitionSpec as P

tau_coarse = 0.56
tau_fine = 0.62
scale_to_fine = tau_fine / (2.0 * tau_coarse)
scale_to_coarse = 2.0 * tau_coarse / tau_fine
smagorinsky = 18.0 * math.sqrt(2.0) * 0.17 * 0.17
weights = (8.0 / 27, 2.0 / 27, 1.0 / 54, 1.0 / 216)
ROWS = 8
LANES = 128
VMEM_BYTES = 16 * 1024 * 1024


def comp(a, b, e):
    return 9 * (a + 1) + 3 * (b + 1) + (e + 1)


def face(b, e):
    return 3 * (b + 1) + (e + 1)


DIRS = [(a, b, e) for a in (-1, 0, 1) for b in (-1, 0, 1) for e in (-1, 0, 1)]
HALF = [c for c in DIRS if c > (0, 0, 0)]


def lane_block(edge):
    return lax.broadcasted_iota(jnp.int32, (ROWS, LANES), 1) // edge


def sublane():
    return lax.broadcasted_iota(jnp.int32, (ROWS, LANES), 0)


def column_level(levels, shape, blocks, dx, dy):
    count_x, count_y = shape
    ix = lax.rem(lax.axis_index("bx") + (dx + count_x), count_x)
    iy = lax.rem(lax.axis_index("by") + (dy + count_y), count_y)
    base = (ix * count_y + iy) * blocks
    block = lane_block(LANES // blocks)
    value = jnp.full((ROWS, LANES), levels[base], jnp.int32)
    for k in range(1, blocks):
        value = jnp.where(block == k, levels[base + k], value)
    return value


def lane_roll(tile, by):
    return tile if by == 0 else pltpu.roll(tile, by % LANES, 1)


def collide(get, fine, everywhere, factor, put, dirs=None):
    total, diff, quad = {}, {}, {}
    for a in (-1, 0, 1):
        for b in (-1, 0, 1):
            low, mid, high = (get((a, b, e)) for e in (-1, 0, 1))
            both = low + high
            total[a, b] = both + mid
            diff[a, b] = high - low
            quad[a, b] = both
    ta, tb, tbb, da, db, qa = {}, {}, {}, {}, {}, {}
    for a in (-1, 0, 1):
        both = total[a, -1] + total[a, 1]
        tbb[a] = both
        ta[a] = both + total[a, 0]
        tb[a] = total[a, 1] - total[a, -1]
        da[a] = diff[a, -1] + diff[a, 0] + diff[a, 1]
        db[a] = diff[a, 1] - diff[a, -1]
        qa[a] = quad[a, -1] + quad[a, 0] + quad[a, 1]
    pxx = ta[-1] + ta[1]
    rho = pxx + ta[0]
    jx = ta[1] - ta[-1]
    jy = tb[-1] + tb[0] + tb[1]
    jz = da[-1] + da[0] + da[1]
    pyy = tbb[-1] + tbb[0] + tbb[1]
    pzz = qa[-1] + qa[0] + qa[1]
    pxy = tb[1] - tb[-1]
    pxz = da[1] - da[-1]
    pyz = db[-1] + db[0] + db[1]
    inv = 1.0 / rho
    ux, uy, uz = jx * inv, jy * inv, jz * inv
    third = rho * (1.0 / 3.0)
    pxx = pxx - third - jx * ux
    pyy = pyy - third - jy * uy
    pzz = pzz - third - jz * uz
    pxy = pxy - jx * uy
    pxz = pxz - jx * uz
    pyz = pyz - jy * uz
    norm = jnp.sqrt(
        pxx * pxx + pyy * pyy + pzz * pzz + 2.0 * (pxy * pxy + pxz * pxz + pyz * pyz)
    )
    base_time = jnp.where(fine, tau_fine, tau_coarse)
    tau = 0.5 * (base_time + jnp.sqrt(base_time * base_time + smagorinsky * norm * inv))
    keep = 1.0 - 1.0 / tau
    if not everywhere:
        keep = jnp.where(fine, keep, 1.0)
    base = 1.0 - 1.5 * (ux * ux + uy * uy + uz * uz)
    scaled = [rho * w for w in weights]
    rest = [s * base for s in scaled]
    vx, vy, vz = 3.0 * ux, 3.0 * uy, 3.0 * uz
    vel = {(0, 0, 1): vz, (0, 1, 0): vy, (1, 0, 0): vx}
    vel[0, 1, 1], vel[0, 1, -1] = vy + vz, vy - vz
    vel[1, 0, 1], vel[1, 0, -1] = vx + vz, vx - vz
    vel[1, 1, 0], vel[1, -1, 0] = vx + vy, vx - vy
    for b in (-1, 1):
        for e in (-1, 1):
            vel[1, b, e] = vel[1, b, 0] + (vz if e > 0 else -vz)

    def emit(c, balance):
        if dirs is not None and c not in dirs:
            return
        gain = keep if c == (0, 0, 0) else keep * factor(c)
        put(c, balance + gain * (get(c) - balance))

    emit((0, 0, 0), rest[0])
    for c in HALF:
        n = sum(abs(k) for k in c)
        odd = scaled[n] * vel[c]
        even = rest[n] + 0.5 * odd * vel[c]
        emit(c, even + odd)
        emit(tuple(-k for k in c), even - odd)


def level_factor(here, there_rows, e):
    scale = jnp.where(here == 1, scale_to_coarse, scale_to_fine)
    return jnp.where(lane_roll(there_rows, -e) != here, scale, 1.0)


def fill_factors(levels, shape, blocks, table):
    lev = {
        (dx, dy): column_level(levels, shape, blocks, dx, dy)
        for dx in (-1, 0, 1)
        for dy in (-1, 0, 1)
    }
    row = sublane()
    for k, (own, dx) in enumerate(((0, -1), (0, 0), (0, 1), (-1, 0), (1, 0))):
        here = lev[own, 0]
        for e in (-1, 0, 1):
            plain = level_factor(here, lev[dx, 0], e)
            for b in (-1, 0, 1):
                low, high = plain, plain
                if b == -1:
                    low = jnp.where(row == 0, level_factor(here, lev[dx, -1], e), plain)
                if b == 1:
                    high = jnp.where(row == ROWS - 1, level_factor(here, lev[dx, 1], e), plain)
                table[k, b + 1, e + 1, 0:8, :] = low
                table[k, b + 1, e + 1, 8:16, :] = high


def x_side(a, x, last):
    if a == 0:
        return 1
    return jnp.where(x == (0 if a < 0 else last), 1 + a, 1)


def store_by_parity(odd, first, second, up, down):
    @pl.when(odd == 0)
    def _():
        first[...] = up[...]
        second[...] = down[...]

    @pl.when(odd == 1)
    def _():
        first[...] = down[...]
        second[...] = up[...]


def start_kernel(shape, blocks, levels, f, out, table, pay_a, pay_b, up, down):
    fill_factors(levels, shape, blocks, table)
    fine = column_level(levels, shape, blocks, 0, 0) == 1
    last = f.shape[1] - 1

    def layer(x, carry):
        for h in (0, 1):
            rows = slice(8 * h, 8 * h + 8)

            def put(c, value):
                a, b, e = c
                out[comp(*c), x, rows, :] = value
                if b == 1 and h == 1:
                    up[face(a, e), pl.ds(x, 1), :] = value[7:8]
                if b == -1 and h == 0:
                    down[face(a, e), pl.ds(x, 1), :] = value[0:1]

            collide(
                lambda c: f[comp(*c), x, rows, :],
                fine,
                False,
                lambda c: table[x_side(c[0], x, last), c[1] + 1, c[2] + 1, rows, :],
                put,
            )
        return carry

    lax.fori_loop(0, f.shape[1], layer, 0)
    store_by_parity(lax.rem(lax.axis_index("by"), 2), pay_a, pay_b, up, down)


def shifted_read(g, above, below, row, c, x, h):
    a, b, e = c
    i = comp(a, b, e)
    if b == 0:
        tile = g[i, x, 8 * h : 8 * h + 8, :]
    elif b == 1:
        if h == 1:
            tile = g[i, x, 7:15, :]
        else:
            tile = pltpu.roll(g[i, x, 0:8, :], 1, 0)
            tile = jnp.where(row == 0, below[face(a, e), pl.ds(x, 1), :], tile)
    else:
        if h == 0:
            tile = g[i, x, 1:9, :]
        else:
            tile = pltpu.roll(g[i, x, 8:16, :], 7, 0)
            tile = jnp.where(row == 7, above[face(a, e), pl.ds(x, 1), :], tile)
    return lane_roll(tile, e)


def load_by_parity(odd, first, second, above, below):
    @pl.when(odd == 0)
    def _():
        above[...] = first[...]
        below[...] = second[...]

    @pl.when(odd == 1)
    def _():
        above[...] = second[...]
        below[...] = first[...]


def side_kernel(shape, blocks, levels, f, g, got_a, got_b, pay_a, pay_b, above, below, up, down):
    load_by_parity(lax.rem(lax.axis_index("by"), 2), got_a, got_b, above, below)
    fine = column_level(levels, shape, blocks, 0, 0) == 1
    row = sublane()
    last = f.shape[1] - 1
    for ad, edge, inner, pay in ((1, last, last - 1, up), (-1, 0, 1, down)):
        for h in (0, 1):
            rows = slice(8 * h, 8 * h + 8)
            for b in (-1, 0, 1):
                for e in (-1, 0, 1):
                    j = face(b, e)
                    same, flat, back = (ad, b, e), (0, b, e), (-ad, b, e)
                    pay[j, rows, :] = shifted_read(g, above, below, row, same, edge, h)
                    pay[9 + j, rows, :] = jnp.where(
                        fine,
                        shifted_read(g, above, below, row, same, inner, h),
                        f[comp(*same), edge, rows, :],
                    )
                    pay[18 + j, rows, :] = jnp.where(
                        fine,
                        shifted_read(g, above, below, row, flat, edge, h),
                        f[comp(*flat), edge, rows, :],
                    )
                    pay[27 + j, rows, :] = f[comp(*back), edge, rows, :]
    store_by_parity(lax.rem(lax.axis_index("bx"), 2), pay_a, pay_b, up, down)


def body_kernel(
    shape, blocks, levels, f, g, table, ya, yb, xa, xb, out, pay_a, pay_b,
    above, below, right, left, state, sums, up, down,
):
    odd_x = lax.rem(lax.axis_index("bx"), 2)
    odd_y = lax.rem(lax.axis_index("by"), 2)
    load_by_parity(odd_y, ya, yb, above, below)
    load_by_parity(odd_x, xa, xb, right, left)
    fine = {dx: column_level(levels, shape, blocks, dx, 0) == 1 for dx in (-1, 0, 1)}
    row = sublane()
    last = f.shape[1] - 1

    def read(c, x, h):
        return shifted_read(g, above, below, row, c, x, h)

    def finish(x, h, mask, factor, dirs, slot):
        rows = slice(8 * h, 8 * h + 8)
        made = {}

        def put(c, value):
            made[c] = value

        collide(lambda c: state[comp(*c), rows, :], mask, True, factor, put, dirs)
        for a in (-1, 0, 1):
            if dirs is not None and (a, 0, 0) not in dirs:
                continue
            for b in (-1, 0, 1):
                plus = lane_roll(made[a, b, 1], 1)
                minus = lane_roll(made[a, b, -1], -1)
                sums[a + 1, b + 1, 0, slot, rows, :] = made[a, b, 0] + (plus + minus)
                sums[a + 1, b + 1, 1, slot, rows, :] = plus - minus

    def own(x, skip):
        for h in (0, 1):
            rows = slice(8 * h, 8 * h + 8)
            for c in DIRS:
                a, b, e = c
                if a == skip == 1:
                    tile = left[face(b, e), rows, :]
                elif a == skip == -1:
                    tile = right[face(b, e), rows, :]
                else:
                    tile = read(c, x - a, h)
                state[comp(*c), rows, :] = jnp.where(fine[0], tile, f[comp(*c), x, rows, :])
            dirs = None if skip == 0 else [c for c in DIRS if c[0] != -skip]
            finish(
                x, h, fine[0],
                lambda c: table[
                    1 + (c[0] if skip == -c[0] else 0), c[1] + 1, c[2] + 1, rows, :
                ],
                dirs, x + 1,
            )

    def halo(side, slot, pay, edge, k):
        for h in (0, 1):
            rows = slice(8 * h, 8 * h + 8)
            for b in (-1, 0, 1):
                for e in (-1, 0, 1):
                    j = face(b, e)
                    state[comp(-side, b, e), rows, :] = pay[9 + j, rows, :]
                    state[comp(0, b, e), rows, :] = pay[18 + j, rows, :]
                    state[comp(side, b, e), rows, :] = jnp.where(
                        fine[side], read((side, b, e), edge, h), pay[27 + j, rows, :]
                    )
            finish(
                0, h, fine[side],
                lambda c: table[k, c[1] + 1, c[2] + 1, rows, :],
                [c for c in DIRS if c[0] == -side], slot,
            )

    def layer(x, carry):
        own(x, 0)
        return carry

    lax.fori_loop(1, last, layer, 0)
    own(0, 1)
    own(last, -1)
    halo(-1, 0, left, 0, 3)
    halo(1, last + 2, right, last, 4)

    def gather(x, carry):
        for h in (0, 1):
            rows = slice(8 * h, 8 * h + 8)
        total, cross, along = {}, {}, {}
        for b in (-1, 0, 1):
            for h in (0, 1):
                rows = slice(8 * h, 8 * h + 8)
                low = sums[2, b + 1, 0, x, rows, :]
                mid = sums[1, b + 1, 0, x + 1, rows, :]
                high = sums[0, b + 1, 0, x + 2, rows, :]
                total[b, h] = low + mid + high
                cross[b, h] = low - high
                along[b, h] = (
                    sums[2, b + 1, 1, x, rows, :]
                    + sums[1, b + 1, 1, x + 1, rows, :]
                    + sums[0, b + 1, 1, x + 2, rows, :]
                )
        for n, part in enumerate((total, cross, along)):
            up[n, pl.ds(x, 1), :] = part[1, 1][7:8]
            down[n, pl.ds(x, 1), :] = part[-1, 0][0:1]
            rise = [pltpu.roll(part[1, h], 1, 0) for h in (0, 1)]
            fall = [pltpu.roll(part[-1, h], 7, 0) for h in (0, 1)]
            rise = [jnp.where(row == 0, 0.0, rise[0]), jnp.where(row == 0, rise[0], rise[1])]
            fall = [jnp.where(row == 7, fall[1], fall[0]), jnp.where(row == 7, 0.0, fall[1])]
            for h in (0, 1):
                rows = slice(8 * h, 8 * h + 8)
                out[(0, 1, 3)[n], x, rows, :] = part[0, h] + rise[h] + fall[h]
                if n == 0:
                    out[2, x, rows, :] = rise[h] - fall[h]
        return carry

    lax.fori_loop(0, last + 1, gather, 0)
    store_by_parity(odd_y, pay_a, pay_b, up, down)


def block_rows(tile, reflect, turn):
    tile = pltpu.roll(tile, 0, 1, stride=LANES // 8, stride_axis=0)
    tile = jnp.take_along_axis(tile, reflect, axis=0)
    return jnp.take_along_axis(tile, turn, axis=1)


def leaving(slots, blocks, step):
    here = lax.axis_index("bx") * lax.axis_size("by") + lax.axis_index("by")
    which = jnp.int32(-1)
    for k in range(blocks):
        which = jnp.where(slots[k] // blocks == here + step, k, which)
    return which


def moments_kernel(
    blocks, slots, part, got_a, got_b, rho_out, vel_out, pay_a, pay_b,
    above, below, made, up, down,
):
    odd = lax.rem(lax.axis_index("by"), 2)
    load_by_parity(odd, got_a, got_b, above, below)
    row = sublane()
    group = lane_block(LANES // 8)
    reflect = (group - row) & 7
    turn = (lane_block(1) + row * (LANES // 8)) & (LANES - 1)

    def layer(x, carry):
        for h in (0, 1):
            rows = slice(8 * h, 8 * h + 8)
            edge, halo, sign = (0, below, 1.0) if h == 0 else (7, above, -1.0)
            total, cross, along = (halo[n, pl.ds(x, 1), :] for n in range(3))
            values = []
            for n, extra in enumerate((total, cross, sign * total, along)):
                values.append(part[n, x, rows, :] + jnp.where(row == edge, extra, 0.0))
            inv = 1.0 / values[0]
            for n in range(4):
                tile = values[0] if n == 0 else values[n] * inv
                tile = block_rows(tile, reflect, turn)
                made[2 * n + h, pl.ds(x * 8, 8), :] = tile
        return carry

    lax.fori_loop(0, part.shape[1], layer, 0)
    for x in range(part.shape[1]):
        for h in (0, 1):
            lanes = slice((2 * x + h) * LANES, (2 * x + h + 1) * LANES)
            rho_out[:, lanes] = made[h, 8 * x : 8 * x + 8, :]
            for n in range(3):
                vel_out[n, :, lanes] = made[2 * n + 2 + h, 8 * x : 8 * x + 8, :]
    for step, pay in ((1, up), (-1, down)):
        which = jnp.maximum(leaving(slots, blocks, step), 0)
        for n in range(8):
            pay[n, :, :] = made[n, pl.ds(which, part.shape[1], stride=8), :]
    store_by_parity(odd, pay_a, pay_b, up, down)


def place_kernel(blocks, slots, rho, vel, got_a, got_b, rho_out, vel_out, after, before):
    odd = lax.rem(lax.axis_index("by"), 2)
    load_by_parity(odd, got_a, got_b, after, before)
    row = sublane()
    to_next = row == leaving(slots, blocks, 1)
    to_prev = row == leaving(slots, blocks, -1)
    for x in range(after.shape[1]):
        for h in (0, 1):
            lanes = slice((2 * x + h) * LANES, (2 * x + h + 1) * LANES)
            for n in range(4):
                k = 2 * n + h
                tile = rho[:, lanes] if n == 0 else vel[n - 1, :, lanes]
                tile = jnp.where(to_next, after[k, x : x + 1, :], tile)
                tile = jnp.where(to_prev, before[k, x : x + 1, :], tile)
                if n == 0:
                    rho_out[:, lanes] = tile
                else:
                    vel_out[n - 1, :, lanes] = tile


def swap(value, axis, odd, curve=False):
    count_x, count_y = lax.axis_size("bx"), lax.axis_size("by")
    pairs = []
    if curve:
        pairs = [(j, j + 1) for j in range(odd, count_x * count_y - 1, 2)]
    elif axis == "by":
        for x in range(count_x):
            for y in range(odd, count_y, 2):
                pairs.append((x * count_y + y, x * count_y + (y + 1) % count_y))
    else:
        for y in range(count_y):
            for x in range(odd, count_x, 2):
                pairs.append((x * count_y + y, (x + 1) % count_x * count_y + y))
    pairs = pairs + [(b, a) for a, b in pairs]
    return lax.ppermute(value, ("bx", "by"), pairs)


def call(kernel, outs, specs, scratch, name):
    space = {"v": pltpu.VMEM, "s": pltpu.SMEM}
    return pl.pallas_call(
        kernel,
        out_shape=[jax.ShapeDtypeStruct(s, jnp.float32) for s in outs],
        in_specs=[pl.BlockSpec(memory_space=space[k]) for k in specs],
        out_specs=[pl.BlockSpec(memory_space=pltpu.VMEM)] * len(outs),
        scratch_shapes=[pltpu.VMEM(s, jnp.float32) for s in scratch],
        compiler_params=pltpu.CompilerParams(vmem_limit_bytes=VMEM_BYTES),
        name=name,
    )


def on_device(populations, block_level, new_slot):
    shape = (lax.axis_size("bx"), lax.axis_size("by"))
    blocks = new_slot.shape[0]
    _, nx, ny, nz = populations.shape
    yface, xface, yedge, block = (9, nx, nz), (36, ny, nz), (3, nx, nz), (8, nx, nz)

    def start(*refs):
        start_kernel(shape, blocks, *refs)

    out, table, pay_a, pay_b = call(
        start,
        [populations.shape, (5, 3, 3, ny, nz), yface, yface],
        "sv",
        [yface, yface],
        "start",
    )(block_level, populations)
    ya, yb = swap(pay_a, "by", 0), swap(pay_b, "by", 1)

    def side(*refs):
        side_kernel(shape, blocks, *refs)

    pay_a, pay_b = call(
        side, [xface, xface], "svvvv", [yface, yface, xface, xface], "side"
    )(block_level, populations, out, ya, yb)
    xa, xb = swap(pay_a, "bx", 0), swap(pay_b, "bx", 1)

    def body(*refs):
        body_kernel(shape, blocks, *refs)

    part, pay_a, pay_b = call(
        body,
        [(4, nx, ny, nz), yedge, yedge],
        "svvvvvvv",
        [yface, yface, xface, xface, (27, ny, nz), (3, 3, 2, nx + 2, ny, nz), yedge, yedge],
        "body",
    )(block_level, populations, out, table, ya, yb, xa, xb)
    ya, yb = swap(pay_a, "by", 0), swap(pay_b, "by", 1)

    def moments(*refs):
        moments_kernel(blocks, *refs)

    cells = nx * ny * nz // blocks
    rho, vel, pay_a, pay_b = call(
        moments,
        [(blocks, cells), (3, blocks, cells), block, block],
        "svvv",
        [yedge, yedge, (8, nx * 8, nz), block, block],
        "moments",
    )(new_slot, part, ya, yb)
    ma, mb = swap(pay_a, "by", 0, True), swap(pay_b, "by", 1, True)

    def place(*refs):
        place_kernel(blocks, *refs)

    return tuple(
        call(place, [(blocks, cells), (3, blocks, cells)], "svvvv", [block, block], "place")(
            new_slot, rho, vel, ma, mb
        )
    )


def solution(mesh):
    in_specs = (P(None, "bx", "by", None), P(), P(("bx", "by")))
    out_specs = (P(("bx", "by"), None), P(None, ("bx", "by"), None))
    return jax.shard_map(
        on_device, mesh=mesh, in_specs=in_specs, out_specs=out_specs, check_vma=False
    )
```

```python
import functools
import math

import jax
import jax.numpy as jnp
import numpy as np
from jax import lax
from jax.experimental import pallas as pl
from jax.experimental.pallas import tpu as pltpu
from jax.sharding import PartitionSpec as P

tau_coarse = 0.56
tau_fine = 0.62
scale_to_fine = tau_fine / (2.0 * tau_coarse)
scale_to_coarse = 2.0 * tau_coarse / tau_fine
smagorinsky = 18.0 * math.sqrt(2.0) * 0.17 * 0.17
weights = (8.0 / 27, 2.0 / 27, 1.0 / 54, 1.0 / 216)
ROWS = 8
LANES = 128
VMEM_BYTES = 16 * 1024 * 1024


def comp(a, b, e):
    return 9 * (a + 1) + 3 * (b + 1) + (e + 1)


def face(b, e):
    return 3 * (b + 1) + (e + 1)


DIRS = [(a, b, e) for a in (-1, 0, 1) for b in (-1, 0, 1) for e in (-1, 0, 1)]
HALF = [c for c in DIRS if c > (0, 0, 0)]


def lane_block(edge):
    return lax.broadcasted_iota(jnp.int32, (ROWS, LANES), 1) // edge


def sublane():
    return lax.broadcasted_iota(jnp.int32, (ROWS, LANES), 0)


def column_level(levels, shape, blocks, dx, dy):
    count_x, count_y = shape
    ix = lax.rem(lax.axis_index("bx") + (dx + count_x), count_x)
    iy = lax.rem(lax.axis_index("by") + (dy + count_y), count_y)
    base = (ix * count_y + iy) * blocks
    block = lane_block(LANES // blocks)
    value = jnp.full((ROWS, LANES), levels[base], jnp.int32)
    for k in range(1, blocks):
        value = jnp.where(block == k, levels[base + k], value)
    return value


def lane_roll(tile, by):
    return tile if by == 0 else pltpu.roll(tile, by % LANES, 1)


def group_sums(get):
    total, diff, quad = {}, {}, {}
    for b in (-1, 0, 1):
        low, mid, high = (get(b, e) for e in (-1, 0, 1))
        quad[b] = low + high
        total[b] = quad[b] + mid
        diff[b] = high - low
    both = total[-1] + total[1]
    return (
        both + total[0],
        total[1] - total[-1],
        both,
        diff[-1] + diff[0] + diff[1],
        diff[1] - diff[-1],
        quad[-1] + quad[0] + quad[1],
    )


def add_sums(first, second):
    return tuple(p + q for p, q in zip(first, second))


def collide(groups, get, fine, everywhere, factor, put, dirs=None):
    low, mid, high = (groups[a] for a in (-1, 0, 1))
    ends = add_sums(low, high)
    rho, jy, pyy, jz, pyz, pzz = add_sums(ends, mid)
    pxx = ends[0]
    jx, pxy, pxz = high[0] - low[0], high[1] - low[1], high[3] - low[3]
    inv = 1.0 / rho
    ux, uy, uz = jx * inv, jy * inv, jz * inv
    third = rho * (1.0 / 3.0)
    pxx = pxx - third - jx * ux
    pyy = pyy - third - jy * uy
    pzz = pzz - third - jz * uz
    pxy = pxy - jx * uy
    pxz = pxz - jx * uz
    pyz = pyz - jy * uz
    norm = jnp.sqrt(
        pxx * pxx + pyy * pyy + pzz * pzz + 2.0 * (pxy * pxy + pxz * pxz + pyz * pyz)
    )
    base_time = jnp.where(fine, tau_fine, tau_coarse)
    tau = 0.5 * (base_time + jnp.sqrt(base_time * base_time + smagorinsky * norm * inv))
    keep = 1.0 - 1.0 / tau
    if not everywhere:
        keep = jnp.where(fine, keep, 1.0)
    base = 1.0 - 1.5 * (ux * ux + uy * uy + uz * uz)
    scaled = [rho * w for w in weights]
    rest = [s * base for s in scaled]
    vx, vy, vz = 3.0 * ux, 3.0 * uy, 3.0 * uz
    vel = {(0, 0, 1): vz, (0, 1, 0): vy, (1, 0, 0): vx}
    vel[0, 1, 1], vel[0, 1, -1] = vy + vz, vy - vz
    vel[1, 0, 1], vel[1, 0, -1] = vx + vz, vx - vz
    vel[1, 1, 0], vel[1, -1, 0] = vx + vy, vx - vy
    for b in (-1, 1):
        for e in (-1, 1):
            vel[1, b, e] = vel[1, b, 0] + (vz if e > 0 else -vz)

    def emit(c, balance):
        if dirs is not None and c not in dirs:
            return
        gain = keep if c == (0, 0, 0) else keep * factor(c)
        put(c, balance + gain * (get(c) - balance))

    emit((0, 0, 0), rest[0])
    for c in HALF:
        n = sum(abs(k) for k in c)
        odd = scaled[n] * vel[c]
        even = rest[n] + 0.5 * odd * vel[c]
        emit(c, even + odd)
        emit(tuple(-k for k in c), even - odd)


def sums_of(get):
    return {a: group_sums(lambda b, e, a=a: get((a, b, e))) for a in (-1, 0, 1)}


def level_factor(here, there_rows, e):
    scale = jnp.where(here == 1, scale_to_coarse, scale_to_fine)
    return jnp.where(lane_roll(there_rows, -e) != here, scale, 1.0)


def fill_factors(levels, shape, blocks, table):
    lev = {
        (dx, dy): column_level(levels, shape, blocks, dx, dy)
        for dx in (-1, 0, 1)
        for dy in (-1, 0, 1)
    }
    row = sublane()
    for k, (own, dx) in enumerate(((0, -1), (0, 0), (0, 1), (-1, 0), (1, 0))):
        here = lev[own, 0]
        for e in (-1, 0, 1):
            plain = level_factor(here, lev[dx, 0], e)
            for b in (-1, 0, 1):
                low, high = plain, plain
                if b == -1:
                    low = jnp.where(row == 0, level_factor(here, lev[dx, -1], e), plain)
                if b == 1:
                    high = jnp.where(row == ROWS - 1, level_factor(here, lev[dx, 1], e), plain)
                table[k, b + 1, e + 1, 0:8, :] = low
                table[k, b + 1, e + 1, 8:16, :] = high


def x_side(a, x, last):
    if a == 0:
        return 1
    return jnp.where(x == (0 if a < 0 else last), 1 + a, 1)


def store_by_parity(odd, first, second, up, down):
    @pl.when(odd == 0)
    def _():
        first[...] = up[...]
        second[...] = down[...]

    @pl.when(odd == 1)
    def _():
        first[...] = down[...]
        second[...] = up[...]


def face_kernel(shape, blocks, levels, f, pay_a, pay_b, up, down):
    _, nx, ny, nz = f.shape
    flat = f.reshape(27 * nx * ny, nz)
    here = column_level(levels, shape, blocks, 0, 0)
    row = sublane()
    for b, y, pay in ((1, ny - 1, up), (-1, 0, down)):
        near = [column_level(levels, shape, blocks, dx, b) for dx in (-1, 0, 1)]
        plain = {e: level_factor(here, near[1], e) for e in (-1, 0, 1)}
        for x in range(0, nx, ROWS):

            def get(c):
                return flat[pl.ds((comp(*c) * nx + x) * ny + y, ROWS, stride=ny), :]

            def factor(c):
                if c[0] == -1 and x == 0:
                    return jnp.where(row == 0, level_factor(here, near[0], c[2]), plain[c[2]])
                if c[0] == 1 and x + ROWS == nx:
                    return jnp.where(
                        row == ROWS - 1, level_factor(here, near[2], c[2]), plain[c[2]]
                    )
                return plain[c[2]]

            def put(c, value):
                pay[face(c[0], c[2]), x : x + ROWS, :] = value

            collide(
                sums_of(get), get, here == 1, False, factor, put, [c for c in DIRS if c[1] == b]
            )
    store_by_parity(lax.rem(lax.axis_index("by"), 2), pay_a, pay_b, up, down)


def first_collide(f, table, fine, x, near, put):
    for h in (0, 1):
        rows = slice(8 * h, 8 * h + 8)

        def get(c):
            return f[comp(*c), x, rows, :]

        def factor(c):
            return table[near(c[0]), c[1] + 1, c[2] + 1, rows, :]

        collide(sums_of(get), get, fine, False, factor, lambda c, value: put(c, rows, value))


def edge_kernel(shape, blocks, levels, f, table, out):
    fill_factors(levels, shape, blocks, table)
    fine = column_level(levels, shape, blocks, 0, 0) == 1
    nx = f.shape[1]
    for k, x in enumerate((0, 1, nx - 2, nx - 1)):

        def near(a):
            return 1 + a if (x, a) in ((0, -1), (nx - 1, 1)) else 1

        def put(c, rows, value):
            out[comp(*c), k, rows, :] = value

        first_collide(f, table, fine, x, near, put)


def shifted_read(g, above, below, row, c, k, x, h):
    a, b, e = c
    i = comp(a, b, e)
    if b == 0:
        tile = g[i, k, 8 * h : 8 * h + 8, :]
    elif b == 1:
        if h == 1:
            tile = g[i, k, 7:15, :]
        else:
            tile = pltpu.roll(g[i, k, 0:8, :], 1, 0)
            tile = jnp.where(row == 0, below[face(a, e), pl.ds(x, 1), :], tile)
    else:
        if h == 0:
            tile = g[i, k, 1:9, :]
        else:
            tile = pltpu.roll(g[i, k, 8:16, :], 7, 0)
            tile = jnp.where(row == 7, above[face(a, e), pl.ds(x, 1), :], tile)
    return lane_roll(tile, e)


def load_by_parity(odd, first, second, above, below):
    @pl.when(odd == 0)
    def _():
        above[...] = first[...]
        below[...] = second[...]

    @pl.when(odd == 1)
    def _():
        above[...] = second[...]
        below[...] = first[...]


def side_kernel(
    shape, blocks, levels, f, g, got_a, got_b, pay_a, pay_b, above, below, up, down
):
    load_by_parity(lax.rem(lax.axis_index("by"), 2), got_a, got_b, above, below)
    fine = column_level(levels, shape, blocks, 0, 0) == 1
    row = sublane()
    nx = f.shape[1]
    for ad, x, inner, k, near, pay in ((1, nx - 1, nx - 2, 3, 2, up), (-1, 0, 1, 0, 1, down)):
        for h in (0, 1):
            rows = slice(8 * h, 8 * h + 8)

            def old(c):
                return f[comp(*c), x, rows, :]

            def flat(b, e):
                moved = shifted_read(g, above, below, row, (0, b, e), k, x, h)
                return jnp.where(fine, moved, old((0, b, e)))

            for b in (-1, 0, 1):
                for e in (-1, 0, 1):
                    c = (ad, b, e)
                    pay[face(b, e), rows, :] = shifted_read(g, above, below, row, c, k, x, h)
                    moved = shifted_read(g, above, below, row, c, near, inner, h)
                    pay[9 + face(b, e), rows, :] = jnp.where(fine, moved, old(c))
            middle = group_sums(flat)
            back = group_sums(lambda b, e: old((-ad, b, e)))
            back = [jnp.where(fine, 0.0, s) for s in back]
            parts = [middle[0], middle[1], middle[2] + back[2], middle[3]]
            parts += [middle[4] + back[4], middle[5] + back[5], back[0], back[1], back[3]]
            for n, part in enumerate(parts):
                pay[18 + n, rows, :] = part
    store_by_parity(lax.rem(lax.axis_index("bx"), 2), pay_a, pay_b, up, down)


def second_collide(groups, get, fine, factor, put, dirs):
    made = {}

    def keep(c, value):
        made[c] = value

    collide(groups, get, fine, True, factor, keep, dirs)
    for a in (-1, 0, 1):
        if dirs is not None and (a, 0, 0) not in dirs:
            continue
        for b in (-1, 0, 1):
            plus = lane_roll(made[a, b, 1], 1)
            minus = lane_roll(made[a, b, -1], -1)
            put(a, b, made[a, b, 0] + (plus + minus), plus - minus)


def gather_layer(sums, row, put, up, down):
    total, cross, along = {}, {}, {}
    for b in (-1, 0, 1):
        for h in (0, 1):
            low, mid, high = (sums(a, b, 0, h) for a in (1, 0, -1))
            total[b, h] = low + mid + high
            cross[b, h] = low - high
            along[b, h] = sums(1, b, 1, h) + sums(0, b, 1, h) + sums(-1, b, 1, h)
    for n, part in enumerate((total, cross, along)):
        up(n, part[1, 1][7:8])
        down(n, part[-1, 0][0:1])
        rise = [pltpu.roll(part[1, h], 1, 0) for h in (0, 1)]
        fall = [pltpu.roll(part[-1, h], 7, 0) for h in (0, 1)]
        rise = [jnp.where(row == 0, 0.0, rise[0]), jnp.where(row == 0, rise[0], rise[1])]
        fall = [jnp.where(row == 7, fall[1], fall[0]), jnp.where(row == 7, 0.0, fall[1])]
        for h in (0, 1):
            put((0, 1, 3)[n], h, part[0, h] + rise[h] + fall[h])
            if n == 0:
                put(2, h, rise[h] - fall[h])


def turns():
    row = sublane()
    reflect = (lane_block(LANES // ROWS) - row) & (ROWS - 1)
    turn = (lane_block(1) + row * (LANES // ROWS)) & (LANES - 1)
    return reflect, turn


def block_rows(tile, reflect, turn):
    tile = pltpu.roll(tile, 0, 1, stride=LANES // ROWS, stride_axis=0)
    tile = jnp.take_along_axis(tile, reflect, axis=0)
    return jnp.take_along_axis(tile, turn, axis=1)


def inner_kernel(
    shape, blocks, levels, f, edges, table, ya, yb, tie, sums, made, up, down,
    above, below, g, state,
):
    load_by_parity(lax.rem(lax.axis_index("by"), 2), ya, yb, above, below)
    fine = column_level(levels, shape, blocks, 0, 0) == 1
    row = sublane()
    reflect, turn = turns()
    nx = f.shape[1]
    for k, x in enumerate((0, 1, nx - 2, nx - 1)):
        g[:, x, :, :] = edges[:, k, :, :]

    def first(x, carry):
        def put(c, rows, value):
            g[comp(*c), x, rows, :] = value

        first_collide(f, table, fine, x, lambda a: 1, put)
        return carry

    lax.fori_loop(2, nx - 2, first, 0)

    def second(x, carry):
        for h in (0, 1):
            rows = slice(8 * h, 8 * h + 8)

            def moved(c):
                tile = shifted_read(g, above, below, row, c, x - c[0], x - c[0], h)
                tile = jnp.where(fine, tile, f[comp(*c), x, rows, :])
                state[comp(*c), rows, :] = tile
                return tile

            def put(a, b, total, along):
                sums[a + 1, b + 1, 0, x, rows, :] = total
                sums[a + 1, b + 1, 1, x, rows, :] = along

            second_collide(
                sums_of(moved),
                lambda c: state[comp(*c), rows, :],
                fine,
                lambda c: table[1, c[1] + 1, c[2] + 1, rows, :],
                put,
                None,
            )
        return carry

    lax.fori_loop(1, nx - 1, second, 0)

    def gather(x, carry):
        def put(n, h, tile):
            made[2 * n + h, pl.ds(x * ROWS, ROWS), :] = block_rows(tile, reflect, turn)

        def put_up(n, value):
            up[n, pl.ds(x, 1), :] = value

        def put_down(n, value):
            down[n, pl.ds(x, 1), :] = value

        gather_layer(
            lambda a, b, q, h: sums[a + 1, b + 1, q, x - a, 8 * h : 8 * h + 8, :],
            row, put, put_up, put_down,
        )
        return carry

    lax.fori_loop(2, nx - 2, gather, 0)


def outer_kernel(
    shape, blocks, levels, f, g, table, ya, yb, xa, xb, sums, in_up, in_down,
    part, pay_a, pay_b, above, below, right, left, state, ends, up, down,
):
    load_by_parity(lax.rem(lax.axis_index("by"), 2), ya, yb, above, below)
    load_by_parity(lax.rem(lax.axis_index("bx"), 2), xa, xb, right, left)
    fine = {dx: column_level(levels, shape, blocks, dx, 0) == 1 for dx in (-1, 0, 1)}
    row = sublane()
    reflect, turn = turns()
    nx = f.shape[1]
    hold = {-1: 0, 0: 1, nx - 1: 2, nx: 3}
    at = {0: 0, 1: 1, nx - 2: 2, nx - 1: 3}
    for side, x, k, pay in ((-1, 0, 3, left), (1, nx - 1, 4, right)):
        for h in (0, 1):
            rows = slice(8 * h, 8 * h + 8)

            def keep(slot):
                def put(a, b, total, along):
                    ends[a + 1, b + 1, 0, slot, rows, :] = total
                    ends[a + 1, b + 1, 1, slot, rows, :] = along

                return put

            def read(c, x):
                return shifted_read(g, above, below, row, c, at[x], x, h)

            def moved(c):
                a, b, e = c
                if a == -side:
                    tile = pay[face(b, e), rows, :]
                else:
                    tile = read(c, x - a)
                tile = jnp.where(fine[0], tile, f[comp(*c), x, rows, :])
                state[comp(*c), rows, :] = tile
                return tile

            second_collide(
                sums_of(moved),
                lambda c: state[comp(*c), rows, :],
                fine[0],
                lambda c: table[1, c[1] + 1, c[2] + 1, rows, :],
                keep(hold[x]),
                [c for c in DIRS if c[0] != side],
            )
            got = [pay[18 + n, rows, :] for n in range(9)]
            own = group_sums(lambda b, e: read((side, b, e), x))
            own = [jnp.where(fine[side], s, 0.0) for s in own]
            outer = (own[0] + got[6], own[1] + got[7], own[2], own[3] + got[8], own[4], own[5])

            def toward(c):
                return pay[9 + face(c[1], c[2]), rows, :]

            second_collide(
                {
                    side: outer,
                    0: tuple(got[:6]),
                    -side: group_sums(lambda b, e: toward((-side, b, e))),
                },
                toward,
                fine[side],
                lambda c: table[k, c[1] + 1, c[2] + 1, rows, :],
                keep(hold[x + side]),
                [c for c in DIRS if c[0] == -side],
            )
    up[...] = in_up[...]
    down[...] = in_down[...]
    for m, x in enumerate((0, 1, nx - 2, nx - 1)):

        def fetch(a, b, q, h):
            rows = slice(8 * h, 8 * h + 8)
            if x - a in hold:
                return ends[a + 1, b + 1, q, hold[x - a], rows, :]
            return sums[a + 1, b + 1, q, x - a, rows, :]

        def put(n, h, tile):
            part[2 * n + h, ROWS * m : ROWS * m + ROWS, :] = tile

        def put_up(n, value):
            up[n, x : x + 1, :] = value

        def put_down(n, value):
            down[n, x : x + 1, :] = value

        gather_layer(fetch, row, put, put_up, put_down)
    for pay in (up, down):
        for n in range(3):
            for x in range(0, nx, ROWS):
                rows = slice(x, x + ROWS)
                pay[n, rows, :] = block_rows(pay[n, rows, :], reflect, turn)
    store_by_parity(lax.rem(lax.axis_index("by"), 2), pay_a, pay_b, up, down)


def turn_kernel(part, out):
    reflect, turn = turns()
    for n in range(part.shape[0]):
        for m in range(4):
            rows = slice(ROWS * m, ROWS * m + ROWS)
            out[n, rows, :] = block_rows(part[n, rows, :], reflect, turn)


def leaving(slots, blocks, step):
    here = lax.axis_index("bx") * lax.axis_size("by") + lax.axis_index("by")
    which = jnp.int32(-1)
    for k in range(blocks):
        which = jnp.where(slots[k] // blocks == here + step, k, which)
    return which


def moments_kernel(
    blocks, slots, inner, outer, got_a, got_b, rho_out, vel_out, pay_a, pay_b,
    above, below, made, up, down,
):
    odd = lax.rem(lax.axis_index("by"), 2)
    load_by_parity(odd, got_a, got_b, above, below)
    nx = above.shape[1]
    width = LANES // ROWS
    group = lane_block(width)
    at = {0: 0, 1: 1, nx - 2: 2, nx - 1: 3}
    for x in range(nx):
        for h in (0, 1):
            rows = slice(ROWS * x, ROWS * x + ROWS)
            spot, halo, sign = (0, below, 1.0) if h == 0 else (ROWS - 1, above, -1.0)
            first = x // ROWS * ROWS
            extra = []
            for n in range(3):
                tile = lane_roll(halo[n, first : first + ROWS, :], width * (spot - x % ROWS))
                extra.append(jnp.where(group == spot, tile, 0.0))
            total, cross, along = extra
            values = []
            for n, more in enumerate((total, cross, sign * total, along)):
                if x in at:
                    tile = outer[2 * n + h, ROWS * at[x] : ROWS * at[x] + ROWS, :]
                else:
                    tile = inner[2 * n + h, rows, :]
                values.append(tile + more)
            inv = 1.0 / values[0]
            lanes = slice((2 * x + h) * LANES, (2 * x + h + 1) * LANES)
            for n in range(4):
                tile = values[0] if n == 0 else values[n] * inv
                made[2 * n + h, rows, :] = tile
                if n == 0:
                    rho_out[:, lanes] = tile
                else:
                    vel_out[n - 1, :, lanes] = tile
    for step, pay in ((1, up), (-1, down)):
        which = jnp.maximum(leaving(slots, blocks, step), 0)
        for n in range(8):
            pay[n, :, :] = made[n, pl.ds(which, nx, stride=ROWS), :]
    store_by_parity(odd, pay_a, pay_b, up, down)


def place_kernel(blocks, slots, rho, vel, got_a, got_b, rho_out, vel_out, after, before):
    odd = lax.rem(lax.axis_index("by"), 2)
    load_by_parity(odd, got_a, got_b, after, before)
    row = sublane()
    to_next = row == leaving(slots, blocks, 1)
    to_prev = row == leaving(slots, blocks, -1)
    for x in range(after.shape[1]):
        for h in (0, 1):
            lanes = slice((2 * x + h) * LANES, (2 * x + h + 1) * LANES)
            for n in range(4):
                k = 2 * n + h
                tile = rho[:, lanes] if n == 0 else vel[n - 1, :, lanes]
                tile = jnp.where(to_next, after[k, x : x + 1, :], tile)
                tile = jnp.where(to_prev, before[k, x : x + 1, :], tile)
                if n == 0:
                    rho_out[:, lanes] = tile
                else:
                    vel_out[n - 1, :, lanes] = tile


def swap(value, axis, odd, curve=False):
    count_x, count_y = lax.axis_size("bx"), lax.axis_size("by")
    pairs = []
    if curve:
        pairs = [(j, j + 1) for j in range(odd, count_x * count_y - 1, 2)]
    elif axis == "by":
        for x in range(count_x):
            for y in range(odd, count_y, 2):
                pairs.append((x * count_y + y, x * count_y + (y + 1) % count_y))
    else:
        for y in range(count_y):
            for x in range(odd, count_x, 2):
                pairs.append((x * count_y + y, (x + 1) % count_x * count_y + y))
    pairs = pairs + [(b, a) for a, b in pairs]
    return lax.ppermute(value, ("bx", "by"), pairs)


def call(kernel, outs, specs, scratch, name, work):
    space = {"v": pltpu.VMEM, "s": pltpu.SMEM, "a": pl.ANY}
    return pl.pallas_call(
        kernel,
        out_shape=[jax.ShapeDtypeStruct(s, jnp.float32) for s in outs],
        in_specs=[pl.BlockSpec(memory_space=space[k]) for k in specs],
        out_specs=[pl.BlockSpec(memory_space=pltpu.VMEM)] * len(outs),
        scratch_shapes=[pltpu.VMEM(s, jnp.float32) for s in scratch],
        compiler_params=pltpu.CompilerParams(vmem_limit_bytes=VMEM_BYTES),
        cost_estimate=pl.CostEstimate(
            flops=work * 2000000, bytes_accessed=work * 1000000, transcendentals=0
        ),
        name=name,
    )


def on_device(populations, block_level, new_slot):
    shape = (lax.axis_size("bx"), lax.axis_size("by"))
    blocks = new_slot.shape[0]
    _, nx, ny, nz = populations.shape
    yface, xface, yedge, block = (9, nx, nz), (27, ny, nz), (3, nx, nz), (8, nx, nz)
    edge, table = (27, 4, ny, nz), (5, 3, 3, ny, nz)

    def run(kernel, *args, outs, specs, scratch=(), work=1):
        def body(*refs):
            kernel(*refs)

        return call(body, outs, specs, scratch, kernel.func.__name__[:-7], work)(*args)

    def leveled(kernel):
        return functools.partial(kernel, shape, blocks)

    pay_a, pay_b = run(
        leveled(face_kernel), block_level, populations,
        outs=[yface, yface], specs="sv", scratch=[yface, yface],
    )
    ya, yb = swap(pay_a, "by", 0), swap(pay_b, "by", 1)
    tables, edges = run(
        leveled(edge_kernel), block_level, populations,
        outs=[table, edge], specs="sv", work=2,
    )
    pay_a, pay_b = run(
        leveled(side_kernel), block_level, populations, edges, ya, yb,
        outs=[xface, xface], specs="svvvv", scratch=[yface, yface, xface, xface],
    )
    xa, xb = swap(pay_a, "bx", 0), swap(pay_b, "bx", 1)
    sums, inner, up, down = run(
        leveled(inner_kernel), block_level, populations, edges, tables, ya, yb, pay_a,
        outs=[(3, 3, 2, nx, ny, nz), (8, nx * ROWS, nz), yedge, yedge],
        specs="svvvvva",
        scratch=[yface, yface, populations.shape, (27, ny, nz)],
        work=10,
    )
    part, pay_a, pay_b = run(
        leveled(outer_kernel),
        block_level, populations, edges, tables, ya, yb, xa, xb, sums, up, down,
        outs=[(8, 4 * ROWS, nz), yedge, yedge],
        specs="svvvvvvvvvv",
        scratch=[yface, yface, xface, xface, (27, ny, nz), (3, 3, 2, 4, ny, nz), yedge, yedge],
    )
    ya, yb = swap(pay_a, "by", 0), swap(pay_b, "by", 1)
    (outer,) = run(
        functools.partial(turn_kernel), part, outs=[(8, 4 * ROWS, nz)], specs="v"
    )
    cells = nx * ny * nz // blocks
    whole = [(blocks, cells), (3, blocks, cells)]
    rho, vel, pay_a, pay_b = run(
        functools.partial(moments_kernel, blocks), new_slot, inner, outer, ya, yb,
        outs=whole + [block, block],
        specs="svvvv",
        scratch=[yedge, yedge, (8, nx * ROWS, nz), block, block],
    )
    ma, mb = swap(pay_a, "by", 0, True), swap(pay_b, "by", 1, True)
    return tuple(
        run(
            functools.partial(place_kernel, blocks), new_slot, rho, vel, ma, mb,
            outs=whole, specs="svvvv", scratch=[block, block],
        )
    )


def solution(mesh):
    in_specs = (P(None, "bx", "by", None), P(), P(("bx", "by")))
    out_specs = (P(("bx", "by"), None), P(None, ("bx", "by"), None))
    return jax.shard_map(
        on_device, mesh=mesh, in_specs=in_specs, out_specs=out_specs, check_vma=False
    )
```

```python
import functools
import math

import jax
import jax.numpy as jnp
import numpy as np
from jax import lax
from jax.experimental import pallas as pl
from jax.experimental.pallas import tpu as pltpu
from jax.sharding import PartitionSpec as P

tau_coarse = 0.56
tau_fine = 0.62
scale_to_fine = tau_fine / (2.0 * tau_coarse)
scale_to_coarse = 2.0 * tau_coarse / tau_fine
smagorinsky = 18.0 * math.sqrt(2.0) * 0.17 * 0.17
weights = (8.0 / 27, 2.0 / 27, 1.0 / 54, 1.0 / 216)
ROWS = 8
LANES = 128
VMEM_BYTES = 16 * 1024 * 1024
FACE_BYTES = 53 * 1024 * 1024


def comp(a, b, e):
    return 9 * (a + 1) + 3 * (b + 1) + (e + 1)


def face(b, e):
    return 3 * (b + 1) + (e + 1)


DIRS = [(a, b, e) for a in (-1, 0, 1) for b in (-1, 0, 1) for e in (-1, 0, 1)]
HALF = [c for c in DIRS if c > (0, 0, 0)]


def lane_block(edge):
    return lax.broadcasted_iota(jnp.int32, (ROWS, LANES), 1) // edge


def sublane():
    return lax.broadcasted_iota(jnp.int32, (ROWS, LANES), 0)


def column_level(levels, shape, blocks, dx, dy):
    count_x, count_y = shape
    ix = lax.rem(lax.axis_index("bx") + (dx + count_x), count_x)
    iy = lax.rem(lax.axis_index("by") + (dy + count_y), count_y)
    base = (ix * count_y + iy) * blocks
    block = lane_block(LANES // blocks)
    value = jnp.full((ROWS, LANES), levels[base], jnp.int32)
    for k in range(1, blocks):
        value = jnp.where(block == k, levels[base + k], value)
    return value


def lane_roll(tile, by):
    return tile if by == 0 else pltpu.roll(tile, by % LANES, 1)


def group_sums(get):
    total, diff, quad = {}, {}, {}
    for b in (-1, 0, 1):
        low, mid, high = (get(b, e) for e in (-1, 0, 1))
        quad[b] = low + high
        total[b] = quad[b] + mid
        diff[b] = high - low
    both = total[-1] + total[1]
    return (
        both + total[0],
        total[1] - total[-1],
        both,
        diff[-1] + diff[0] + diff[1],
        diff[1] - diff[-1],
        quad[-1] + quad[0] + quad[1],
    )


def add_sums(first, second):
    return tuple(p + q for p, q in zip(first, second))


def collide(groups, get, fine, everywhere, factor, put, dirs=None):
    low, mid, high = (groups[a] for a in (-1, 0, 1))
    ends = add_sums(low, high)
    rho, jy, pyy, jz, pyz, pzz = add_sums(ends, mid)
    pxx = ends[0]
    jx, pxy, pxz = high[0] - low[0], high[1] - low[1], high[3] - low[3]
    inv = 1.0 / rho
    ux, uy, uz = jx * inv, jy * inv, jz * inv
    third = rho * (1.0 / 3.0)
    pxx = pxx - third - jx * ux
    pyy = pyy - third - jy * uy
    pzz = pzz - third - jz * uz
    pxy = pxy - jx * uy
    pxz = pxz - jx * uz
    pyz = pyz - jy * uz
    norm = jnp.sqrt(
        pxx * pxx + pyy * pyy + pzz * pzz + 2.0 * (pxy * pxy + pxz * pxz + pyz * pyz)
    )
    base_time = jnp.where(fine, tau_fine, tau_coarse)
    tau = 0.5 * (base_time + jnp.sqrt(base_time * base_time + smagorinsky * norm * inv))
    keep = 1.0 - 1.0 / tau
    if not everywhere:
        keep = jnp.where(fine, keep, 1.0)
    base = 1.0 - 1.5 * (ux * ux + uy * uy + uz * uz)
    scaled = [rho * w for w in weights]
    rest = [s * base for s in scaled]
    vx, vy, vz = 3.0 * ux, 3.0 * uy, 3.0 * uz
    vel = {(0, 0, 1): vz, (0, 1, 0): vy, (1, 0, 0): vx}
    vel[0, 1, 1], vel[0, 1, -1] = vy + vz, vy - vz
    vel[1, 0, 1], vel[1, 0, -1] = vx + vz, vx - vz
    vel[1, 1, 0], vel[1, -1, 0] = vx + vy, vx - vy
    for b in (-1, 1):
        for e in (-1, 1):
            vel[1, b, e] = vel[1, b, 0] + (vz if e > 0 else -vz)

    def emit(c, balance):
        if dirs is not None and c not in dirs:
            return
        gain = keep if c == (0, 0, 0) else keep * factor(c)
        put(c, balance + gain * (get(c) - balance))

    emit((0, 0, 0), rest[0])
    for c in HALF:
        n = sum(abs(k) for k in c)
        odd = scaled[n] * vel[c]
        even = rest[n] + 0.5 * odd * vel[c]
        emit(c, even + odd)
        emit(tuple(-k for k in c), even - odd)


def sums_of(get):
    return {a: group_sums(lambda b, e, a=a: get((a, b, e))) for a in (-1, 0, 1)}


def level_factor(here, there_rows, e):
    scale = jnp.where(here == 1, scale_to_coarse, scale_to_fine)
    return jnp.where(lane_roll(there_rows, -e) != here, scale, 1.0)


def fill_factors(marks, table):
    row = sublane()
    for k, (own, dx) in enumerate(((0, -1), (0, 0), (0, 1), (-1, 0), (1, 0))):
        here = marks[own + 1, 1, :, :]
        near = [marks[dx + 1, b, :, :] for b in range(3)]
        for e in (-1, 0, 1):
            plain = level_factor(here, near[1], e)
            for b in (-1, 0, 1):
                low, high = plain, plain
                if b == -1:
                    low = jnp.where(row == 0, level_factor(here, near[0], e), plain)
                if b == 1:
                    high = jnp.where(row == ROWS - 1, level_factor(here, near[2], e), plain)
                table[k, b + 1, e + 1, 0:8, :] = low
                table[k, b + 1, e + 1, 8:16, :] = high


def x_side(a, x, last):
    if a == 0:
        return 1
    return jnp.where(x == (0 if a < 0 else last), 1 + a, 1)


def store_by_parity(odd, first, second, up, down):
    @pl.when(odd == 0)
    def _():
        first[...] = up[...]
        second[...] = down[...]

    @pl.when(odd == 1)
    def _():
        first[...] = down[...]
        second[...] = up[...]


def face_kernel(
    shape, blocks, levels, f, marks, pay_a, pay_b, level, high, low, sems, up, down
):
    _, nx, ny, nz = f.shape
    copies = [
        pltpu.make_async_copy(levels, level, sems.at[0]),
        pltpu.make_async_copy(f.at[:, :, ny - 1, :], high, sems.at[1]),
        pltpu.make_async_copy(f.at[:, :, 0, :], low, sems.at[2]),
    ]
    for copy in copies:
        copy.start()
    copies[0].wait()
    for dx in (-1, 0, 1):
        for dy in (-1, 0, 1):
            marks[dx + 1, dy + 1, :, :] = column_level(level, shape, blocks, dx, dy)
    here = marks[1, 1, :, :]
    row = sublane()
    for b, rows, pay, copy in ((1, high, up, copies[1]), (-1, low, down, copies[2])):
        near = [marks[dx, b + 1, :, :] for dx in range(3)]
        plain = {e: level_factor(here, near[1], e) for e in (-1, 0, 1)}
        copy.wait()
        for x in range(0, nx, ROWS):

            def get(c):
                return rows[comp(*c), x : x + ROWS, :]

            def factor(c):
                if c[0] == -1 and x == 0:
                    return jnp.where(row == 0, level_factor(here, near[0], c[2]), plain[c[2]])
                if c[0] == 1 and x + ROWS == nx:
                    return jnp.where(
                        row == ROWS - 1, level_factor(here, near[2], c[2]), plain[c[2]]
                    )
                return plain[c[2]]

            def put(c, value):
                pay[face(c[0], c[2]), x : x + ROWS, :] = value

            collide(
                sums_of(get), get, here == 1, False, factor, put, [c for c in DIRS if c[1] == b]
            )
    store_by_parity(lax.rem(lax.axis_index("by"), 2), pay_a, pay_b, up, down)


def first_collide(f, table, fine, x, near, put):
    for h in (0, 1):
        rows = slice(8 * h, 8 * h + 8)

        def get(c):
            return f[comp(*c), x, rows, :]

        def factor(c):
            return table[near(c[0]), c[1] + 1, c[2] + 1, rows, :]

        collide(sums_of(get), get, fine, False, factor, lambda c, value: put(c, rows, value))


def first_kernel(marks, f, table, out, calm):
    fill_factors(marks, table)
    fine = marks[1, 1, :, :] == 1
    nx = f.shape[1]
    for n, (x, a) in enumerate(((0, -1), (nx - 1, 1))):
        for h in (0, 1):
            rows = slice(8 * h, 8 * h + 8)

            def get(c):
                return f[comp(*c), x, rows, :]

            def put(c, value):
                calm[n, face(c[1], c[2]), rows, :] = value

            collide(
                sums_of(get), get, fine, True,
                lambda c: table[1 + c[0], c[1] + 1, c[2] + 1, rows, :],
                put, [c for c in DIRS if c[0] == a],
            )

    def layer(x, carry):
        def near(a):
            return 1 if a == 0 else jnp.where(x == (0 if a < 0 else nx - 1), 1 + a, 1)

        def put(c, rows, value):
            out[comp(*c), x, rows, :] = value

        first_collide(f, table, fine, x, near, put)
        return carry

    lax.fori_loop(0, nx, layer, 0)


def shifted_read(g, above, below, row, c, x, h):
    a, b, e = c
    i = comp(a, b, e)
    if b == 0:
        tile = g[i, x, 8 * h : 8 * h + 8, :]
    elif b == 1:
        if h == 1:
            tile = g[i, x, 7:15, :]
        else:
            tile = pltpu.roll(g[i, x, 0:8, :], 1, 0)
            tile = jnp.where(row == 0, below[face(a, e), pl.ds(x, 1), :], tile)
    else:
        if h == 0:
            tile = g[i, x, 1:9, :]
        else:
            tile = pltpu.roll(g[i, x, 8:16, :], 7, 0)
            tile = jnp.where(row == 7, above[face(a, e), pl.ds(x, 1), :], tile)
    return lane_roll(tile, e)


def load_by_parity(odd, first, second, above, below):
    @pl.when(odd == 0)
    def _():
        above[...] = first[...]
        below[...] = second[...]

    @pl.when(odd == 1)
    def _():
        above[...] = second[...]
        below[...] = first[...]


def side_kernel(marks, f, g, calm, got_a, got_b, pay_a, pay_b, above, below, up, down):
    load_by_parity(lax.rem(lax.axis_index("by"), 2), got_a, got_b, above, below)
    fine = marks[1, 1, :, :] == 1
    row = sublane()
    nx = f.shape[1]
    for n, (ad, x, pay) in enumerate(((-1, 0, down), (1, nx - 1, up))):
        for h in (0, 1):
            rows = slice(8 * h, 8 * h + 8)

            def flat(b, e):
                return shifted_read(g, above, below, row, (0, b, e), x, h)

            for b in (-1, 0, 1):
                for e in (-1, 0, 1):
                    c, j = (ad, b, e), face(b, e)
                    pay[j, rows, :] = shifted_read(g, above, below, row, c, x, h)
                    moved = shifted_read(g, above, below, row, c, x - ad, h)
                    pay[9 + j, rows, :] = jnp.where(fine, moved, calm[n, j, rows, :])
            for m, part in enumerate(group_sums(flat)):
                pay[18 + m, rows, :] = part
    store_by_parity(lax.rem(lax.axis_index("bx"), 2), pay_a, pay_b, up, down)


def second_collide(groups, get, fine, factor, put, dirs, known=None):
    made = {}

    def keep(c, value):
        made[c] = value if known is None else jnp.where(fine, value, known(c))

    collide(groups, get, fine, True, factor, keep, dirs)
    for a in (-1, 0, 1):
        if dirs is not None and (a, 0, 0) not in dirs:
            continue
        for b in (-1, 0, 1):
            plus = lane_roll(made[a, b, 1], 1)
            minus = lane_roll(made[a, b, -1], -1)
            put(a, b, made[a, b, 0] + (plus + minus), plus - minus)


def gather_layer(sums, row, put, up, down):
    total, cross, along = {}, {}, {}
    for b in (-1, 0, 1):
        for h in (0, 1):
            low, mid, high = (sums(a, b, 0, h) for a in (1, 0, -1))
            total[b, h] = low + mid + high
            cross[b, h] = low - high
            along[b, h] = sums(1, b, 1, h) + sums(0, b, 1, h) + sums(-1, b, 1, h)
    for n, part in enumerate((total, cross, along)):
        up(n, part[1, 1][7:8])
        down(n, part[-1, 0][0:1])
        rise = [pltpu.roll(part[1, h], 1, 0) for h in (0, 1)]
        fall = [pltpu.roll(part[-1, h], 7, 0) for h in (0, 1)]
        rise = [jnp.where(row == 0, 0.0, rise[0]), jnp.where(row == 0, rise[0], rise[1])]
        fall = [jnp.where(row == 7, fall[1], fall[0]), jnp.where(row == 7, 0.0, fall[1])]
        for h in (0, 1):
            put((0, 1, 3)[n], h, part[0, h] + rise[h] + fall[h])
            if n == 0:
                put(2, h, rise[h] - fall[h])


def turns():
    row = sublane()
    reflect = (lane_block(LANES // ROWS) - row) & (ROWS - 1)
    turn = (lane_block(1) + row * (LANES // ROWS)) & (LANES - 1)
    return reflect, turn


def block_rows(tile, reflect, turn):
    tile = pltpu.roll(tile, 0, 1, stride=LANES // ROWS, stride_axis=0)
    tile = jnp.take_along_axis(tile, reflect, axis=0)
    return jnp.take_along_axis(tile, turn, axis=1)


def leaving(slots, blocks, step):
    here = lax.axis_index("bx") * lax.axis_size("by") + lax.axis_index("by")
    which = jnp.int32(-1)
    for k in range(blocks):
        which = jnp.where(slots[k] // blocks == here + step, k, which)
    return which


def inner_kernel(
    blocks, slots, marks, f, g, table, ya, yb, tie, sums, made, up, down, moves,
    above, below, state,
):
    load_by_parity(lax.rem(lax.axis_index("by"), 2), ya, yb, above, below)
    for n, step in enumerate((1, -1)):
        moves[n, :, :] = jnp.full((ROWS, LANES), leaving(slots, blocks, step), jnp.int32)
    fine = marks[1, 1, :, :] == 1
    row = sublane()
    reflect, turn = turns()
    nx = f.shape[1]

    def second(x, carry):
        for h in (0, 1):
            rows = slice(8 * h, 8 * h + 8)

            def moved(c):
                tile = shifted_read(g, above, below, row, c, x - c[0], h)
                tile = jnp.where(fine, tile, f[comp(*c), x, rows, :])
                state[comp(*c), rows, :] = tile
                return tile

            def put(a, b, total, along):
                sums[a + 1, b + 1, 0, x, rows, :] = total
                sums[a + 1, b + 1, 1, x, rows, :] = along

            second_collide(
                sums_of(moved),
                lambda c: state[comp(*c), rows, :],
                fine,
                lambda c: table[1, c[1] + 1, c[2] + 1, rows, :],
                put,
                None,
            )
        return carry

    lax.fori_loop(1, nx - 1, second, 0)

    def gather(x, carry):
        def put(n, h, tile):
            made[2 * n + h, pl.ds(x * ROWS, ROWS), :] = block_rows(tile, reflect, turn)

        def put_up(n, value):
            up[n, pl.ds(x, 1), :] = value

        def put_down(n, value):
            down[n, pl.ds(x, 1), :] = value

        gather_layer(
            lambda a, b, q, h: sums[a + 1, b + 1, q, x - a, 8 * h : 8 * h + 8, :],
            row, put, put_up, put_down,
        )
        return carry

    lax.fori_loop(2, nx - 2, gather, 0)


def outer_kernel(
    marks, f, g, table, ya, yb, xa, xb, sums, in_up, in_down,
    part, pay_a, pay_b, above, below, right, left, state, ends, up, down,
):
    load_by_parity(lax.rem(lax.axis_index("by"), 2), ya, yb, above, below)
    load_by_parity(lax.rem(lax.axis_index("bx"), 2), xa, xb, right, left)
    fine = {dx: marks[dx + 1, 1, :, :] == 1 for dx in (-1, 0, 1)}
    row = sublane()
    reflect, turn = turns()
    nx = f.shape[1]
    hold = {-1: 0, 0: 1, nx - 1: 2, nx: 3}
    for side, x, k, pay in ((-1, 0, 3, left), (1, nx - 1, 4, right)):
        for h in (0, 1):
            rows = slice(8 * h, 8 * h + 8)

            def keep(slot):
                def put(a, b, total, along):
                    ends[a + 1, b + 1, 0, slot, rows, :] = total
                    ends[a + 1, b + 1, 1, slot, rows, :] = along

                return put

            def read(c, x):
                return shifted_read(g, above, below, row, c, x, h)

            def moved(c):
                a, b, e = c
                if a == -side:
                    tile = pay[face(b, e), rows, :]
                else:
                    tile = read(c, x - a)
                tile = jnp.where(fine[0], tile, f[comp(*c), x, rows, :])
                state[comp(*c), rows, :] = tile
                return tile

            second_collide(
                sums_of(moved),
                lambda c: state[comp(*c), rows, :],
                fine[0],
                lambda c: table[1, c[1] + 1, c[2] + 1, rows, :],
                keep(hold[x]),
                [c for c in DIRS if c[0] != side],
            )

            def toward(c):
                return pay[9 + face(c[1], c[2]), rows, :]

            second_collide(
                {
                    side: group_sums(lambda b, e: read((side, b, e), x)),
                    0: tuple(pay[18 + n, rows, :] for n in range(6)),
                    -side: group_sums(lambda b, e: toward((-side, b, e))),
                },
                toward,
                fine[side],
                lambda c: table[k, c[1] + 1, c[2] + 1, rows, :],
                keep(hold[x + side]),
                [c for c in DIRS if c[0] == -side],
                toward,
            )
    up[...] = in_up[...]
    down[...] = in_down[...]
    for m, x in enumerate((0, 1, nx - 2, nx - 1)):

        def fetch(a, b, q, h):
            rows = slice(8 * h, 8 * h + 8)
            if x - a in hold:
                return ends[a + 1, b + 1, q, hold[x - a], rows, :]
            return sums[a + 1, b + 1, q, x - a, rows, :]

        def put(n, h, tile):
            part[2 * n + h, ROWS * m : ROWS * m + ROWS, :] = tile

        def put_up(n, value):
            up[n, x : x + 1, :] = value

        def put_down(n, value):
            down[n, x : x + 1, :] = value

        gather_layer(fetch, row, put, put_up, put_down)
    for pay in (up, down):
        for n in range(3):
            for x in range(0, nx, ROWS):
                rows = slice(x, x + ROWS)
                pay[n, rows, :] = block_rows(pay[n, rows, :], reflect, turn)
    store_by_parity(lax.rem(lax.axis_index("by"), 2), pay_a, pay_b, up, down)


def turn_kernel(part, out):
    reflect, turn = turns()
    for n in range(part.shape[0]):
        for m in range(4):
            rows = slice(ROWS * m, ROWS * m + ROWS)
            out[n, rows, :] = block_rows(part[n, rows, :], reflect, turn)


def moments_kernel(
    moves, inner, outer, got_a, got_b, rho_out, vel_out, pay_a, pay_b,
    above, below, made, up, down,
):
    odd = lax.rem(lax.axis_index("by"), 2)
    load_by_parity(odd, got_a, got_b, above, below)
    nx = above.shape[1]
    width = LANES // ROWS
    group = lane_block(width)
    at = {0: 0, 1: 1, nx - 2: 2, nx - 1: 3}
    for x in range(nx):
        for h in (0, 1):
            rows = slice(ROWS * x, ROWS * x + ROWS)
            spot, halo, sign = (0, below, 1.0) if h == 0 else (ROWS - 1, above, -1.0)
            first = x // ROWS * ROWS
            extra = []
            for n in range(3):
                tile = lane_roll(halo[n, first : first + ROWS, :], width * (spot - x % ROWS))
                extra.append(jnp.where(group == spot, tile, 0.0))
            total, cross, along = extra
            values = []
            for n, more in enumerate((total, cross, sign * total, along)):
                if x in at:
                    tile = outer[2 * n + h, ROWS * at[x] : ROWS * at[x] + ROWS, :]
                else:
                    tile = inner[2 * n + h, rows, :]
                values.append(tile + more)
            inv = 1.0 / values[0]
            lanes = slice((2 * x + h) * LANES, (2 * x + h + 1) * LANES)
            for n in range(4):
                tile = values[0] if n == 0 else values[n] * inv
                made[2 * n + h, rows, :] = tile
                if n == 0:
                    rho_out[:, lanes] = tile
                else:
                    vel_out[n - 1, :, lanes] = tile
    for k, pay in enumerate((up, down)):
        which = jnp.maximum(jnp.max(moves[k, :, :]), 0)
        for n in range(8):
            pay[n, :, :] = made[n, pl.ds(which, nx, stride=ROWS), :]
    store_by_parity(odd, pay_a, pay_b, up, down)


def place_kernel(moves, rho, vel, got_a, got_b, rho_out, vel_out, after, before):
    odd = lax.rem(lax.axis_index("by"), 2)
    load_by_parity(odd, got_a, got_b, after, before)
    row = sublane()
    to_next = row == moves[0, :, :]
    to_prev = row == moves[1, :, :]
    for x in range(after.shape[1]):
        for h in (0, 1):
            lanes = slice((2 * x + h) * LANES, (2 * x + h + 1) * LANES)
            for n in range(4):
                k = 2 * n + h
                tile = rho[:, lanes] if n == 0 else vel[n - 1, :, lanes]
                tile = jnp.where(to_next, after[k, x : x + 1, :], tile)
                tile = jnp.where(to_prev, before[k, x : x + 1, :], tile)
                if n == 0:
                    rho_out[:, lanes] = tile
                else:
                    vel_out[n - 1, :, lanes] = tile


def swap(value, axis, odd, curve=False):
    count_x, count_y = lax.axis_size("bx"), lax.axis_size("by")
    pairs = []
    if curve:
        pairs = [(j, j + 1) for j in range(odd, count_x * count_y - 1, 2)]
    elif axis == "by":
        for x in range(count_x):
            for y in range(odd, count_y, 2):
                pairs.append((x * count_y + y, x * count_y + (y + 1) % count_y))
    else:
        for y in range(count_y):
            for x in range(odd, count_x, 2):
                pairs.append((x * count_y + y, (x + 1) % count_x * count_y + y))
    pairs = pairs + [(b, a) for a, b in pairs]
    return lax.ppermute(value, ("bx", "by"), pairs)


def call(kernel, outs, specs, scratch, name, work, limit):
    space = {"v": pltpu.VMEM, "s": pltpu.SMEM, "h": pltpu.HBM, "a": pl.ANY}
    return pl.pallas_call(
        kernel,
        out_shape=outs,
        in_specs=[pl.BlockSpec(memory_space=space[k]) for k in specs],
        out_specs=[pl.BlockSpec(memory_space=pltpu.VMEM)] * len(outs),
        scratch_shapes=scratch,
        compiler_params=pltpu.CompilerParams(vmem_limit_bytes=limit),
        cost_estimate=pl.CostEstimate(
            flops=work * 2000000, bytes_accessed=work * 1000000, transcendentals=0
        ),
        name=name,
    )


def on_device(populations, block_level, new_slot):
    shape = (lax.axis_size("bx"), lax.axis_size("by"))
    blocks = new_slot.shape[0]
    _, nx, ny, nz = populations.shape
    yface, xface, yedge, block = (9, nx, nz), (24, ny, nz), (3, nx, nz), (8, nx, nz)
    tile = (ROWS, nz)

    def real(*dims):
        return jax.ShapeDtypeStruct(dims, jnp.float32)

    def whole(*dims):
        return jax.ShapeDtypeStruct(dims, jnp.int32)

    def room(*shapes):
        return [pltpu.VMEM(dims, jnp.float32) for dims in shapes]

    def run(kernel, *args, outs, specs, scratch=(), work=1, limit=VMEM_BYTES):
        def body(*refs):
            kernel(*refs)

        return call(body, outs, specs, scratch, kernel.func.__name__[:-7], work, limit)(*args)

    marks, pay_a, pay_b = run(
        functools.partial(face_kernel, shape, blocks), block_level, populations,
        outs=[whole(3, 3, *tile), real(*yface), real(*yface)],
        specs="hh",
        scratch=[pltpu.SMEM(block_level.shape, jnp.int32)]
        + room((27, nx, nz), (27, nx, nz))
        + [pltpu.SemaphoreType.DMA((3,))]
        + room(yface, yface),
        limit=FACE_BYTES,
    )
    ya, yb = swap(pay_a, "by", 0), swap(pay_b, "by", 1)
    table, g, calm = run(
        functools.partial(first_kernel), marks, populations,
        outs=[real(5, 3, 3, ny, nz), real(*populations.shape), real(2, 9, ny, nz)],
        specs="vv", work=3,
    )
    pay_a, pay_b = run(
        functools.partial(side_kernel), marks, populations, g, calm, ya, yb,
        outs=[real(*xface)] * 2, specs="vvvvvv", scratch=room(yface, yface, xface, xface),
    )
    xa, xb = swap(pay_a, "bx", 0), swap(pay_b, "bx", 1)
    sums, inner, up, down, moves = run(
        functools.partial(inner_kernel, blocks),
        new_slot, marks, populations, g, table, ya, yb, pay_a,
        outs=[
            real(3, 3, 2, nx, ny, nz), real(8, nx * ROWS, nz), real(*yedge), real(*yedge),
            whole(2, *tile),
        ],
        specs="svvvvvva",
        scratch=room(yface, yface, (27, ny, nz)),
        work=10,
    )
    part, pay_a, pay_b = run(
        functools.partial(outer_kernel),
        marks, populations, g, table, ya, yb, xa, xb, sums, up, down,
        outs=[real(8, 4 * ROWS, nz), real(*yedge), real(*yedge)],
        specs="vvvvvvvvvvv",
        scratch=room(
            yface, yface, xface, xface, (27, ny, nz), (3, 3, 2, 4, ny, nz), yedge, yedge
        ),
    )
    ya, yb = swap(pay_a, "by", 0), swap(pay_b, "by", 1)
    (outer,) = run(
        functools.partial(turn_kernel), part, outs=[real(8, 4 * ROWS, nz)], specs="v"
    )
    cells = nx * ny * nz // blocks
    results = [real(blocks, cells), real(3, blocks, cells)]
    rho, vel, pay_a, pay_b = run(
        functools.partial(moments_kernel), moves, inner, outer, ya, yb,
        outs=results + [real(*block), real(*block)],
        specs="vvvvv",
        scratch=room(yedge, yedge, (8, nx * ROWS, nz), block, block),
    )
    ma, mb = swap(pay_a, "by", 0, True), swap(pay_b, "by", 1, True)
    return tuple(
        run(
            functools.partial(place_kernel), moves, rho, vel, ma, mb,
            outs=results, specs="vvvvv", scratch=room(block, block),
        )
    )


def solution(mesh):
    in_specs = (P(None, "bx", "by", None), P(), P(("bx", "by")))
    out_specs = (P(("bx", "by"), None), P(None, ("bx", "by"), None))
    return jax.shard_map(
        on_device, mesh=mesh, in_specs=in_specs, out_specs=out_specs, check_vma=False
    )
```

```python
import functools
import math

import jax
import jax.numpy as jnp
import numpy as np
from jax import lax
from jax.experimental import pallas as pl
from jax.experimental.pallas import tpu as pltpu
from jax.sharding import PartitionSpec as P

tau_coarse = 0.56
tau_fine = 0.62
scale_to_fine = tau_fine / (2.0 * tau_coarse)
scale_to_coarse = 2.0 * tau_coarse / tau_fine
smagorinsky = 18.0 * math.sqrt(2.0) * 0.17 * 0.17
weights = (8.0 / 27, 2.0 / 27, 1.0 / 54, 1.0 / 216)
ROWS = 8
LANES = 128
VMEM_BYTES = 16 * 1024 * 1024
FACE_BYTES = 53 * 1024 * 1024


def comp(a, b, e):
    return 9 * (a + 1) + 3 * (b + 1) + (e + 1)


def face(b, e):
    return 3 * (b + 1) + (e + 1)


DIRS = [(a, b, e) for a in (-1, 0, 1) for b in (-1, 0, 1) for e in (-1, 0, 1)]
HALF = [c for c in DIRS if c > (0, 0, 0)]


def lane_block(edge):
    return lax.broadcasted_iota(jnp.int32, (ROWS, LANES), 1) // edge


def sublane():
    return lax.broadcasted_iota(jnp.int32, (ROWS, LANES), 0)


def column_level(levels, shape, blocks, dx, dy):
    count_x, count_y = shape
    ix = lax.rem(lax.axis_index("bx") + (dx + count_x), count_x)
    iy = lax.rem(lax.axis_index("by") + (dy + count_y), count_y)
    base = (ix * count_y + iy) * blocks
    block = lane_block(LANES // blocks)
    value = jnp.full((ROWS, LANES), levels[base], jnp.int32)
    for k in range(1, blocks):
        value = jnp.where(block == k, levels[base + k], value)
    return value


def lane_roll(tile, by):
    return tile if by == 0 else pltpu.roll(tile, by % LANES, 1)


def group_sums(get):
    total, diff, quad = {}, {}, {}
    for b in (-1, 0, 1):
        low, mid, high = (get(b, e) for e in (-1, 0, 1))
        quad[b] = low + high
        total[b] = quad[b] + mid
        diff[b] = high - low
    both = total[-1] + total[1]
    return (
        both + total[0],
        total[1] - total[-1],
        both,
        diff[-1] + diff[0] + diff[1],
        diff[1] - diff[-1],
        quad[-1] + quad[0] + quad[1],
    )


def add_sums(first, second):
    return tuple(p + q for p, q in zip(first, second))


def collide(groups, get, fine, everywhere, factor, put, dirs=None):
    low, mid, high = (groups[a] for a in (-1, 0, 1))
    ends = add_sums(low, high)
    rho, jy, pyy, jz, pyz, pzz = add_sums(ends, mid)
    pxx = ends[0]
    jx, pxy, pxz = high[0] - low[0], high[1] - low[1], high[3] - low[3]
    inv = 1.0 / rho
    ux, uy, uz = jx * inv, jy * inv, jz * inv
    third = rho * (1.0 / 3.0)
    pxx = pxx - third - jx * ux
    pyy = pyy - third - jy * uy
    pzz = pzz - third - jz * uz
    pxy = pxy - jx * uy
    pxz = pxz - jx * uz
    pyz = pyz - jy * uz
    norm = jnp.sqrt(
        pxx * pxx + pyy * pyy + pzz * pzz + 2.0 * (pxy * pxy + pxz * pxz + pyz * pyz)
    )
    base_time = jnp.where(fine, tau_fine, tau_coarse)
    tau = 0.5 * (base_time + jnp.sqrt(base_time * base_time + smagorinsky * norm * inv))
    keep = 1.0 - 1.0 / tau
    if not everywhere:
        keep = jnp.where(fine, keep, 1.0)
    base = 1.0 - 1.5 * (ux * ux + uy * uy + uz * uz)
    scaled = [rho * w for w in weights]
    rest = [s * base for s in scaled]
    vx, vy, vz = 3.0 * ux, 3.0 * uy, 3.0 * uz
    vel = {(0, 0, 1): vz, (0, 1, 0): vy, (1, 0, 0): vx}
    vel[0, 1, 1], vel[0, 1, -1] = vy + vz, vy - vz
    vel[1, 0, 1], vel[1, 0, -1] = vx + vz, vx - vz
    vel[1, 1, 0], vel[1, -1, 0] = vx + vy, vx - vy
    for b in (-1, 1):
        for e in (-1, 1):
            vel[1, b, e] = vel[1, b, 0] + (vz if e > 0 else -vz)

    def emit(c, balance):
        if dirs is not None and c not in dirs:
            return
        gain = keep if c == (0, 0, 0) else keep * factor(c)
        put(c, balance + gain * (get(c) - balance))

    emit((0, 0, 0), rest[0])
    for c in HALF:
        n = sum(abs(k) for k in c)
        odd = scaled[n] * vel[c]
        even = rest[n] + 0.5 * odd * vel[c]
        emit(c, even + odd)
        emit(tuple(-k for k in c), even - odd)


def sums_of(get):
    return {a: group_sums(lambda b, e, a=a: get((a, b, e))) for a in (-1, 0, 1)}


def level_factor(here, there_rows, e):
    scale = jnp.where(here == 1, scale_to_coarse, scale_to_fine)
    return jnp.where(lane_roll(there_rows, -e) != here, scale, 1.0)


def fill_factors(marks, table):
    row = sublane()
    for k, (own, dx) in enumerate(((0, -1), (0, 0), (0, 1), (-1, 0), (1, 0))):
        here = marks[own + 1, 1, :, :]
        near = [marks[dx + 1, b, :, :] for b in range(3)]
        for e in (-1, 0, 1):
            plain = level_factor(here, near[1], e)
            for b in (-1, 0, 1):
                low, high = plain, plain
                if b == -1:
                    low = jnp.where(row == 0, level_factor(here, near[0], e), plain)
                if b == 1:
                    high = jnp.where(row == ROWS - 1, level_factor(here, near[2], e), plain)
                table[k, b + 1, e + 1, 0:8, :] = low
                table[k, b + 1, e + 1, 8:16, :] = high


def x_side(a, x, last):
    if a == 0:
        return 1
    return jnp.where(x == (0 if a < 0 else last), 1 + a, 1)


def store_by_parity(odd, first, second, up, down):
    @pl.when(odd == 0)
    def _():
        if first is not None:
            first[...] = up[...]
        second[...] = down[...]

    @pl.when(odd == 1)
    def _():
        if first is not None:
            first[...] = down[...]
        second[...] = up[...]


def face_kernel(
    shape, blocks, levels, f, marks, pay_a, pay_b, level, high, low, sems, up, down
):
    _, nx, ny, nz = f.shape
    copies = [
        pltpu.make_async_copy(levels, level, sems.at[0]),
        pltpu.make_async_copy(f.at[:, :, ny - 1, :], high, sems.at[1]),
        pltpu.make_async_copy(f.at[:, :, 0, :], low, sems.at[2]),
    ]
    for copy in copies:
        copy.start()
    copies[0].wait()
    for dx in (-1, 0, 1):
        for dy in (-1, 0, 1):
            marks[dx + 1, dy + 1, :, :] = column_level(level, shape, blocks, dx, dy)
    here = marks[1, 1, :, :]
    row = sublane()
    for b, rows, pay, copy in ((1, high, up, copies[1]), (-1, low, down, copies[2])):
        near = [marks[dx, b + 1, :, :] for dx in range(3)]
        plain = {e: level_factor(here, near[1], e) for e in (-1, 0, 1)}
        copy.wait()
        for x in range(0, nx, ROWS):

            def get(c):
                return rows[comp(*c), x : x + ROWS, :]

            def factor(c):
                if c[0] == -1 and x == 0:
                    return jnp.where(row == 0, level_factor(here, near[0], c[2]), plain[c[2]])
                if c[0] == 1 and x + ROWS == nx:
                    return jnp.where(
                        row == ROWS - 1, level_factor(here, near[2], c[2]), plain[c[2]]
                    )
                return plain[c[2]]

            def put(c, value):
                pay[face(c[0], c[2]), x : x + ROWS, :] = value

            collide(
                sums_of(get), get, here == 1, False, factor, put, [c for c in DIRS if c[1] == b]
            )
    store_by_parity(lax.rem(lax.axis_index("by"), 2), pay_a, pay_b, up, down)


def first_collide(f, table, fine, x, near, put):
    for h in (0, 1):
        rows = slice(8 * h, 8 * h + 8)

        def get(c):
            return f[comp(*c), x, rows, :]

        def factor(c):
            return table[near(c[0]), c[1] + 1, c[2] + 1, rows, :]

        collide(sums_of(get), get, fine, False, factor, lambda c, value: put(c, rows, value))


def first_kernel(marks, f, table, out, calm):
    fill_factors(marks, table)
    fine = marks[1, 1, :, :] == 1
    nx = f.shape[1]
    for n, (x, a) in enumerate(((0, -1), (nx - 1, 1))):
        for h in (0, 1):
            rows = slice(8 * h, 8 * h + 8)

            def get(c):
                return f[comp(*c), x, rows, :]

            def put(c, value):
                calm[n, face(c[1], c[2]), rows, :] = value

            collide(
                sums_of(get), get, fine, True,
                lambda c: table[1 + c[0], c[1] + 1, c[2] + 1, rows, :],
                put, [c for c in DIRS if c[0] == a],
            )

    def layer(x, carry):
        def near(a):
            return 1 if a == 0 else jnp.where(x == (0 if a < 0 else nx - 1), 1 + a, 1)

        def put(c, rows, value):
            out[comp(*c), x, rows, :] = value

        first_collide(f, table, fine, x, near, put)
        return carry

    lax.fori_loop(0, nx, layer, 0)


def shifted_read(g, above, below, row, c, x, h):
    a, b, e = c
    i = comp(a, b, e)
    if b == 0:
        tile = g[i, x, 8 * h : 8 * h + 8, :]
    elif b == 1:
        if h == 1:
            tile = g[i, x, 7:15, :]
        else:
            tile = pltpu.roll(g[i, x, 0:8, :], 1, 0)
            tile = jnp.where(row == 0, below[face(a, e), pl.ds(x, 1), :], tile)
    else:
        if h == 0:
            tile = g[i, x, 1:9, :]
        else:
            tile = pltpu.roll(g[i, x, 8:16, :], 7, 0)
            tile = jnp.where(row == 7, above[face(a, e), pl.ds(x, 1), :], tile)
    return lane_roll(tile, e)


def load_by_parity(odd, first, second, above, below):
    @pl.when(odd == 0)
    def _():
        above[...] = first[...]
        below[...] = second[...]

    @pl.when(odd == 1)
    def _():
        above[...] = second[...]
        below[...] = first[...]


def side_kernel(marks, f, g, calm, got_a, got_b, pay_a, pay_b, above, below, up, down):
    load_by_parity(lax.rem(lax.axis_index("by"), 2), got_a, got_b, above, below)
    fine = marks[1, 1, :, :] == 1
    row = sublane()
    nx = f.shape[1]
    for n, (ad, x, pay) in enumerate(((-1, 0, down), (1, nx - 1, up))):
        for h in (0, 1):
            rows = slice(8 * h, 8 * h + 8)

            def flat(b, e):
                return shifted_read(g, above, below, row, (0, b, e), x, h)

            for b in (-1, 0, 1):
                for e in (-1, 0, 1):
                    c, j = (ad, b, e), face(b, e)
                    pay[j, rows, :] = shifted_read(g, above, below, row, c, x, h)
                    moved = shifted_read(g, above, below, row, c, x - ad, h)
                    pay[9 + j, rows, :] = jnp.where(fine, moved, calm[n, j, rows, :])
            for m, part in enumerate(group_sums(flat)):
                pay[18 + m, rows, :] = part
    store_by_parity(lax.rem(lax.axis_index("bx"), 2), pay_a, pay_b, up, down)


def second_collide(groups, get, fine, factor, put, dirs, known=None):
    made = {}

    def keep(c, value):
        made[c] = value if known is None else jnp.where(fine, value, known(c))

    collide(groups, get, fine, True, factor, keep, dirs)
    for a in (-1, 0, 1):
        if dirs is not None and (a, 0, 0) not in dirs:
            continue
        for b in (-1, 0, 1):
            plus = lane_roll(made[a, b, 1], 1)
            minus = lane_roll(made[a, b, -1], -1)
            put(a, b, made[a, b, 0] + (plus + minus), plus - minus)


def gather_layer(sums, row, put, up, down):
    total, cross, along = {}, {}, {}
    for b in (-1, 0, 1):
        for h in (0, 1):
            low, mid, high = (sums(a, b, 0, h) for a in (1, 0, -1))
            total[b, h] = low + mid + high
            cross[b, h] = low - high
            along[b, h] = sums(1, b, 1, h) + sums(0, b, 1, h) + sums(-1, b, 1, h)
    for n, part in enumerate((total, cross, along)):
        up(n, part[1, 1][7:8])
        down(n, part[-1, 0][0:1])
        rise = [pltpu.roll(part[1, h], 1, 0) for h in (0, 1)]
        fall = [pltpu.roll(part[-1, h], 7, 0) for h in (0, 1)]
        rise = [jnp.where(row == 0, 0.0, rise[0]), jnp.where(row == 0, rise[0], rise[1])]
        fall = [jnp.where(row == 7, fall[1], fall[0]), jnp.where(row == 7, 0.0, fall[1])]
        for h in (0, 1):
            put((0, 1, 3)[n], h, part[0, h] + rise[h] + fall[h])
            if n == 0:
                put(2, h, rise[h] - fall[h])


def turns():
    row = sublane()
    reflect = (lane_block(LANES // ROWS) - row) & (ROWS - 1)
    turn = (lane_block(1) + row * (LANES // ROWS)) & (LANES - 1)
    return reflect, turn


def block_rows(tile, reflect, turn):
    tile = pltpu.roll(tile, 0, 1, stride=LANES // ROWS, stride_axis=0)
    tile = jnp.take_along_axis(tile, reflect, axis=0)
    return jnp.take_along_axis(tile, turn, axis=1)


def leaving(slots, blocks, step):
    here = lax.axis_index("bx") * lax.axis_size("by") + lax.axis_index("by")
    which, theirs = jnp.int32(-1), jnp.int32(0)
    for k in range(blocks):
        goes = slots[k] // blocks == here + step
        which = jnp.where(goes, k, which)
        theirs = jnp.where(goes, lax.rem(slots[k], blocks), theirs)
    return which, theirs


def inner_kernel(
    blocks, slots, marks, f, g, table, ya, yb, tie, sums, made, up, down, moves,
    above, below, state,
):
    load_by_parity(lax.rem(lax.axis_index("by"), 2), ya, yb, above, below)
    for n, step in enumerate((1, -1)):
        which, theirs = leaving(slots, blocks, step)
        moves[n, :, :] = jnp.full((ROWS, LANES), which, jnp.int32)
        moves[2 + n, :, :] = jnp.full((ROWS, LANES), theirs, jnp.int32)
    fine = marks[1, 1, :, :] == 1
    row = sublane()
    reflect, turn = turns()
    nx = f.shape[1]

    def second(x, carry):
        for h in (0, 1):
            rows = slice(8 * h, 8 * h + 8)

            def moved(c):
                tile = shifted_read(g, above, below, row, c, x - c[0], h)
                tile = jnp.where(fine, tile, f[comp(*c), x, rows, :])
                state[comp(*c), rows, :] = tile
                return tile

            def put(a, b, total, along):
                sums[a + 1, b + 1, 0, x, rows, :] = total
                sums[a + 1, b + 1, 1, x, rows, :] = along

            second_collide(
                sums_of(moved),
                lambda c: state[comp(*c), rows, :],
                fine,
                lambda c: table[1, c[1] + 1, c[2] + 1, rows, :],
                put,
                None,
            )
        return carry

    lax.fori_loop(1, nx - 1, second, 0)

    def gather(x, carry):
        def put(n, h, tile):
            made[2 * n + h, pl.ds(x * ROWS, ROWS), :] = block_rows(tile, reflect, turn)

        def put_up(n, value):
            up[n, pl.ds(x, 1), :] = value

        def put_down(n, value):
            down[n, pl.ds(x, 1), :] = value

        gather_layer(
            lambda a, b, q, h: sums[a + 1, b + 1, q, x - a, 8 * h : 8 * h + 8, :],
            row, put, put_up, put_down,
        )
        return carry

    lax.fori_loop(2, nx - 2, gather, 0)


def outer_kernel(
    marks, f, g, table, ya, yb, xa, xb, sums, in_up, in_down,
    part, pay, away, above, below, right, left, state, ends, up, down,
):
    load_by_parity(lax.rem(lax.axis_index("by"), 2), ya, yb, above, below)
    load_by_parity(lax.rem(lax.axis_index("bx"), 2), xa, xb, right, left)
    fine = {dx: marks[dx + 1, 1, :, :] == 1 for dx in (-1, 0, 1)}
    row = sublane()
    reflect, turn = turns()
    nx = f.shape[1]
    hold = {-1: 0, 0: 1, nx - 1: 2, nx: 3}
    for side, x, k, got in ((-1, 0, 3, left), (1, nx - 1, 4, right)):
        for h in (0, 1):
            rows = slice(8 * h, 8 * h + 8)

            def keep(slot):
                def put(a, b, total, along):
                    ends[a + 1, b + 1, 0, slot, rows, :] = total
                    ends[a + 1, b + 1, 1, slot, rows, :] = along

                return put

            def read(c, x):
                return shifted_read(g, above, below, row, c, x, h)

            def moved(c):
                a, b, e = c
                if a == -side:
                    tile = got[face(b, e), rows, :]
                else:
                    tile = read(c, x - a)
                tile = jnp.where(fine[0], tile, f[comp(*c), x, rows, :])
                state[comp(*c), rows, :] = tile
                return tile

            second_collide(
                sums_of(moved),
                lambda c: state[comp(*c), rows, :],
                fine[0],
                lambda c: table[1, c[1] + 1, c[2] + 1, rows, :],
                keep(hold[x]),
                [c for c in DIRS if c[0] != side],
            )

            def toward(c):
                return got[9 + face(c[1], c[2]), rows, :]

            second_collide(
                {
                    side: group_sums(lambda b, e: read((side, b, e), x)),
                    0: tuple(got[18 + n, rows, :] for n in range(6)),
                    -side: group_sums(lambda b, e: toward((-side, b, e))),
                },
                toward,
                fine[side],
                lambda c: table[k, c[1] + 1, c[2] + 1, rows, :],
                keep(hold[x + side]),
                [c for c in DIRS if c[0] == -side],
                toward,
            )
    up[...] = in_up[...]
    down[...] = in_down[...]
    for m, x in enumerate((0, 1, nx - 2, nx - 1)):

        def fetch(a, b, q, h):
            rows = slice(8 * h, 8 * h + 8)
            if x - a in hold:
                return ends[a + 1, b + 1, q, hold[x - a], rows, :]
            return sums[a + 1, b + 1, q, x - a, rows, :]

        def put(n, h, tile):
            part[2 * n + h, ROWS * m : ROWS * m + ROWS, :] = tile

        def put_up(n, value):
            up[n, x : x + 1, :] = value

        def put_down(n, value):
            down[n, x : x + 1, :] = value

        gather_layer(fetch, row, put, put_up, put_down)
    for edge in (up, down):
        for n in range(3):
            for x in range(0, nx, ROWS):
                rows = slice(x, x + ROWS)
                edge[n, rows, :] = block_rows(edge[n, rows, :], reflect, turn)
    odd = lax.rem(lax.axis_index("by"), 2)
    store_by_parity(odd, pay.at[pl.ds(0, 3)], pay.at[pl.ds(3, 3)], up, down)
    store_by_parity(odd, None, away, up, down)


def turn_kernel(part, out):
    reflect, turn = turns()
    for n in range(part.shape[0]):
        for m in range(4):
            rows = slice(ROWS * m, ROWS * m + ROWS)
            out[n, rows, :] = block_rows(part[n, rows, :], reflect, turn)


def add_crossed(made, crossed, top):
    nx = crossed.shape[1]
    width = LANES // ROWS
    spot = top * (ROWS - 1)
    sign = jnp.where(top == 1, -1.0, 1.0)
    mask = lane_block(width) == spot
    for x in range(nx):
        rows = slice(ROWS * x, ROWS * x + ROWS)
        first = x // ROWS * ROWS
        shift = lax.rem(width * (spot - x % ROWS) + LANES, LANES)
        total, cross, along = (
            jnp.where(mask, pltpu.roll(crossed[n, first : first + ROWS, :], shift, 1), 0.0)
            for n in range(3)
        )
        for n, more in enumerate((total, cross, sign * total, along)):
            made[2 * n + top, rows, :] += more


def pack_block(made, pay, start, which):
    for n in range(8):
        pay[start + n, :, :] = made[n, pl.ds(which, pay.shape[1], stride=ROWS), :]


def number(tile):
    return jnp.maximum(jnp.max(tile), 0)


def pack_kernel(moves, inner, outer, got, made, block, pay_w):
    iy = lax.axis_index("by")
    odd = lax.rem(iy, 2)
    nx = got.shape[1]
    low, high = ROWS * 2, ROWS * (nx - 2)
    made[:, 0:low, :] = outer[:, 0:low, :]
    made[:, low:high, :] = inner[:, low:high, :]
    made[:, high:, :] = outer[:, low:, :]
    add_crossed(made, got, 1 - odd)
    pack_block(made, block, 0, number(moves[1 - odd, :, :]))
    end = jnp.logical_or(iy == 0, iy == lax.axis_size("by") - 1)

    @pl.when(end)
    def _():
        pay_w[0:8, :, :] = block[...]

    @pl.when(jnp.logical_not(end))
    def _():
        pay_w[0:3, :, :] = got[3:6, :, :]


def join_kernel(first, second, out):
    out[0 : first.shape[0], :, :] = first[...]
    out[first.shape[0] :, :, :] = second[...]


def moments_kernel(moves, part, got_b, got_w, rho_out, vel_out, pay_a, made):
    odd = lax.rem(lax.axis_index("by"), 2)
    nx = got_b.shape[1]
    made[...] = part[...]
    add_crossed(made, got_b, odd)
    for x in range(nx):
        rows = slice(ROWS * x, ROWS * x + ROWS)
        for h in (0, 1):
            rho = made[h, rows, :]
            inv = 1.0 / rho
            lanes = slice((2 * x + h) * LANES, (2 * x + h + 1) * LANES)
            rho_out[:, lanes] = rho
            for n in range(1, 4):
                tile = made[2 * n + h, rows, :] * inv
                made[2 * n + h, rows, :] = tile
                vel_out[n - 1, :, lanes] = tile
    pack_block(made, pay_a, 0, number(moves[odd, :, :]))
    pay_a[8:11, :, :] = got_w[0:3, :, :]


def place_kernel(moves, rho, vel, away, got_a, got_b, got_w, rho_out, vel_out, block, crossed):
    iy = lax.axis_index("by")
    odd = lax.rem(iy, 2)
    end = jnp.logical_or(iy == 0, iy == lax.axis_size("by") - 1)

    @pl.when(end)
    def _():
        block[...] = got_w[0:8, :, :]
        crossed[...] = got_a[8:11, :, :]

    @pl.when(jnp.logical_not(end))
    def _():
        block[...] = got_b[3:11, :, :]
        crossed[...] = away[...]

    row = sublane()
    width = LANES // ROWS
    top = 1 - odd
    sign = jnp.where(top == 1, -1.0, 1.0)
    mask = lane_block(width) == top * (ROWS - 1)
    spread = row * width + (lane_block(1) & (width - 1))
    theirs = number(moves[3 - odd, :, :])
    for first in range(0, block.shape[1], ROWS):
        rows = slice(first, first + ROWS)
        extra = []
        for n in range(3):
            line = jnp.broadcast_to(crossed[n, pl.ds(first + theirs, 1), :], (ROWS, LANES))
            extra.append(jnp.where(mask, jnp.take_along_axis(line, spread, axis=1), 0.0))
        total, cross, along = extra
        for n, more in enumerate((total, cross, sign * total, along)):
            block[2 * n + top, rows, :] += more
        for h in (0, 1):
            inv = 1.0 / block[h, rows, :]
            for n in range(1, 4):
                block[2 * n + h, rows, :] *= inv
    near = row == moves[odd, :, :]
    far = row == moves[1 - odd, :, :]
    for x in range(block.shape[1]):
        for h in (0, 1):
            lanes = slice((2 * x + h) * LANES, (2 * x + h + 1) * LANES)
            for n in range(4):
                k = 2 * n + h
                tile = rho[:, lanes] if n == 0 else vel[n - 1, :, lanes]
                tile = jnp.where(near, got_a[k, x : x + 1, :], tile)
                tile = jnp.where(far, block[k, x : x + 1, :], tile)
                if n == 0:
                    rho_out[:, lanes] = tile
                else:
                    vel_out[n - 1, :, lanes] = tile


def swap(value, axis, odd):
    count_x, count_y = lax.axis_size("bx"), lax.axis_size("by")
    pairs = []
    if axis == "by":
        for x in range(count_x):
            for y in range(odd, count_y, 2):
                pairs.append((x * count_y + y, x * count_y + (y + 1) % count_y))
    else:
        for y in range(count_y):
            for x in range(odd, count_x, 2):
                pairs.append((x * count_y + y, (x + 1) % count_x * count_y + y))
    pairs = pairs + [(b, a) for a, b in pairs]
    return lax.ppermute(value, ("bx", "by"), pairs)


def swap_ends(value):
    count_x, count_y = lax.axis_size("bx"), lax.axis_size("by")
    pairs = []
    for x in range(count_x):
        here, after = x * count_y, (x + 1) * count_y
        if x + 1 < count_x:
            pairs += [(after - 1, after), (after, after - 1)]
            pairs += [(here + 1, after + 1), (after + count_y - 2, after - 2)]
        pairs += [(here + y, here + (y ^ 1)) for y in range(2, count_y - 2)]
    pairs += [(0, 1), (after - 1, after - 2)]
    pairs += [(after - count_y + 1, after - 1), (count_y - 2, 0)]
    return lax.ppermute(value, ("bx", "by"), pairs)


def call(kernel, outs, specs, scratch, name, work, limit):
    space = {"v": pltpu.VMEM, "s": pltpu.SMEM, "h": pltpu.HBM, "a": pl.ANY}
    return pl.pallas_call(
        kernel,
        out_shape=outs,
        in_specs=[pl.BlockSpec(memory_space=space[k]) for k in specs],
        out_specs=[pl.BlockSpec(memory_space=pltpu.VMEM)] * len(outs),
        scratch_shapes=scratch,
        compiler_params=pltpu.CompilerParams(vmem_limit_bytes=limit),
        cost_estimate=pl.CostEstimate(
            flops=work * 2000000, bytes_accessed=work * 1000000, transcendentals=0
        ),
        name=name,
    )


def on_device(populations, block_level, new_slot):
    shape = (lax.axis_size("bx"), lax.axis_size("by"))
    blocks = new_slot.shape[0]
    _, nx, ny, nz = populations.shape
    yface, xface, yedge = (9, nx, nz), (24, ny, nz), (3, nx, nz)
    tile = (ROWS, nz)

    def real(*dims):
        return jax.ShapeDtypeStruct(dims, jnp.float32)

    def whole(*dims):
        return jax.ShapeDtypeStruct(dims, jnp.int32)

    def room(*shapes):
        return [pltpu.VMEM(dims, jnp.float32) for dims in shapes]

    def run(kernel, *args, outs, specs, scratch=(), work=1, limit=VMEM_BYTES):
        def body(*refs):
            kernel(*refs)

        return call(body, outs, specs, scratch, kernel.func.__name__[:-7], work, limit)(*args)

    marks, pay_a, pay_b = run(
        functools.partial(face_kernel, shape, blocks), block_level, populations,
        outs=[whole(3, 3, *tile), real(*yface), real(*yface)],
        specs="hh",
        scratch=[pltpu.SMEM(block_level.shape, jnp.int32)]
        + room((27, nx, nz), (27, nx, nz))
        + [pltpu.SemaphoreType.DMA((3,))]
        + room(yface, yface),
        limit=FACE_BYTES,
    )
    ya, yb = swap(pay_a, "by", 0), swap(pay_b, "by", 1)
    table, g, calm = run(
        functools.partial(first_kernel), marks, populations,
        outs=[real(5, 3, 3, ny, nz), real(*populations.shape), real(2, 9, ny, nz)],
        specs="vv", work=3,
    )
    pay_a, pay_b = run(
        functools.partial(side_kernel), marks, populations, g, calm, ya, yb,
        outs=[real(*xface)] * 2, specs="vvvvvv", scratch=room(yface, yface, xface, xface),
    )
    xa, xb = swap(pay_a, "bx", 0), swap(pay_b, "bx", 1)
    sums, inner, up, down, moves = run(
        functools.partial(inner_kernel, blocks),
        new_slot, marks, populations, g, table, ya, yb, pay_a,
        outs=[
            real(3, 3, 2, nx, ny, nz), real(8, nx * ROWS, nz), real(*yedge), real(*yedge),
            whole(4, *tile),
        ],
        specs="svvvvvva",
        scratch=room(yface, yface, (27, ny, nz)),
        work=10,
    )
    part, pay_a, away = run(
        functools.partial(outer_kernel),
        marks, populations, g, table, ya, yb, xa, xb, sums, up, down,
        outs=[real(8, 4 * ROWS, nz), real(6, nx, nz), real(*yedge)],
        specs="vvvvvvvvvvv",
        scratch=room(
            yface, yface, xface, xface, (27, ny, nz), (3, 3, 2, 4, ny, nz), yedge, yedge
        ),
    )
    got_a = swap(pay_a, "by", 0)
    (outer,) = run(
        functools.partial(turn_kernel), part, outs=[real(8, 4 * ROWS, nz)], specs="v"
    )
    part, block, pay_w = run(
        functools.partial(pack_kernel), moves, inner, outer, got_a,
        outs=[real(8, nx * ROWS, nz), real(8, nx, nz), real(12, nx, nz)], specs="vvvv",
    )
    got_w = swap_ends(pay_w)
    (pay_b,) = run(
        functools.partial(join_kernel), away, block, outs=[real(11, nx, nz)], specs="vv"
    )
    got_b = swap(pay_b, "by", 1)
    cells = nx * ny * nz // blocks
    results = [real(blocks, cells), real(3, blocks, cells)]
    rho, vel, pay_a = run(
        functools.partial(moments_kernel), moves, part, got_b, got_w,
        outs=results + [real(11, nx, nz)],
        specs="vvvv",
        scratch=room((8, nx * ROWS, nz)),
    )
    got_a = swap(pay_a, "by", 0)
    return tuple(
        run(
            functools.partial(place_kernel), moves, rho, vel, away, got_a, got_b, got_w,
            outs=results, specs="vvvvvvv", scratch=room((8, nx, nz), yedge),
        )
    )


def solution(mesh):
    in_specs = (P(None, "bx", "by", None), P(), P(("bx", "by")))
    out_specs = (P(("bx", "by"), None), P(None, ("bx", "by"), None))
    return jax.shard_map(
        on_device, mesh=mesh, in_specs=in_specs, out_specs=out_specs, check_vma=False
    )
```

```python
import functools
import math

import jax
import jax.numpy as jnp
import numpy as np
from jax import lax
from jax.experimental import pallas as pl
from jax.experimental.pallas import tpu as pltpu
from jax.sharding import PartitionSpec as P

tau_coarse = 0.56
tau_fine = 0.62
scale_to_fine = tau_fine / (2.0 * tau_coarse)
scale_to_coarse = 2.0 * tau_coarse / tau_fine
smagorinsky = 18.0 * math.sqrt(2.0) * 0.17 * 0.17
weights = (8.0 / 27, 2.0 / 27, 1.0 / 54, 1.0 / 216)
ROWS = 8
LANES = 128
VMEM_BYTES = 16 * 1024 * 1024
FACE_BYTES = 53 * 1024 * 1024


def comp(a, b, e):
    return 9 * (a + 1) + 3 * (b + 1) + (e + 1)


def face(b, e):
    return 3 * (b + 1) + (e + 1)


DIRS = [(a, b, e) for a in (-1, 0, 1) for b in (-1, 0, 1) for e in (-1, 0, 1)]
HALF = [c for c in DIRS if c > (0, 0, 0)]


def lane_block(edge):
    return lax.broadcasted_iota(jnp.int32, (ROWS, LANES), 1) // edge


def sublane():
    return lax.broadcasted_iota(jnp.int32, (ROWS, LANES), 0)


def column_level(levels, shape, blocks, dx, dy):
    count_x, count_y = shape
    ix = lax.rem(lax.axis_index("bx") + (dx + count_x), count_x)
    iy = lax.rem(lax.axis_index("by") + (dy + count_y), count_y)
    base = (ix * count_y + iy) * blocks
    line = jnp.broadcast_to(levels[pl.ds(base // LANES, 1), :], (ROWS, LANES))
    line = pltpu.roll(line, lax.rem(LANES - lax.rem(base, LANES), LANES), 1)
    return jnp.take_along_axis(line, lane_block(LANES // blocks), axis=1)


def lane_roll(tile, by):
    return tile if by == 0 else pltpu.roll(tile, by % LANES, 1)


def group_sums(get):
    total, diff, quad = {}, {}, {}
    for b in (-1, 0, 1):
        low, mid, high = (get(b, e) for e in (-1, 0, 1))
        quad[b] = low + high
        total[b] = quad[b] + mid
        diff[b] = high - low
    both = total[-1] + total[1]
    return (
        both + total[0],
        total[1] - total[-1],
        both,
        diff[-1] + diff[0] + diff[1],
        diff[1] - diff[-1],
        quad[-1] + quad[0] + quad[1],
    )


def add_sums(first, second):
    return tuple(p + q for p, q in zip(first, second))


def collide(groups, get, fine, everywhere, factor, put, dirs=None):
    low, mid, high = (groups[a] for a in (-1, 0, 1))
    ends = add_sums(low, high)
    rho, jy, pyy, jz, pyz, pzz = add_sums(ends, mid)
    pxx = ends[0]
    jx, pxy, pxz = high[0] - low[0], high[1] - low[1], high[3] - low[3]
    inv = 1.0 / rho
    ux, uy, uz = jx * inv, jy * inv, jz * inv
    third = rho * (1.0 / 3.0)
    pxx = pxx - third - jx * ux
    pyy = pyy - third - jy * uy
    pzz = pzz - third - jz * uz
    pxy = pxy - jx * uy
    pxz = pxz - jx * uz
    pyz = pyz - jy * uz
    norm = jnp.sqrt(
        pxx * pxx + pyy * pyy + pzz * pzz + 2.0 * (pxy * pxy + pxz * pxz + pyz * pyz)
    )
    base_time = jnp.where(fine, tau_fine, tau_coarse)
    tau = 0.5 * (base_time + jnp.sqrt(base_time * base_time + smagorinsky * norm * inv))
    keep = 1.0 - 1.0 / tau
    if not everywhere:
        keep = jnp.where(fine, keep, 1.0)
    base = 1.0 - 1.5 * (ux * ux + uy * uy + uz * uz)
    scaled = [rho * w for w in weights]
    rest = [s * base for s in scaled]
    vx, vy, vz = 3.0 * ux, 3.0 * uy, 3.0 * uz
    vel = {(0, 0, 1): vz, (0, 1, 0): vy, (1, 0, 0): vx}
    vel[0, 1, 1], vel[0, 1, -1] = vy + vz, vy - vz
    vel[1, 0, 1], vel[1, 0, -1] = vx + vz, vx - vz
    vel[1, 1, 0], vel[1, -1, 0] = vx + vy, vx - vy
    for b in (-1, 1):
        for e in (-1, 1):
            vel[1, b, e] = vel[1, b, 0] + (vz if e > 0 else -vz)

    def emit(c, balance):
        if dirs is not None and c not in dirs:
            return
        gain = keep if c == (0, 0, 0) else keep * factor(c)
        put(c, balance + gain * (get(c) - balance))

    emit((0, 0, 0), rest[0])
    for c in HALF:
        n = sum(abs(k) for k in c)
        odd = scaled[n] * vel[c]
        even = rest[n] + 0.5 * odd * vel[c]
        emit(c, even + odd)
        emit(tuple(-k for k in c), even - odd)


def sums_of(get):
    return {a: group_sums(lambda b, e, a=a: get((a, b, e))) for a in (-1, 0, 1)}


def level_factor(here, there_rows, e):
    scale = jnp.where(here == 1, scale_to_coarse, scale_to_fine)
    return jnp.where(lane_roll(there_rows, -e) != here, scale, 1.0)


def fill_factors(marks, table):
    row = sublane()
    for k, (own, dx) in enumerate(((0, -1), (0, 0), (0, 1), (-1, 0), (1, 0))):
        here = marks[own + 1, 1, :, :]
        near = [marks[dx + 1, b, :, :] for b in range(3)]
        for e in (-1, 0, 1):
            plain = level_factor(here, near[1], e)
            for b in (-1, 0, 1):
                low, high = plain, plain
                if b == -1:
                    low = jnp.where(row == 0, level_factor(here, near[0], e), plain)
                if b == 1:
                    high = jnp.where(row == ROWS - 1, level_factor(here, near[2], e), plain)
                table[k, b + 1, e + 1, 0:8, :] = low
                table[k, b + 1, e + 1, 8:16, :] = high


def x_side(a, x, last):
    if a == 0:
        return 1
    return jnp.where(x == (0 if a < 0 else last), 1 + a, 1)


def store_by_parity(odd, first, second, up, down):
    @pl.when(odd == 0)
    def _():
        if first is not None:
            first[...] = up[...]
        second[...] = down[...]

    @pl.when(odd == 1)
    def _():
        if first is not None:
            first[...] = down[...]
        second[...] = up[...]


def fetch_kernel(f, high, low, sems):
    ny = f.shape[2]
    copies = [
        pltpu.make_async_copy(f.at[:, :, ny - 1, :], high, sems.at[0]),
        pltpu.make_async_copy(f.at[:, :, 0, :], low, sems.at[1]),
    ]
    for copy in copies:
        copy.start()
    for copy in copies:
        copy.wait()


def face_kernel(shape, blocks, levels, high, low, marks, pay_a, pay_b, up, down):
    nx = high.shape[1]
    for dx in (-1, 0, 1):
        for dy in (-1, 0, 1):
            marks[dx + 1, dy + 1, :, :] = column_level(levels, shape, blocks, dx, dy)
    here = marks[1, 1, :, :]
    row = sublane()
    for b, rows, pay in ((1, high, up), (-1, low, down)):
        near = [marks[dx, b + 1, :, :] for dx in range(3)]
        plain = {e: level_factor(here, near[1], e) for e in (-1, 0, 1)}
        for x in range(0, nx, ROWS):

            def get(c):
                return rows[comp(*c), x : x + ROWS, :]

            def factor(c):
                if c[0] == -1 and x == 0:
                    return jnp.where(row == 0, level_factor(here, near[0], c[2]), plain[c[2]])
                if c[0] == 1 and x + ROWS == nx:
                    return jnp.where(
                        row == ROWS - 1, level_factor(here, near[2], c[2]), plain[c[2]]
                    )
                return plain[c[2]]

            def put(c, value):
                pay[face(c[0], c[2]), x : x + ROWS, :] = value

            collide(
                sums_of(get), get, here == 1, False, factor, put, [c for c in DIRS if c[1] == b]
            )
    store_by_parity(lax.rem(lax.axis_index("by"), 2), pay_a, pay_b, up, down)


def first_collide(f, table, fine, x, near, put):
    for h in (0, 1):
        rows = slice(8 * h, 8 * h + 8)

        def get(c):
            return f[comp(*c), x, rows, :]

        def factor(c):
            return table[near(c[0]), c[1] + 1, c[2] + 1, rows, :]

        collide(sums_of(get), get, fine, False, factor, lambda c, value: put(c, rows, value))


def first_kernel(marks, f, table, out, calm):
    fill_factors(marks, table)
    fine = marks[1, 1, :, :] == 1
    nx = f.shape[1]
    for n, (x, a) in enumerate(((0, -1), (nx - 1, 1))):
        for h in (0, 1):
            rows = slice(8 * h, 8 * h + 8)

            def get(c):
                return f[comp(*c), x, rows, :]

            def put(c, value):
                calm[n, face(c[1], c[2]), rows, :] = value

            collide(
                sums_of(get), get, fine, True,
                lambda c: table[1 + c[0], c[1] + 1, c[2] + 1, rows, :],
                put, [c for c in DIRS if c[0] == a],
            )

    def layer(x, carry):
        def near(a):
            return 1 if a == 0 else jnp.where(x == (0 if a < 0 else nx - 1), 1 + a, 1)

        def put(c, rows, value):
            out[comp(*c), x, rows, :] = value

        first_collide(f, table, fine, x, near, put)
        return carry

    lax.fori_loop(0, nx, layer, 0)


def shifted_read(g, above, below, row, c, x, h):
    a, b, e = c
    i = comp(a, b, e)
    if b == 0:
        tile = g[i, x, 8 * h : 8 * h + 8, :]
    elif b == 1:
        if h == 1:
            tile = g[i, x, 7:15, :]
        else:
            tile = pltpu.roll(g[i, x, 0:8, :], 1, 0)
            tile = jnp.where(row == 0, below[face(a, e), pl.ds(x, 1), :], tile)
    else:
        if h == 0:
            tile = g[i, x, 1:9, :]
        else:
            tile = pltpu.roll(g[i, x, 8:16, :], 7, 0)
            tile = jnp.where(row == 7, above[face(a, e), pl.ds(x, 1), :], tile)
    return lane_roll(tile, e)


def load_by_parity(odd, first, second, above, below):
    @pl.when(odd == 0)
    def _():
        above[...] = first[...]
        below[...] = second[...]

    @pl.when(odd == 1)
    def _():
        above[...] = second[...]
        below[...] = first[...]


def side_kernel(marks, f, g, calm, got_a, got_b, pay_a, pay_b, above, below, up, down):
    load_by_parity(lax.rem(lax.axis_index("by"), 2), got_a, got_b, above, below)
    fine = marks[1, 1, :, :] == 1
    row = sublane()
    nx = f.shape[1]
    for n, (ad, x, pay) in enumerate(((-1, 0, down), (1, nx - 1, up))):
        for h in (0, 1):
            rows = slice(8 * h, 8 * h + 8)

            def flat(b, e):
                return shifted_read(g, above, below, row, (0, b, e), x, h)

            for b in (-1, 0, 1):
                for e in (-1, 0, 1):
                    c, j = (ad, b, e), face(b, e)
                    pay[j, rows, :] = shifted_read(g, above, below, row, c, x, h)
                    moved = shifted_read(g, above, below, row, c, x - ad, h)
                    pay[9 + j, rows, :] = jnp.where(fine, moved, calm[n, j, rows, :])
            for m, part in enumerate(group_sums(flat)):
                pay[18 + m, rows, :] = part
    store_by_parity(lax.rem(lax.axis_index("bx"), 2), pay_a, pay_b, up, down)


def second_collide(groups, get, fine, factor, put, dirs, known=None):
    made = {}

    def keep(c, value):
        made[c] = value if known is None else jnp.where(fine, value, known(c))

    collide(groups, get, fine, True, factor, keep, dirs)
    for a in (-1, 0, 1):
        if dirs is not None and (a, 0, 0) not in dirs:
            continue
        for b in (-1, 0, 1):
            plus = lane_roll(made[a, b, 1], 1)
            minus = lane_roll(made[a, b, -1], -1)
            put(a, b, made[a, b, 0] + (plus + minus), plus - minus)


def gather_layer(sums, row, put, up, down):
    total, cross, along = {}, {}, {}
    for b in (-1, 0, 1):
        for h in (0, 1):
            low, mid, high = (sums(a, b, 0, h) for a in (1, 0, -1))
            total[b, h] = low + mid + high
            cross[b, h] = low - high
            along[b, h] = sums(1, b, 1, h) + sums(0, b, 1, h) + sums(-1, b, 1, h)
    for n, part in enumerate((total, cross, along)):
        up(n, part[1, 1][7:8])
        down(n, part[-1, 0][0:1])
        rise = [pltpu.roll(part[1, h], 1, 0) for h in (0, 1)]
        fall = [pltpu.roll(part[-1, h], 7, 0) for h in (0, 1)]
        rise = [jnp.where(row == 0, 0.0, rise[0]), jnp.where(row == 0, rise[0], rise[1])]
        fall = [jnp.where(row == 7, fall[1], fall[0]), jnp.where(row == 7, 0.0, fall[1])]
        for h in (0, 1):
            put((0, 1, 3)[n], h, part[0, h] + rise[h] + fall[h])
            if n == 0:
                put(2, h, rise[h] - fall[h])


def turns():
    row = sublane()
    reflect = (lane_block(LANES // ROWS) - row) & (ROWS - 1)
    turn = (lane_block(1) + row * (LANES // ROWS)) & (LANES - 1)
    return reflect, turn


def block_rows(tile, reflect, turn):
    tile = pltpu.roll(tile, 0, 1, stride=LANES // ROWS, stride_axis=0)
    tile = jnp.take_along_axis(tile, reflect, axis=0)
    return jnp.take_along_axis(tile, turn, axis=1)


def leaving(slots, blocks, step):
    here = lax.axis_index("bx") * lax.axis_size("by") + lax.axis_index("by")
    which, theirs = jnp.int32(-1), jnp.int32(0)
    for k in range(blocks):
        goes = slots[k] // blocks == here + step
        which = jnp.where(goes, k, which)
        theirs = jnp.where(goes, lax.rem(slots[k], blocks), theirs)
    return which, theirs


def inner_kernel(
    blocks, slots, marks, f, g, table, ya, yb, tie, sums, made, up, down, moves,
    above, below, state,
):
    load_by_parity(lax.rem(lax.axis_index("by"), 2), ya, yb, above, below)
    for n, step in enumerate((1, -1)):
        which, theirs = leaving(slots, blocks, step)
        moves[n, :, :] = jnp.full((ROWS, LANES), which, jnp.int32)
        moves[2 + n, :, :] = jnp.full((ROWS, LANES), theirs, jnp.int32)
    fine = marks[1, 1, :, :] == 1
    row = sublane()
    reflect, turn = turns()
    nx = f.shape[1]

    def second(x, carry):
        for h in (0, 1):
            rows = slice(8 * h, 8 * h + 8)

            def moved(c):
                tile = shifted_read(g, above, below, row, c, x - c[0], h)
                tile = jnp.where(fine, tile, f[comp(*c), x, rows, :])
                state[comp(*c), rows, :] = tile
                return tile

            def put(a, b, total, along):
                sums[a + 1, b + 1, 0, x, rows, :] = total
                sums[a + 1, b + 1, 1, x, rows, :] = along

            second_collide(
                sums_of(moved),
                lambda c: state[comp(*c), rows, :],
                fine,
                lambda c: table[1, c[1] + 1, c[2] + 1, rows, :],
                put,
                None,
            )
        return carry

    lax.fori_loop(1, nx - 1, second, 0)

    def gather(x, carry):
        def put(n, h, tile):
            made[2 * n + h, pl.ds(x * ROWS, ROWS), :] = block_rows(tile, reflect, turn)

        def put_up(n, value):
            up[n, pl.ds(x, 1), :] = value

        def put_down(n, value):
            down[n, pl.ds(x, 1), :] = value

        gather_layer(
            lambda a, b, q, h: sums[a + 1, b + 1, q, x - a, 8 * h : 8 * h + 8, :],
            row, put, put_up, put_down,
        )
        return carry

    lax.fori_loop(2, nx - 2, gather, 0)


def outer_kernel(
    marks, f, g, table, ya, yb, xa, xb, sums, in_up, in_down,
    part, pay, away, above, below, right, left, state, ends, up, down,
):
    load_by_parity(lax.rem(lax.axis_index("by"), 2), ya, yb, above, below)
    load_by_parity(lax.rem(lax.axis_index("bx"), 2), xa, xb, right, left)
    fine = {dx: marks[dx + 1, 1, :, :] == 1 for dx in (-1, 0, 1)}
    row = sublane()
    reflect, turn = turns()
    nx = f.shape[1]
    hold = {-1: 0, 0: 1, nx - 1: 2, nx: 3}
    for side, x, k, got in ((-1, 0, 3, left), (1, nx - 1, 4, right)):
        for h in (0, 1):
            rows = slice(8 * h, 8 * h + 8)

            def keep(slot):
                def put(a, b, total, along):
                    ends[a + 1, b + 1, 0, slot, rows, :] = total
                    ends[a + 1, b + 1, 1, slot, rows, :] = along

                return put

            def read(c, x):
                return shifted_read(g, above, below, row, c, x, h)

            def moved(c):
                a, b, e = c
                if a == -side:
                    tile = got[face(b, e), rows, :]
                else:
                    tile = read(c, x - a)
                tile = jnp.where(fine[0], tile, f[comp(*c), x, rows, :])
                state[comp(*c), rows, :] = tile
                return tile

            second_collide(
                sums_of(moved),
                lambda c: state[comp(*c), rows, :],
                fine[0],
                lambda c: table[1, c[1] + 1, c[2] + 1, rows, :],
                keep(hold[x]),
                [c for c in DIRS if c[0] != side],
            )

            def toward(c):
                return got[9 + face(c[1], c[2]), rows, :]

            second_collide(
                {
                    side: group_sums(lambda b, e: read((side, b, e), x)),
                    0: tuple(got[18 + n, rows, :] for n in range(6)),
                    -side: group_sums(lambda b, e: toward((-side, b, e))),
                },
                toward,
                fine[side],
                lambda c: table[k, c[1] + 1, c[2] + 1, rows, :],
                keep(hold[x + side]),
                [c for c in DIRS if c[0] == -side],
                toward,
            )
    up[...] = in_up[...]
    down[...] = in_down[...]
    for m, x in enumerate((0, 1, nx - 2, nx - 1)):

        def fetch(a, b, q, h):
            rows = slice(8 * h, 8 * h + 8)
            if x - a in hold:
                return ends[a + 1, b + 1, q, hold[x - a], rows, :]
            return sums[a + 1, b + 1, q, x - a, rows, :]

        def put(n, h, tile):
            part[2 * n + h, ROWS * m : ROWS * m + ROWS, :] = tile

        def put_up(n, value):
            up[n, x : x + 1, :] = value

        def put_down(n, value):
            down[n, x : x + 1, :] = value

        gather_layer(fetch, row, put, put_up, put_down)
    for edge in (up, down):
        for n in range(3):
            for x in range(0, nx, ROWS):
                rows = slice(x, x + ROWS)
                edge[n, rows, :] = block_rows(edge[n, rows, :], reflect, turn)
    odd = lax.rem(lax.axis_index("by"), 2)
    store_by_parity(odd, pay.at[pl.ds(0, 3)], pay.at[pl.ds(3, 3)], up, down)
    store_by_parity(odd, None, away, up, down)


def turn_kernel(part, out):
    reflect, turn = turns()
    for n in range(part.shape[0]):
        for m in range(4):
            rows = slice(ROWS * m, ROWS * m + ROWS)
            out[n, rows, :] = block_rows(part[n, rows, :], reflect, turn)


def add_crossed(made, crossed, top):
    nx = crossed.shape[1]
    width = LANES // ROWS
    spot = top * (ROWS - 1)
    sign = jnp.where(top == 1, -1.0, 1.0)
    mask = lane_block(width) == spot
    for x in range(nx):
        rows = slice(ROWS * x, ROWS * x + ROWS)
        first = x // ROWS * ROWS
        shift = lax.rem(width * (spot - x % ROWS) + LANES, LANES)
        total, cross, along = (
            jnp.where(mask, pltpu.roll(crossed[n, first : first + ROWS, :], shift, 1), 0.0)
            for n in range(3)
        )
        for n, more in enumerate((total, cross, sign * total, along)):
            made[2 * n + top, rows, :] += more


def pack_block(made, pay, start, which):
    for n in range(8):
        pay[start + n, :, :] = made[n, pl.ds(which, pay.shape[1], stride=ROWS), :]


def number(tile):
    return jnp.maximum(jnp.max(tile), 0)


def pack_kernel(moves, inner, outer, got, made, block, pay_w):
    iy = lax.axis_index("by")
    odd = lax.rem(iy, 2)
    nx = got.shape[1]
    low, high = ROWS * 2, ROWS * (nx - 2)
    made[:, 0:low, :] = outer[:, 0:low, :]
    made[:, low:high, :] = inner[:, low:high, :]
    made[:, high:, :] = outer[:, low:, :]
    add_crossed(made, got, 1 - odd)
    pack_block(made, block, 0, number(moves[1 - odd, :, :]))
    end = jnp.logical_or(iy == 0, iy == lax.axis_size("by") - 1)

    @pl.when(end)
    def _():
        pay_w[0:8, :, :] = block[...]

    @pl.when(jnp.logical_not(end))
    def _():
        pay_w[0:3, :, :] = got[3:6, :, :]


def join_kernel(first, second, out):
    out[0 : first.shape[0], :, :] = first[...]
    out[first.shape[0] :, :, :] = second[...]


def moments_kernel(moves, part, got_b, got_w, rho_out, vel_out, pay_a, made):
    odd = lax.rem(lax.axis_index("by"), 2)
    nx = got_b.shape[1]
    made[...] = part[...]
    add_crossed(made, got_b, odd)
    for x in range(nx):
        rows = slice(ROWS * x, ROWS * x + ROWS)
        for h in (0, 1):
            rho = made[h, rows, :]
            inv = 1.0 / rho
            lanes = slice((2 * x + h) * LANES, (2 * x + h + 1) * LANES)
            rho_out[:, lanes] = rho
            for n in range(1, 4):
                tile = made[2 * n + h, rows, :] * inv
                made[2 * n + h, rows, :] = tile
                vel_out[n - 1, :, lanes] = tile
    pack_block(made, pay_a, 0, number(moves[odd, :, :]))
    pay_a[8:11, :, :] = got_w[0:3, :, :]


def place_kernel(moves, rho, vel, away, got_a, got_b, got_w, rho_out, vel_out, block, crossed, made, sems):
    iy = lax.axis_index("by")
    odd = lax.rem(iy, 2)
    end = jnp.logical_or(iy == 0, iy == lax.axis_size("by") - 1)

    @pl.when(end)
    def _():
        block[...] = got_w[0:8, :, :]
        crossed[...] = got_a[8:11, :, :]

    @pl.when(jnp.logical_not(end))
    def _():
        block[...] = got_b[3:11, :, :]
        crossed[...] = away[...]

    row = sublane()
    width = LANES // ROWS
    top = 1 - odd
    sign = jnp.where(top == 1, -1.0, 1.0)
    mask = lane_block(width) == top * (ROWS - 1)
    spread = row * width + (lane_block(1) & (width - 1))
    theirs = number(moves[3 - odd, :, :])
    for first in range(0, block.shape[1], ROWS):
        rows = slice(first, first + ROWS)
        extra = []
        for n in range(3):
            line = jnp.broadcast_to(crossed[n, pl.ds(first + theirs, 1), :], (ROWS, LANES))
            extra.append(jnp.where(mask, jnp.take_along_axis(line, spread, axis=1), 0.0))
        total, cross, along = extra
        for n, more in enumerate((total, cross, sign * total, along)):
            block[2 * n + top, rows, :] += more
        for h in (0, 1):
            inv = 1.0 / block[h, rows, :]
            for n in range(1, 4):
                block[2 * n + h, rows, :] *= inv
    near = row == moves[odd, :, :]
    far = row == moves[1 - odd, :, :]
    copies = []
    for n in range(4):
        for x in range(block.shape[1]):
            for h in (0, 1):
                lanes = slice((2 * x + h) * LANES, (2 * x + h + 1) * LANES)
                k = 2 * n + h
                tile = rho[:, lanes] if n == 0 else vel[n - 1, :, lanes]
                tile = jnp.where(near, got_a[k, x : x + 1, :], tile)
                made[n, :, lanes] = jnp.where(far, block[k, x : x + 1, :], tile)
        target = rho_out if n == 0 else vel_out.at[n - 1]
        copies.append(pltpu.make_async_copy(made.at[n], target, sems.at[n]))
        copies[n].start()
    for copy in copies:
        copy.wait()


def swap(value, axis, odd):
    count_x, count_y = lax.axis_size("bx"), lax.axis_size("by")
    pairs = []
    if axis == "by":
        for x in range(count_x):
            for y in range(odd, count_y, 2):
                pairs.append((x * count_y + y, x * count_y + (y + 1) % count_y))
    else:
        for y in range(count_y):
            for x in range(odd, count_x, 2):
                pairs.append((x * count_y + y, (x + 1) % count_x * count_y + y))
    pairs = pairs + [(b, a) for a, b in pairs]
    return lax.ppermute(value, ("bx", "by"), pairs)


def swap_ends(value):
    count_x, count_y = lax.axis_size("bx"), lax.axis_size("by")
    pairs = []
    for x in range(count_x):
        here, after = x * count_y, (x + 1) * count_y
        if x + 1 < count_x:
            pairs += [(after - 1, after), (after, after - 1)]
            pairs += [(here + 1, after + 1), (after + count_y - 2, after - 2)]
        pairs += [(here + y, here + (y ^ 1)) for y in range(2, count_y - 2)]
    pairs += [(0, 1), (after - 1, after - 2)]
    pairs += [(after - count_y + 1, after - 1), (count_y - 2, 0)]
    return lax.ppermute(value, ("bx", "by"), pairs)


def call(kernel, outs, specs, scratch, name, work, limit, kept):
    space = {"v": pltpu.VMEM, "s": pltpu.SMEM, "h": pltpu.HBM, "a": pl.ANY}
    return pl.pallas_call(
        kernel,
        out_shape=outs,
        in_specs=[pl.BlockSpec(memory_space=space[k]) for k in specs],
        out_specs=[pl.BlockSpec(memory_space=pltpu.VMEM if kept else pl.ANY)] * len(outs),
        scratch_shapes=scratch,
        compiler_params=pltpu.CompilerParams(vmem_limit_bytes=limit),
        cost_estimate=pl.CostEstimate(
            flops=work * 2000000, bytes_accessed=work * 1000000, transcendentals=0
        ),
        name=name,
    )


def on_device(populations, block_level, new_slot):
    shape = (lax.axis_size("bx"), lax.axis_size("by"))
    blocks = new_slot.shape[0]
    _, nx, ny, nz = populations.shape
    yface, xface, yedge = (9, nx, nz), (24, ny, nz), (3, nx, nz)
    tile = (ROWS, nz)

    def real(*dims):
        return jax.ShapeDtypeStruct(dims, jnp.float32)

    def whole(*dims):
        return jax.ShapeDtypeStruct(dims, jnp.int32)

    def room(*shapes):
        return [pltpu.VMEM(dims, jnp.float32) for dims in shapes]

    def run(kernel, *args, outs, specs, scratch=(), work=1, limit=VMEM_BYTES, kept=True):
        def body(*refs):
            kernel(*refs)

        return call(body, outs, specs, scratch, kernel.func.__name__[:-7], work, limit, kept)(*args)

    high, low = run(
        functools.partial(fetch_kernel), populations,
        outs=[real(27, nx, nz)] * 2, specs="h", scratch=[pltpu.SemaphoreType.DMA((2,))],
        limit=FACE_BYTES,
    )
    marks, pay_a, pay_b = run(
        functools.partial(face_kernel, shape, blocks),
        block_level.reshape(block_level.shape[0] // nz, nz), high, low,
        outs=[whole(3, 3, *tile), real(*yface), real(*yface)],
        specs="vvv", scratch=room(yface, yface),
    )
    ya, yb = swap(pay_a, "by", 0), swap(pay_b, "by", 1)
    table, g, calm = run(
        functools.partial(first_kernel), marks, populations,
        outs=[real(5, 3, 3, ny, nz), real(*populations.shape), real(2, 9, ny, nz)],
        specs="vv", work=3,
    )
    pay_a, pay_b = run(
        functools.partial(side_kernel), marks, populations, g, calm, ya, yb,
        outs=[real(*xface)] * 2, specs="vvvvvv", scratch=room(yface, yface, xface, xface),
    )
    xa, xb = swap(pay_a, "bx", 0), swap(pay_b, "bx", 1)
    sums, inner, up, down, moves = run(
        functools.partial(inner_kernel, blocks),
        new_slot, marks, populations, g, table, ya, yb, pay_a,
        outs=[
            real(3, 3, 2, nx, ny, nz), real(8, nx * ROWS, nz), real(*yedge), real(*yedge),
            whole(4, *tile),
        ],
        specs="svvvvvva",
        scratch=room(yface, yface, (27, ny, nz)),
        work=10,
    )
    part, pay_a, away = run(
        functools.partial(outer_kernel),
        marks, populations, g, table, ya, yb, xa, xb, sums, up, down,
        outs=[real(8, 4 * ROWS, nz), real(6, nx, nz), real(*yedge)],
        specs="vvvvvvvvvvv",
        scratch=room(
            yface, yface, xface, xface, (27, ny, nz), (3, 3, 2, 4, ny, nz), yedge, yedge
        ),
    )
    got_a = swap(pay_a, "by", 0)
    (outer,) = run(
        functools.partial(turn_kernel), part, outs=[real(8, 4 * ROWS, nz)], specs="v"
    )
    part, block, pay_w = run(
        functools.partial(pack_kernel), moves, inner, outer, got_a,
        outs=[real(8, nx * ROWS, nz), real(8, nx, nz), real(12, nx, nz)], specs="vvvv",
    )
    got_w = swap_ends(pay_w)
    (pay_b,) = run(
        functools.partial(join_kernel), away, block, outs=[real(11, nx, nz)], specs="vv"
    )
    got_b = swap(pay_b, "by", 1)
    cells = nx * ny * nz // blocks
    results = [real(blocks, cells), real(3, blocks, cells)]
    rho, vel, pay_a = run(
        functools.partial(moments_kernel), moves, part, got_b, got_w,
        outs=results + [real(11, nx, nz)],
        specs="vvvv",
        scratch=room((8, nx * ROWS, nz)),
    )
    got_a = swap(pay_a, "by", 0)
    return tuple(
        run(
            functools.partial(place_kernel), moves, rho, vel, away, got_a, got_b, got_w,
            outs=results, specs="vvvvvvv", kept=False,
            scratch=room((8, nx, nz), yedge, (4, blocks, cells)) + [pltpu.SemaphoreType.DMA((4,))],
        )
    )


def solution(mesh):
    in_specs = (P(None, "bx", "by", None), P(), P(("bx", "by")))
    out_specs = (P(("bx", "by"), None), P(None, ("bx", "by"), None))
    return jax.shard_map(
        on_device, mesh=mesh, in_specs=in_specs, out_specs=out_specs, check_vma=False
    )
```

```python
import functools
import math

import jax
import jax.numpy as jnp
import numpy as np
from jax import lax
from jax.experimental import pallas as pl
from jax.experimental.pallas import tpu as pltpu
from jax.sharding import PartitionSpec as P

tau_coarse = 0.56
tau_fine = 0.62
scale_to_fine = tau_fine / (2.0 * tau_coarse)
scale_to_coarse = 2.0 * tau_coarse / tau_fine
smagorinsky = 18.0 * math.sqrt(2.0) * 0.17 * 0.17
weights = (8.0 / 27, 2.0 / 27, 1.0 / 54, 1.0 / 216)
ROWS = 8
LANES = 128
VMEM_BYTES = 16 * 1024 * 1024
FACE_BYTES = 53 * 1024 * 1024


def comp(a, b, e):
    return 9 * (a + 1) + 3 * (b + 1) + (e + 1)


def face(b, e):
    return 3 * (b + 1) + (e + 1)


DIRS = [(a, b, e) for a in (-1, 0, 1) for b in (-1, 0, 1) for e in (-1, 0, 1)]
HALF = [c for c in DIRS if c > (0, 0, 0)]


def lane_block(edge):
    return lax.broadcasted_iota(jnp.int32, (ROWS, LANES), 1) // edge


def sublane():
    return lax.broadcasted_iota(jnp.int32, (ROWS, LANES), 0)


def column_level(levels, shape, blocks, dx, dy):
    count_x, count_y = shape
    ix = lax.rem(lax.axis_index("bx") + (dx + count_x), count_x)
    iy = lax.rem(lax.axis_index("by") + (dy + count_y), count_y)
    base = (ix * count_y + iy) * blocks
    line = jnp.broadcast_to(levels[pl.ds(base // LANES, 1), :], (ROWS, LANES))
    line = pltpu.roll(line, lax.rem(LANES - lax.rem(base, LANES), LANES), 1)
    return jnp.take_along_axis(line, lane_block(LANES // blocks), axis=1)


def lane_roll(tile, by):
    return tile if by == 0 else pltpu.roll(tile, by % LANES, 1)


def group_sums(get):
    total, diff, quad = {}, {}, {}
    for b in (-1, 0, 1):
        low, mid, high = (get(b, e) for e in (-1, 0, 1))
        quad[b] = low + high
        total[b] = quad[b] + mid
        diff[b] = high - low
    both = total[-1] + total[1]
    return (
        both + total[0],
        total[1] - total[-1],
        both,
        diff[-1] + diff[0] + diff[1],
        diff[1] - diff[-1],
        quad[-1] + quad[0] + quad[1],
    )


def add_sums(first, second):
    return tuple(p + q for p, q in zip(first, second))


def collide(groups, get, fine, everywhere, factor, put, dirs=None):
    low, mid, high = (groups[a] for a in (-1, 0, 1))
    ends = add_sums(low, high)
    rho, jy, pyy, jz, pyz, pzz = add_sums(ends, mid)
    pxx = ends[0]
    jx, pxy, pxz = high[0] - low[0], high[1] - low[1], high[3] - low[3]
    inv = 1.0 / rho
    ux, uy, uz = jx * inv, jy * inv, jz * inv
    third = rho * (1.0 / 3.0)
    pxx = pxx - third - jx * ux
    pyy = pyy - third - jy * uy
    pzz = pzz - third - jz * uz
    pxy = pxy - jx * uy
    pxz = pxz - jx * uz
    pyz = pyz - jy * uz
    norm = jnp.sqrt(
        pxx * pxx + pyy * pyy + pzz * pzz + 2.0 * (pxy * pxy + pxz * pxz + pyz * pyz)
    )
    base_time = jnp.where(fine, tau_fine, tau_coarse)
    tau = 0.5 * (base_time + jnp.sqrt(base_time * base_time + smagorinsky * norm * inv))
    keep = 1.0 - 1.0 / tau
    if not everywhere:
        keep = jnp.where(fine, keep, 1.0)
    base = 1.0 - 1.5 * (ux * ux + uy * uy + uz * uz)
    scaled = [rho * w for w in weights]
    rest = [s * base for s in scaled]
    vx, vy, vz = 3.0 * ux, 3.0 * uy, 3.0 * uz
    vel = {(0, 0, 1): vz, (0, 1, 0): vy, (1, 0, 0): vx}
    vel[0, 1, 1], vel[0, 1, -1] = vy + vz, vy - vz
    vel[1, 0, 1], vel[1, 0, -1] = vx + vz, vx - vz
    vel[1, 1, 0], vel[1, -1, 0] = vx + vy, vx - vy
    for b in (-1, 1):
        for e in (-1, 1):
            vel[1, b, e] = vel[1, b, 0] + (vz if e > 0 else -vz)

    def emit(c, balance):
        if dirs is not None and c not in dirs:
            return
        gain = keep if c == (0, 0, 0) else keep * factor(c)
        put(c, balance + gain * (get(c) - balance))

    emit((0, 0, 0), rest[0])
    for c in HALF:
        n = sum(abs(k) for k in c)
        odd = scaled[n] * vel[c]
        even = rest[n] + 0.5 * odd * vel[c]
        emit(c, even + odd)
        emit(tuple(-k for k in c), even - odd)


def sums_of(get):
    return {a: group_sums(lambda b, e, a=a: get((a, b, e))) for a in (-1, 0, 1)}


def level_factor(here, there_rows, e):
    scale = jnp.where(here == 1, scale_to_coarse, scale_to_fine)
    return jnp.where(lane_roll(there_rows, -e) != here, scale, 1.0)


def fill_factors(marks, table):
    row = sublane()
    for k, (own, dx) in enumerate(((0, -1), (0, 0), (0, 1), (-1, 0), (1, 0))):
        here = marks[own + 1, 1, :, :]
        near = [marks[dx + 1, b, :, :] for b in range(3)]
        for e in (-1, 0, 1):
            plain = level_factor(here, near[1], e)
            for b in (-1, 0, 1):
                low, high = plain, plain
                if b == -1:
                    low = jnp.where(row == 0, level_factor(here, near[0], e), plain)
                if b == 1:
                    high = jnp.where(row == ROWS - 1, level_factor(here, near[2], e), plain)
                table[k, b + 1, e + 1, 0:8, :] = low
                table[k, b + 1, e + 1, 8:16, :] = high


def x_side(a, x, last):
    if a == 0:
        return 1
    return jnp.where(x == (0 if a < 0 else last), 1 + a, 1)


def store_by_parity(odd, first, second, up, down):
    @pl.when(odd == 0)
    def _():
        if first is not None:
            first[...] = up[...]
        second[...] = down[...]

    @pl.when(odd == 1)
    def _():
        if first is not None:
            first[...] = down[...]
        second[...] = up[...]


def fetch_kernel(f, high, low, sems):
    ny = f.shape[2]
    copies = [
        pltpu.make_async_copy(f.at[:, :, ny - 1, :], high, sems.at[0]),
        pltpu.make_async_copy(f.at[:, :, 0, :], low, sems.at[1]),
    ]
    for copy in copies:
        copy.start()
    for copy in copies:
        copy.wait()


def face_kernel(shape, blocks, levels, high, low, marks, pay_a, pay_b, up, down):
    nx = high.shape[1]
    for dx in (-1, 0, 1):
        for dy in (-1, 0, 1):
            marks[dx + 1, dy + 1, :, :] = column_level(levels, shape, blocks, dx, dy)
    here = marks[1, 1, :, :]
    row = sublane()
    for b, rows, pay in ((1, high, up), (-1, low, down)):
        near = [marks[dx, b + 1, :, :] for dx in range(3)]
        plain = {e: level_factor(here, near[1], e) for e in (-1, 0, 1)}
        for x in range(0, nx, ROWS):

            def get(c):
                return rows[comp(*c), x : x + ROWS, :]

            def factor(c):
                if c[0] == -1 and x == 0:
                    return jnp.where(row == 0, level_factor(here, near[0], c[2]), plain[c[2]])
                if c[0] == 1 and x + ROWS == nx:
                    return jnp.where(
                        row == ROWS - 1, level_factor(here, near[2], c[2]), plain[c[2]]
                    )
                return plain[c[2]]

            def put(c, value):
                pay[face(c[0], c[2]), x : x + ROWS, :] = value

            collide(
                sums_of(get), get, here == 1, False, factor, put, [c for c in DIRS if c[1] == b]
            )
    store_by_parity(lax.rem(lax.axis_index("by"), 2), pay_a, pay_b, up, down)


def first_collide(f, table, fine, x, near, put):
    for h in (0, 1):
        rows = slice(8 * h, 8 * h + 8)

        def get(c):
            return f[comp(*c), x, rows, :]

        def factor(c):
            return table[near(c[0]), c[1] + 1, c[2] + 1, rows, :]

        collide(sums_of(get), get, fine, False, factor, lambda c, value: put(c, rows, value))


def first_kernel(marks, f, table, out, calm):
    fill_factors(marks, table)
    fine = marks[1, 1, :, :] == 1
    nx = f.shape[1]
    for n, (x, a) in enumerate(((0, -1), (nx - 1, 1))):
        for h in (0, 1):
            rows = slice(8 * h, 8 * h + 8)

            def get(c):
                return f[comp(*c), x, rows, :]

            def put(c, value):
                calm[n, face(c[1], c[2]), rows, :] = value

            collide(
                sums_of(get), get, fine, True,
                lambda c: table[1 + c[0], c[1] + 1, c[2] + 1, rows, :],
                put, [c for c in DIRS if c[0] == a],
            )

    def layer(x, carry):
        def near(a):
            return 1 if a == 0 else jnp.where(x == (0 if a < 0 else nx - 1), 1 + a, 1)

        def put(c, rows, value):
            out[comp(*c), x, rows, :] = value

        first_collide(f, table, fine, x, near, put)
        return carry

    lax.fori_loop(0, nx, layer, 0)


def shifted_read(g, above, below, row, c, x, h):
    a, b, e = c
    i = comp(a, b, e)
    if b == 0:
        tile = g[i, x, 8 * h : 8 * h + 8, :]
    elif b == 1:
        if h == 1:
            tile = g[i, x, 7:15, :]
        else:
            tile = pltpu.roll(g[i, x, 0:8, :], 1, 0)
            tile = jnp.where(row == 0, below[face(a, e), pl.ds(x, 1), :], tile)
    else:
        if h == 0:
            tile = g[i, x, 1:9, :]
        else:
            tile = pltpu.roll(g[i, x, 8:16, :], 7, 0)
            tile = jnp.where(row == 7, above[face(a, e), pl.ds(x, 1), :], tile)
    return lane_roll(tile, e)


def load_by_parity(odd, first, second, above, below):
    @pl.when(odd == 0)
    def _():
        above[...] = first[...]
        below[...] = second[...]

    @pl.when(odd == 1)
    def _():
        above[...] = second[...]
        below[...] = first[...]


def side_kernel(marks, f, g, calm, got_a, got_b, pay_a, pay_b, above, below, up, down):
    load_by_parity(lax.rem(lax.axis_index("by"), 2), got_a, got_b, above, below)
    fine = marks[1, 1, :, :] == 1
    row = sublane()
    nx = f.shape[1]
    for n, (ad, x, pay) in enumerate(((-1, 0, down), (1, nx - 1, up))):
        for h in (0, 1):
            rows = slice(8 * h, 8 * h + 8)

            def flat(b, e):
                return shifted_read(g, above, below, row, (0, b, e), x, h)

            for b in (-1, 0, 1):
                for e in (-1, 0, 1):
                    c, j = (ad, b, e), face(b, e)
                    pay[j, rows, :] = shifted_read(g, above, below, row, c, x, h)
                    moved = shifted_read(g, above, below, row, c, x - ad, h)
                    pay[9 + j, rows, :] = jnp.where(fine, moved, calm[n, j, rows, :])
            for m, part in enumerate(group_sums(flat)):
                pay[18 + m, rows, :] = part
    store_by_parity(lax.rem(lax.axis_index("bx"), 2), pay_a.at[pl.ds(0, 24)], pay_b, up, down)


def second_collide(groups, get, fine, factor, put, dirs, known=None):
    made = {}

    def keep(c, value):
        made[c] = value if known is None else jnp.where(fine, value, known(c))

    collide(groups, get, fine, True, factor, keep, dirs)
    for a in (-1, 0, 1):
        if dirs is not None and (a, 0, 0) not in dirs:
            continue
        for b in (-1, 0, 1):
            plus = lane_roll(made[a, b, 1], 1)
            minus = lane_roll(made[a, b, -1], -1)
            put(a, b, made[a, b, 0] + (plus + minus), plus - minus)


def gather_layer(sums, row, put, up, down):
    total, cross, along = {}, {}, {}
    for b in (-1, 0, 1):
        for h in (0, 1):
            low, mid, high = (sums(a, b, 0, h) for a in (1, 0, -1))
            total[b, h] = low + mid + high
            cross[b, h] = low - high
            along[b, h] = sums(1, b, 1, h) + sums(0, b, 1, h) + sums(-1, b, 1, h)
    for n, part in enumerate((total, cross, along)):
        up(n, part[1, 1][7:8])
        down(n, part[-1, 0][0:1])
        rise = [pltpu.roll(part[1, h], 1, 0) for h in (0, 1)]
        fall = [pltpu.roll(part[-1, h], 7, 0) for h in (0, 1)]
        rise = [jnp.where(row == 0, 0.0, rise[0]), jnp.where(row == 0, rise[0], rise[1])]
        fall = [jnp.where(row == 7, fall[1], fall[0]), jnp.where(row == 7, 0.0, fall[1])]
        for h in (0, 1):
            put((0, 1, 3)[n], h, part[0, h] + rise[h] + fall[h])
            if n == 0:
                put(2, h, rise[h] - fall[h])


def turns():
    row = sublane()
    reflect = (lane_block(LANES // ROWS) - row) & (ROWS - 1)
    turn = (lane_block(1) + row * (LANES // ROWS)) & (LANES - 1)
    return reflect, turn


def block_rows(tile, reflect, turn):
    tile = pltpu.roll(tile, 0, 1, stride=LANES // ROWS, stride_axis=0)
    tile = jnp.take_along_axis(tile, reflect, axis=0)
    return jnp.take_along_axis(tile, turn, axis=1)


def leaving(slots, blocks, step):
    here = lax.axis_index("bx") * lax.axis_size("by") + lax.axis_index("by")
    which, theirs = jnp.int32(-1), jnp.int32(0)
    for k in range(blocks):
        goes = slots[k] // blocks == here + step
        which = jnp.where(goes, k, which)
        theirs = jnp.where(goes, lax.rem(slots[k], blocks), theirs)
    return which, theirs


def inner_kernel(
    blocks, slots, marks, f, g, table, ya, yb, tie, sums, made, up, down, moves,
    above, below, state,
):
    load_by_parity(lax.rem(lax.axis_index("by"), 2), ya, yb, above, below)
    for n, step in enumerate((1, -1)):
        which, theirs = leaving(slots, blocks, step)
        moves[n, :, :] = jnp.full((ROWS, LANES), which, jnp.int32)
        moves[2 + n, :, :] = jnp.full((ROWS, LANES), theirs, jnp.int32)
    fine = marks[1, 1, :, :] == 1
    row = sublane()
    reflect, turn = turns()
    nx = f.shape[1]

    def second(x, carry):
        for h in (0, 1):
            rows = slice(8 * h, 8 * h + 8)

            def moved(c):
                tile = shifted_read(g, above, below, row, c, x - c[0], h)
                tile = jnp.where(fine, tile, f[comp(*c), x, rows, :])
                state[comp(*c), rows, :] = tile
                return tile

            def put(a, b, total, along):
                sums[a + 1, b + 1, 0, x, rows, :] = total
                sums[a + 1, b + 1, 1, x, rows, :] = along

            second_collide(
                sums_of(moved),
                lambda c: state[comp(*c), rows, :],
                fine,
                lambda c: table[1, c[1] + 1, c[2] + 1, rows, :],
                put,
                None,
            )
        return carry

    lax.fori_loop(1, nx - 1, second, 0)

    def gather(x, carry):
        def put(n, h, tile):
            made[2 * n + h, pl.ds(x * ROWS, ROWS), :] = block_rows(tile, reflect, turn)

        def put_up(n, value):
            up[n, pl.ds(x, 1), :] = value

        def put_down(n, value):
            down[n, pl.ds(x, 1), :] = value

        gather_layer(
            lambda a, b, q, h: sums[a + 1, b + 1, q, x - a, 8 * h : 8 * h + 8, :],
            row, put, put_up, put_down,
        )
        return carry

    lax.fori_loop(2, nx - 2, gather, 0)


def outer_kernel(
    marks, f, g, table, ya, yb, xa, xb, sums, in_up, in_down,
    part, pay, away, above, below, right, left, state, ends, up, down,
):
    load_by_parity(lax.rem(lax.axis_index("by"), 2), ya, yb, above, below)
    load_by_parity(lax.rem(lax.axis_index("bx"), 2), xa.at[pl.ds(0, 24)], xb, right, left)
    fine = {dx: marks[dx + 1, 1, :, :] == 1 for dx in (-1, 0, 1)}
    row = sublane()
    reflect, turn = turns()
    nx = f.shape[1]
    hold = {-1: 0, 0: 1, nx - 1: 2, nx: 3}
    for side, x, k, got in ((-1, 0, 3, left), (1, nx - 1, 4, right)):
        for h in (0, 1):
            rows = slice(8 * h, 8 * h + 8)

            def keep(slot):
                def put(a, b, total, along):
                    ends[a + 1, b + 1, 0, slot, rows, :] = total
                    ends[a + 1, b + 1, 1, slot, rows, :] = along

                return put

            def read(c, x):
                return shifted_read(g, above, below, row, c, x, h)

            def moved(c):
                a, b, e = c
                if a == -side:
                    tile = got[face(b, e), rows, :]
                else:
                    tile = read(c, x - a)
                tile = jnp.where(fine[0], tile, f[comp(*c), x, rows, :])
                state[comp(*c), rows, :] = tile
                return tile

            second_collide(
                sums_of(moved),
                lambda c: state[comp(*c), rows, :],
                fine[0],
                lambda c: table[1, c[1] + 1, c[2] + 1, rows, :],
                keep(hold[x]),
                [c for c in DIRS if c[0] != side],
            )

            def toward(c):
                return got[9 + face(c[1], c[2]), rows, :]

            second_collide(
                {
                    side: group_sums(lambda b, e: read((side, b, e), x)),
                    0: tuple(got[18 + n, rows, :] for n in range(6)),
                    -side: group_sums(lambda b, e: toward((-side, b, e))),
                },
                toward,
                fine[side],
                lambda c: table[k, c[1] + 1, c[2] + 1, rows, :],
                keep(hold[x + side]),
                [c for c in DIRS if c[0] == -side],
                toward,
            )
    up[...] = in_up[...]
    down[...] = in_down[...]
    for m, x in enumerate((0, 1, nx - 2, nx - 1)):

        def fetch(a, b, q, h):
            rows = slice(8 * h, 8 * h + 8)
            if x - a in hold:
                return ends[a + 1, b + 1, q, hold[x - a], rows, :]
            return sums[a + 1, b + 1, q, x - a, rows, :]

        def put(n, h, tile):
            part[2 * n + h, ROWS * m : ROWS * m + ROWS, :] = tile

        def put_up(n, value):
            up[n, x : x + 1, :] = value

        def put_down(n, value):
            down[n, x : x + 1, :] = value

        gather_layer(fetch, row, put, put_up, put_down)
    for edge in (up, down):
        for n in range(3):
            for x in range(0, nx, ROWS):
                rows = slice(x, x + ROWS)
                edge[n, rows, :] = block_rows(edge[n, rows, :], reflect, turn)
    odd = lax.rem(lax.axis_index("by"), 2)
    store_by_parity(odd, pay.at[pl.ds(0, 3)], pay.at[pl.ds(3, 3)], up, down)
    store_by_parity(odd, None, away, up, down)


def turn_kernel(part, out):
    reflect, turn = turns()
    for n in range(part.shape[0]):
        for m in range(4):
            rows = slice(ROWS * m, ROWS * m + ROWS)
            out[n, rows, :] = block_rows(part[n, rows, :], reflect, turn)


def add_crossed(made, crossed, top):
    nx = crossed.shape[1]
    width = LANES // ROWS
    spot = top * (ROWS - 1)
    sign = jnp.where(top == 1, -1.0, 1.0)
    mask = lane_block(width) == spot
    for x in range(nx):
        rows = slice(ROWS * x, ROWS * x + ROWS)
        first = x // ROWS * ROWS
        shift = lax.rem(width * (spot - x % ROWS) + LANES, LANES)
        total, cross, along = (
            jnp.where(mask, pltpu.roll(crossed[n, first : first + ROWS, :], shift, 1), 0.0)
            for n in range(3)
        )
        for n, more in enumerate((total, cross, sign * total, along)):
            made[2 * n + top, rows, :] += more


def pack_block(made, pay, start, which):
    for n in range(8):
        pay[start + n, :, :] = made[n, pl.ds(which, pay.shape[1], stride=ROWS), :]


def number(tile):
    return jnp.maximum(jnp.max(tile), 0)


def pack_kernel(moves, inner, outer, got, made, block, pay_w):
    iy = lax.axis_index("by")
    odd = lax.rem(iy, 2)
    nx = got.shape[1]
    low, high = ROWS * 2, ROWS * (nx - 2)
    made[:, 0:low, :] = outer[:, 0:low, :]
    made[:, low:high, :] = inner[:, low:high, :]
    made[:, high:, :] = outer[:, low:, :]
    add_crossed(made, got, 1 - odd)
    pack_block(made, block, 0, number(moves[1 - odd, :, :]))
    end = jnp.logical_or(iy == 0, iy == lax.axis_size("by") - 1)

    @pl.when(end)
    def _():
        pay_w[0:8, :, :] = block[...]

    @pl.when(jnp.logical_not(end))
    def _():
        pay_w[0:3, :, :] = got[3:6, :, :]


def join_kernel(first, second, out):
    out[0 : first.shape[0], :, :] = first[...]
    out[first.shape[0] :, :, :] = second[...]


def moments_kernel(moves, part, got_b, got_w, rho_out, vel_out, pay_a, made):
    odd = lax.rem(lax.axis_index("by"), 2)
    nx = got_b.shape[1]
    made[...] = part[...]
    add_crossed(made, got_b, odd)
    for x in range(nx):
        rows = slice(ROWS * x, ROWS * x + ROWS)
        for h in (0, 1):
            rho = made[h, rows, :]
            inv = 1.0 / rho
            lanes = slice((2 * x + h) * LANES, (2 * x + h + 1) * LANES)
            rho_out[:, lanes] = rho
            for n in range(1, 4):
                tile = made[2 * n + h, rows, :] * inv
                made[2 * n + h, rows, :] = tile
                vel_out[n - 1, :, lanes] = tile
    pack_block(made, pay_a, 0, number(moves[odd, :, :]))
    pay_a[8:11, :, :] = got_w[0:3, :, :]


def place_kernel(moves, rho, vel, away, got_a, got_b, got_w, rho_out, vel_out, block, crossed, made, sems):
    iy = lax.axis_index("by")
    odd = lax.rem(iy, 2)
    end = jnp.logical_or(iy == 0, iy == lax.axis_size("by") - 1)

    @pl.when(end)
    def _():
        block[...] = got_w[0:8, :, :]
        crossed[...] = got_a[8:11, :, :]

    @pl.when(jnp.logical_not(end))
    def _():
        block[...] = got_b[3:11, :, :]
        crossed[...] = away[...]

    row = sublane()
    width = LANES // ROWS
    top = 1 - odd
    sign = jnp.where(top == 1, -1.0, 1.0)
    mask = lane_block(width) == top * (ROWS - 1)
    spread = row * width + (lane_block(1) & (width - 1))
    theirs = number(moves[3 - odd, :, :])
    for first in range(0, block.shape[1], ROWS):
        rows = slice(first, first + ROWS)
        extra = []
        for n in range(3):
            line = jnp.broadcast_to(crossed[n, pl.ds(first + theirs, 1), :], (ROWS, LANES))
            extra.append(jnp.where(mask, jnp.take_along_axis(line, spread, axis=1), 0.0))
        total, cross, along = extra
        for n, more in enumerate((total, cross, sign * total, along)):
            block[2 * n + top, rows, :] += more
        for h in (0, 1):
            inv = 1.0 / block[h, rows, :]
            for n in range(1, 4):
                block[2 * n + h, rows, :] *= inv
    near = row == moves[odd, :, :]
    far = row == moves[1 - odd, :, :]
    copies = []
    for n in range(4):
        for x in range(block.shape[1]):
            for h in (0, 1):
                lanes = slice((2 * x + h) * LANES, (2 * x + h + 1) * LANES)
                k = 2 * n + h
                tile = rho[:, lanes] if n == 0 else vel[n - 1, :, lanes]
                tile = jnp.where(near, got_a[k, x : x + 1, :], tile)
                made[n, :, lanes] = jnp.where(far, block[k, x : x + 1, :], tile)
        target = rho_out if n == 0 else vel_out.at[n - 1]
        copies.append(pltpu.make_async_copy(made.at[n], target, sems.at[n]))
        copies[n].start()
    for copy in copies:
        copy.wait()


def swap(value, axis, odd):
    count_x, count_y = lax.axis_size("bx"), lax.axis_size("by")
    pairs = []
    if axis == "by":
        for x in range(count_x):
            for y in range(odd, count_y, 2):
                pairs.append((x * count_y + y, x * count_y + (y + 1) % count_y))
    else:
        for y in range(count_y):
            for x in range(odd, count_x, 2):
                pairs.append((x * count_y + y, (x + 1) % count_x * count_y + y))
    pairs = pairs + [(b, a) for a, b in pairs]
    return lax.ppermute(value, ("bx", "by"), pairs)


def swap_ends(value):
    count_x, count_y = lax.axis_size("bx"), lax.axis_size("by")
    pairs = []
    for x in range(count_x):
        here, after = x * count_y, (x + 1) * count_y
        if x + 1 < count_x:
            pairs += [(after - 1, after), (after, after - 1)]
            pairs += [(here + 1, after + 1), (after + count_y - 2, after - 2)]
        pairs += [(here + y, here + (y ^ 1)) for y in range(2, count_y - 2)]
    pairs += [(0, 1), (after - 1, after - 2)]
    pairs += [(after - count_y + 1, after - 1), (count_y - 2, 0)]
    return lax.ppermute(value, ("bx", "by"), pairs)


def call(kernel, outs, specs, scratch, name, work, limit, kept):
    space = {"v": pltpu.VMEM, "s": pltpu.SMEM, "h": pltpu.HBM, "a": pl.ANY}
    return pl.pallas_call(
        kernel,
        out_shape=outs,
        in_specs=[pl.BlockSpec(memory_space=space[k]) for k in specs],
        out_specs=[pl.BlockSpec(memory_space=pltpu.VMEM if kept else pl.ANY)] * len(outs),
        scratch_shapes=scratch,
        compiler_params=pltpu.CompilerParams(vmem_limit_bytes=limit),
        cost_estimate=pl.CostEstimate(
            flops=work * 2000000, bytes_accessed=work * 1000000, transcendentals=0
        ),
        name=name,
    )


def on_device(populations, block_level, new_slot):
    shape = (lax.axis_size("bx"), lax.axis_size("by"))
    blocks = new_slot.shape[0]
    _, nx, ny, nz = populations.shape
    yface, xface, yedge = (9, nx, nz), (24, ny, nz), (3, nx, nz)
    tile = (ROWS, nz)

    def real(*dims):
        return jax.ShapeDtypeStruct(dims, jnp.float32)

    def whole(*dims):
        return jax.ShapeDtypeStruct(dims, jnp.int32)

    def room(*shapes):
        return [pltpu.VMEM(dims, jnp.float32) for dims in shapes]

    def run(kernel, *args, outs, specs, scratch=(), work=1, limit=VMEM_BYTES, kept=True):
        def body(*refs):
            kernel(*refs)

        return call(body, outs, specs, scratch, kernel.func.__name__[:-7], work, limit, kept)(*args)

    high, low = run(
        functools.partial(fetch_kernel), populations,
        outs=[real(27, nx, nz)] * 2, specs="h", scratch=[pltpu.SemaphoreType.DMA((2,))],
        limit=FACE_BYTES,
    )
    marks, pay_a, pay_b = run(
        functools.partial(face_kernel, shape, blocks),
        block_level.reshape(block_level.shape[0] // nz, nz), high, low,
        outs=[whole(3, 3, *tile), real(*yface), real(*yface)],
        specs="vvv", scratch=room(yface, yface),
    )
    ya, yb = swap(pay_a, "by", 0), swap(pay_b, "by", 1)
    table, g, calm = run(
        functools.partial(first_kernel), marks, populations,
        outs=[real(5, 3, 3, ny, nz), real(*populations.shape), real(2, 9, ny, nz)],
        specs="vv", work=3,
    )
    pay_a, pay_b = run(
        functools.partial(side_kernel), marks, populations, g, calm, ya, yb,
        outs=[real(25, ny, nz), real(*xface)], specs="vvvvvv", scratch=room(yface, yface, xface, xface),
    )
    xa, xb = swap(pay_a, "bx", 0), swap(pay_b, "bx", 1)
    sums, inner, up, down, moves = run(
        functools.partial(inner_kernel, blocks),
        new_slot, marks, populations, g, table, ya, yb, pay_a,
        outs=[
            real(3, 3, 2, nx, ny, nz), real(8, nx * ROWS, nz), real(*yedge), real(*yedge),
            whole(4, *tile),
        ],
        specs="svvvvvva",
        scratch=room(yface, yface, (27, ny, nz)),
        work=10,
    )
    part, pay_a, away = run(
        functools.partial(outer_kernel),
        marks, populations, g, table, ya, yb, xa, xb, sums, up, down,
        outs=[real(8, 4 * ROWS, nz), real(6, nx, nz), real(*yedge)],
        specs="vvvvvvvvvvv",
        scratch=room(
            yface, yface, xface, xface, (27, ny, nz), (3, 3, 2, 4, ny, nz), yedge, yedge
        ),
    )
    got_a = swap(pay_a, "by", 0)
    (outer,) = run(
        functools.partial(turn_kernel), part, outs=[real(8, 4 * ROWS, nz)], specs="v"
    )
    part, block, pay_w = run(
        functools.partial(pack_kernel), moves, inner, outer, got_a,
        outs=[real(8, nx * ROWS, nz), real(8, nx, nz), real(12, nx, nz)], specs="vvvv",
    )
    got_w = swap_ends(pay_w)
    (pay_b,) = run(
        functools.partial(join_kernel), away, block, outs=[real(11, nx, nz)], specs="vv"
    )
    got_b = swap(pay_b, "by", 1)
    cells = nx * ny * nz // blocks
    results = [real(blocks, cells), real(3, blocks, cells)]
    rho, vel, pay_a = run(
        functools.partial(moments_kernel), moves, part, got_b, got_w,
        outs=results + [real(11, nx, nz)],
        specs="vvvv",
        scratch=room((8, nx * ROWS, nz)),
    )
    got_a = swap(pay_a, "by", 0)
    return tuple(
        run(
            functools.partial(place_kernel), moves, rho, vel, away, got_a, got_b, got_w,
            outs=results, specs="vvvvvvv", kept=False,
            scratch=room((8, nx, nz), yedge, (4, blocks, cells)) + [pltpu.SemaphoreType.DMA((4,))],
        )
    )


def solution(mesh):
    in_specs = (P(None, "bx", "by", None), P(), P(("bx", "by")))
    out_specs = (P(("bx", "by"), None), P(None, ("bx", "by"), None))
    return jax.shard_map(
        on_device, mesh=mesh, in_specs=in_specs, out_specs=out_specs, check_vma=False
    )
```

```python
import functools
import math

import jax
import jax.numpy as jnp
import numpy as np
from jax import lax
from jax.experimental import pallas as pl
from jax.experimental.pallas import tpu as pltpu
from jax.sharding import PartitionSpec as P

tau_coarse = 0.56
tau_fine = 0.62
scale_to_fine = tau_fine / (2.0 * tau_coarse)
scale_to_coarse = 2.0 * tau_coarse / tau_fine
smagorinsky = 18.0 * math.sqrt(2.0) * 0.17 * 0.17
weights = (8.0 / 27, 2.0 / 27, 1.0 / 54, 1.0 / 216)
ROWS = 8
LANES = 128
VMEM_BYTES = 16 * 1024 * 1024
FACE_BYTES = 53 * 1024 * 1024


def comp(a, b, e):
    return 9 * (a + 1) + 3 * (b + 1) + (e + 1)


def face(b, e):
    return 3 * (b + 1) + (e + 1)


DIRS = [(a, b, e) for a in (-1, 0, 1) for b in (-1, 0, 1) for e in (-1, 0, 1)]
HALF = [c for c in DIRS if c > (0, 0, 0)]


def lane_block(edge):
    return lax.broadcasted_iota(jnp.int32, (ROWS, LANES), 1) // edge


def sublane():
    return lax.broadcasted_iota(jnp.int32, (ROWS, LANES), 0)


def column_level(levels, shape, blocks, dx, dy):
    count_x, count_y = shape
    ix = lax.rem(lax.axis_index("bx") + (dx + count_x), count_x)
    iy = lax.rem(lax.axis_index("by") + (dy + count_y), count_y)
    base = (ix * count_y + iy) * blocks
    line = jnp.broadcast_to(levels[pl.ds(base // LANES, 1), :], (ROWS, LANES))
    line = pltpu.roll(line, lax.rem(LANES - lax.rem(base, LANES), LANES), 1)
    return jnp.take_along_axis(line, lane_block(LANES // blocks), axis=1)


def lane_roll(tile, by):
    return tile if by == 0 else pltpu.roll(tile, by % LANES, 1)


def group_sums(get):
    total, diff, quad = {}, {}, {}
    for b in (-1, 0, 1):
        low, mid, high = (get(b, e) for e in (-1, 0, 1))
        quad[b] = low + high
        total[b] = quad[b] + mid
        diff[b] = high - low
    both = total[-1] + total[1]
    return (
        both + total[0],
        total[1] - total[-1],
        both,
        diff[-1] + diff[0] + diff[1],
        diff[1] - diff[-1],
        quad[-1] + quad[0] + quad[1],
    )


def add_sums(first, second):
    return tuple(p + q for p, q in zip(first, second))


def collide(groups, get, fine, everywhere, factor, put, dirs=None):
    low, mid, high = (groups[a] for a in (-1, 0, 1))
    ends = add_sums(low, high)
    rho, jy, pyy, jz, pyz, pzz = add_sums(ends, mid)
    pxx = ends[0]
    jx, pxy, pxz = high[0] - low[0], high[1] - low[1], high[3] - low[3]
    inv = 1.0 / rho
    ux, uy, uz = jx * inv, jy * inv, jz * inv
    third = rho * (1.0 / 3.0)
    pxx = pxx - third - jx * ux
    pyy = pyy - third - jy * uy
    pzz = pzz - third - jz * uz
    pxy = pxy - jx * uy
    pxz = pxz - jx * uz
    pyz = pyz - jy * uz
    norm = jnp.sqrt(
        pxx * pxx + pyy * pyy + pzz * pzz + 2.0 * (pxy * pxy + pxz * pxz + pyz * pyz)
    )
    base_time = jnp.where(fine, tau_fine, tau_coarse)
    tau = 0.5 * (base_time + jnp.sqrt(base_time * base_time + smagorinsky * norm * inv))
    keep = 1.0 - 1.0 / tau
    if not everywhere:
        keep = jnp.where(fine, keep, 1.0)
    base = 1.0 - 1.5 * (ux * ux + uy * uy + uz * uz)
    scaled = [rho * w for w in weights]
    rest = [s * base for s in scaled]
    vx, vy, vz = 3.0 * ux, 3.0 * uy, 3.0 * uz
    vel = {(0, 0, 1): vz, (0, 1, 0): vy, (1, 0, 0): vx}
    vel[0, 1, 1], vel[0, 1, -1] = vy + vz, vy - vz
    vel[1, 0, 1], vel[1, 0, -1] = vx + vz, vx - vz
    vel[1, 1, 0], vel[1, -1, 0] = vx + vy, vx - vy
    for b in (-1, 1):
        for e in (-1, 1):
            vel[1, b, e] = vel[1, b, 0] + (vz if e > 0 else -vz)

    def emit(c, balance):
        if dirs is not None and c not in dirs:
            return
        gain = keep if c == (0, 0, 0) else keep * factor(c)
        put(c, balance + gain * (get(c) - balance))

    emit((0, 0, 0), rest[0])
    for c in HALF:
        n = sum(abs(k) for k in c)
        odd = scaled[n] * vel[c]
        even = rest[n] + 0.5 * odd * vel[c]
        emit(c, even + odd)
        emit(tuple(-k for k in c), even - odd)


def sums_of(get):
    return {a: group_sums(lambda b, e, a=a: get((a, b, e))) for a in (-1, 0, 1)}


def level_factor(here, there_rows, e):
    scale = jnp.where(here == 1, scale_to_coarse, scale_to_fine)
    return jnp.where(lane_roll(there_rows, -e) != here, scale, 1.0)


def fill_factors(marks, table):
    row = sublane()
    for k, (own, dx) in enumerate(((0, -1), (0, 0), (0, 1), (-1, 0), (1, 0))):
        here = marks[own + 1, 1, :, :]
        near = [marks[dx + 1, b, :, :] for b in range(3)]
        for e in (-1, 0, 1):
            plain = level_factor(here, near[1], e)
            for b in (-1, 0, 1):
                low, high = plain, plain
                if b == -1:
                    low = jnp.where(row == 0, level_factor(here, near[0], e), plain)
                if b == 1:
                    high = jnp.where(row == ROWS - 1, level_factor(here, near[2], e), plain)
                table[k, b + 1, e + 1, 0:8, :] = low
                table[k, b + 1, e + 1, 8:16, :] = high


def x_side(a, x, last):
    if a == 0:
        return 1
    return jnp.where(x == (0 if a < 0 else last), 1 + a, 1)


def store_by_parity(odd, first, second, up, down):
    @pl.when(odd == 0)
    def _():
        if first is not None:
            first[...] = up[...]
        second[...] = down[...]

    @pl.when(odd == 1)
    def _():
        if first is not None:
            first[...] = down[...]
        second[...] = up[...]


def fetch_kernel(f, high, low, sems):
    ny = f.shape[2]
    copies = [
        pltpu.make_async_copy(f.at[:, :, ny - 1, :], high, sems.at[0]),
        pltpu.make_async_copy(f.at[:, :, 0, :], low, sems.at[1]),
    ]
    for copy in copies:
        copy.start()
    for copy in copies:
        copy.wait()


def face_kernel(shape, blocks, levels, high, low, marks, pay_a, pay_b, up, down):
    nx = high.shape[1]
    for dx in (-1, 0, 1):
        for dy in (-1, 0, 1):
            marks[dx + 1, dy + 1, :, :] = column_level(levels, shape, blocks, dx, dy)
    here = marks[1, 1, :, :]
    row = sublane()
    for b, rows, pay in ((1, high, up), (-1, low, down)):
        near = [marks[dx, b + 1, :, :] for dx in range(3)]
        plain = {e: level_factor(here, near[1], e) for e in (-1, 0, 1)}
        for x in range(0, nx, ROWS):

            def get(c):
                return rows[comp(*c), x : x + ROWS, :]

            def factor(c):
                if c[0] == -1 and x == 0:
                    return jnp.where(row == 0, level_factor(here, near[0], c[2]), plain[c[2]])
                if c[0] == 1 and x + ROWS == nx:
                    return jnp.where(
                        row == ROWS - 1, level_factor(here, near[2], c[2]), plain[c[2]]
                    )
                return plain[c[2]]

            def put(c, value):
                pay[face(c[0], c[2]), x : x + ROWS, :] = value

            collide(
                sums_of(get), get, here == 1, False, factor, put, [c for c in DIRS if c[1] == b]
            )
    store_by_parity(lax.rem(lax.axis_index("by"), 2), pay_a, pay_b, up, down)


def first_collide(f, table, fine, x, near, put):
    for h in (0, 1):
        rows = slice(8 * h, 8 * h + 8)

        def get(c):
            return f[comp(*c), x, rows, :]

        def factor(c):
            return table[near(c[0]), c[1] + 1, c[2] + 1, rows, :]

        collide(sums_of(get), get, fine, False, factor, lambda c, value: put(c, rows, value))


def first_kernel(marks, f, table, out, calm):
    fill_factors(marks, table)
    fine = marks[1, 1, :, :] == 1
    nx = f.shape[1]
    for n, (x, a) in enumerate(((0, -1), (nx - 1, 1))):
        for h in (0, 1):
            rows = slice(8 * h, 8 * h + 8)

            def get(c):
                return f[comp(*c), x, rows, :]

            def put(c, value):
                calm[n, face(c[1], c[2]), rows, :] = value

            collide(
                sums_of(get), get, fine, True,
                lambda c: table[1 + c[0], c[1] + 1, c[2] + 1, rows, :],
                put, [c for c in DIRS if c[0] == a],
            )

    def layer(x, carry):
        def near(a):
            return 1 if a == 0 else jnp.where(x == (0 if a < 0 else nx - 1), 1 + a, 1)

        def put(c, rows, value):
            out[comp(*c), x, rows, :] = value

        first_collide(f, table, fine, x, near, put)
        return carry

    lax.fori_loop(0, nx, layer, 0)


def shifted_read(g, above, below, row, c, x, h):
    a, b, e = c
    i = comp(a, b, e)
    if b == 0:
        tile = g[i, x, 8 * h : 8 * h + 8, :]
    elif b == 1:
        if h == 1:
            tile = g[i, x, 7:15, :]
        else:
            tile = pltpu.roll(g[i, x, 0:8, :], 1, 0)
            tile = jnp.where(row == 0, below[face(a, e), pl.ds(x, 1), :], tile)
    else:
        if h == 0:
            tile = g[i, x, 1:9, :]
        else:
            tile = pltpu.roll(g[i, x, 8:16, :], 7, 0)
            tile = jnp.where(row == 7, above[face(a, e), pl.ds(x, 1), :], tile)
    return lane_roll(tile, e)


def load_by_parity(odd, first, second, above, below):
    @pl.when(odd == 0)
    def _():
        above[...] = first[...]
        below[...] = second[...]

    @pl.when(odd == 1)
    def _():
        above[...] = second[...]
        below[...] = first[...]


def side_kernel(marks, f, g, calm, got_a, got_b, pay_a, pay_b, above, below, up, down):
    load_by_parity(lax.rem(lax.axis_index("by"), 2), got_a, got_b, above, below)
    fine = marks[1, 1, :, :] == 1
    row = sublane()
    nx = f.shape[1]
    for n, (ad, x, pay) in enumerate(((-1, 0, down), (1, nx - 1, up))):
        for h in (0, 1):
            rows = slice(8 * h, 8 * h + 8)

            def flat(b, e):
                return shifted_read(g, above, below, row, (0, b, e), x, h)

            for b in (-1, 0, 1):
                for e in (-1, 0, 1):
                    c, j = (ad, b, e), face(b, e)
                    pay[j, rows, :] = shifted_read(g, above, below, row, c, x, h)
                    moved = shifted_read(g, above, below, row, c, x - ad, h)
                    pay[9 + j, rows, :] = jnp.where(fine, moved, calm[n, j, rows, :])
            for m, part in enumerate(group_sums(flat)):
                pay[18 + m, rows, :] = part
    store_by_parity(lax.rem(lax.axis_index("bx"), 2), pay_a.at[pl.ds(0, 24)], pay_b, up, down)


def second_collide(groups, get, fine, factor, put, dirs, known=None):
    made = {}

    def keep(c, value):
        made[c] = value if known is None else jnp.where(fine, value, known(c))

    collide(groups, get, fine, True, factor, keep, dirs)
    for a in (-1, 0, 1):
        if dirs is not None and (a, 0, 0) not in dirs:
            continue
        for b in (-1, 0, 1):
            plus = lane_roll(made[a, b, 1], 1)
            minus = lane_roll(made[a, b, -1], -1)
            put(a, b, made[a, b, 0] + (plus + minus), plus - minus)


def gather_layer(sums, row, put, up, down):
    total, cross, along = {}, {}, {}
    for b in (-1, 0, 1):
        for h in (0, 1):
            low, mid, high = (sums(a, b, 0, h) for a in (1, 0, -1))
            total[b, h] = low + mid + high
            cross[b, h] = low - high
            along[b, h] = sums(1, b, 1, h) + sums(0, b, 1, h) + sums(-1, b, 1, h)
    for n, part in enumerate((total, cross, along)):
        up(n, part[1, 1][7:8])
        down(n, part[-1, 0][0:1])
        rise = [pltpu.roll(part[1, h], 1, 0) for h in (0, 1)]
        fall = [pltpu.roll(part[-1, h], 7, 0) for h in (0, 1)]
        rise = [jnp.where(row == 0, 0.0, rise[0]), jnp.where(row == 0, rise[0], rise[1])]
        fall = [jnp.where(row == 7, fall[1], fall[0]), jnp.where(row == 7, 0.0, fall[1])]
        for h in (0, 1):
            put((0, 1, 3)[n], h, part[0, h] + rise[h] + fall[h])
            if n == 0:
                put(2, h, rise[h] - fall[h])


def turns():
    row = sublane()
    reflect = (lane_block(LANES // ROWS) - row) & (ROWS - 1)
    turn = (lane_block(1) + row * (LANES // ROWS)) & (LANES - 1)
    return reflect, turn


def block_rows(tile, reflect, turn):
    tile = pltpu.roll(tile, 0, 1, stride=LANES // ROWS, stride_axis=0)
    tile = jnp.take_along_axis(tile, reflect, axis=0)
    return jnp.take_along_axis(tile, turn, axis=1)


def leaving(slots, blocks, step):
    here = lax.axis_index("bx") * lax.axis_size("by") + lax.axis_index("by")
    which, theirs = jnp.int32(-1), jnp.int32(0)
    for k in range(blocks):
        goes = slots[k] // blocks == here + step
        which = jnp.where(goes, k, which)
        theirs = jnp.where(goes, lax.rem(slots[k], blocks), theirs)
    return which, theirs


def inner_kernel(
    blocks, slots, marks, f, g, table, ya, yb, tie, sums, made, up, down, moves,
    above, below, state,
):
    load_by_parity(lax.rem(lax.axis_index("by"), 2), ya, yb, above, below)
    for n, step in enumerate((1, -1)):
        which, theirs = leaving(slots, blocks, step)
        moves[n, :, :] = jnp.full((ROWS, LANES), which, jnp.int32)
        moves[2 + n, :, :] = jnp.full((ROWS, LANES), theirs, jnp.int32)
    fine = marks[1, 1, :, :] == 1
    row = sublane()
    reflect, turn = turns()
    nx = f.shape[1]

    def second(x, carry):
        for h in (0, 1):
            rows = slice(8 * h, 8 * h + 8)

            def moved(c):
                tile = shifted_read(g, above, below, row, c, x - c[0], h)
                tile = jnp.where(fine, tile, f[comp(*c), x, rows, :])
                state[comp(*c), rows, :] = tile
                return tile

            def put(a, b, total, along):
                sums[a + 1, b + 1, 0, x, rows, :] = total
                sums[a + 1, b + 1, 1, x, rows, :] = along

            second_collide(
                sums_of(moved),
                lambda c: state[comp(*c), rows, :],
                fine,
                lambda c: table[1, c[1] + 1, c[2] + 1, rows, :],
                put,
                None,
            )
        return carry

    lax.fori_loop(1, nx - 1, second, 0)

    def gather(x, carry):
        def put(n, h, tile):
            made[2 * n + h, pl.ds(x * ROWS, ROWS), :] = block_rows(tile, reflect, turn)

        def put_up(n, value):
            up[n, pl.ds(x, 1), :] = value

        def put_down(n, value):
            down[n, pl.ds(x, 1), :] = value

        gather_layer(
            lambda a, b, q, h: sums[a + 1, b + 1, q, x - a, 8 * h : 8 * h + 8, :],
            row, put, put_up, put_down,
        )
        return carry

    lax.fori_loop(2, nx - 2, gather, 0)


def outer_kernel(
    marks, f, g, table, ya, yb, xa, xb, sums, in_up, in_down,
    part, pay, away, above, below, right, left, state, ends, up, down,
):
    load_by_parity(lax.rem(lax.axis_index("by"), 2), ya, yb, above, below)
    load_by_parity(lax.rem(lax.axis_index("bx"), 2), xa.at[pl.ds(0, 24)], xb, right, left)
    fine = {dx: marks[dx + 1, 1, :, :] == 1 for dx in (-1, 0, 1)}
    row = sublane()
    reflect, turn = turns()
    nx = f.shape[1]
    hold = {-1: 0, 0: 1, nx - 1: 2, nx: 3}
    for side, x, k, got in ((-1, 0, 3, left), (1, nx - 1, 4, right)):
        for h in (0, 1):
            rows = slice(8 * h, 8 * h + 8)

            def keep(slot):
                def put(a, b, total, along):
                    ends[a + 1, b + 1, 0, slot, rows, :] = total
                    ends[a + 1, b + 1, 1, slot, rows, :] = along

                return put

            def read(c, x):
                return shifted_read(g, above, below, row, c, x, h)

            def moved(c):
                a, b, e = c
                if a == -side:
                    tile = got[face(b, e), rows, :]
                else:
                    tile = read(c, x - a)
                tile = jnp.where(fine[0], tile, f[comp(*c), x, rows, :])
                state[comp(*c), rows, :] = tile
                return tile

            second_collide(
                sums_of(moved),
                lambda c: state[comp(*c), rows, :],
                fine[0],
                lambda c: table[1, c[1] + 1, c[2] + 1, rows, :],
                keep(hold[x]),
                [c for c in DIRS if c[0] != side],
            )

            def toward(c):
                return got[9 + face(c[1], c[2]), rows, :]

            second_collide(
                {
                    side: group_sums(lambda b, e: read((side, b, e), x)),
                    0: tuple(got[18 + n, rows, :] for n in range(6)),
                    -side: group_sums(lambda b, e: toward((-side, b, e))),
                },
                toward,
                fine[side],
                lambda c: table[k, c[1] + 1, c[2] + 1, rows, :],
                keep(hold[x + side]),
                [c for c in DIRS if c[0] == -side],
                toward,
            )
    up[...] = in_up[...]
    down[...] = in_down[...]
    for m, x in enumerate((0, 1, nx - 2, nx - 1)):

        def fetch(a, b, q, h):
            rows = slice(8 * h, 8 * h + 8)
            if x - a in hold:
                return ends[a + 1, b + 1, q, hold[x - a], rows, :]
            return sums[a + 1, b + 1, q, x - a, rows, :]

        def put(n, h, tile):
            part[2 * n + h, ROWS * m : ROWS * m + ROWS, :] = tile

        def put_up(n, value):
            up[n, x : x + 1, :] = value

        def put_down(n, value):
            down[n, x : x + 1, :] = value

        gather_layer(fetch, row, put, put_up, put_down)
    for edge in (up, down):
        for n in range(3):
            for x in range(0, nx, ROWS):
                rows = slice(x, x + ROWS)
                edge[n, rows, :] = block_rows(edge[n, rows, :], reflect, turn)
    odd = lax.rem(lax.axis_index("by"), 2)
    store_by_parity(odd, pay.at[pl.ds(0, 3)], pay.at[pl.ds(3, 3)], up, down)
    store_by_parity(odd, None, away, up, down)


def turn_kernel(part, out):
    reflect, turn = turns()
    for n in range(part.shape[0]):
        for m in range(4):
            rows = slice(ROWS * m, ROWS * m + ROWS)
            out[n, rows, :] = block_rows(part[n, rows, :], reflect, turn)


def add_crossed(made, crossed, top):
    nx = crossed.shape[1]
    width = LANES // ROWS
    spot = top * (ROWS - 1)
    sign = jnp.where(top == 1, -1.0, 1.0)
    mask = lane_block(width) == spot
    for x in range(nx):
        rows = slice(ROWS * x, ROWS * x + ROWS)
        first = x // ROWS * ROWS
        shift = lax.rem(width * (spot - x % ROWS) + LANES, LANES)
        total, cross, along = (
            jnp.where(mask, pltpu.roll(crossed[n, first : first + ROWS, :], shift, 1), 0.0)
            for n in range(3)
        )
        for n, more in enumerate((total, cross, sign * total, along)):
            made[2 * n + top, rows, :] += more


def pack_block(made, pay, start, which):
    for n in range(8):
        pay[start + n, :, :] = made[n, pl.ds(which, pay.shape[1], stride=ROWS), :]


def number(tile):
    return jnp.maximum(jnp.max(tile), 0)


def pack_kernel(moves, inner, outer, got, made, block, pay_w):
    iy = lax.axis_index("by")
    odd = lax.rem(iy, 2)
    which = number(moves[1 - odd, :, :])
    nx = got.shape[1]
    low, high = ROWS * 2, ROWS * (nx - 2)
    made[:, 0:low, :] = outer[:, 0:low, :]
    made[:, low:high, :] = inner[:, low:high, :]
    made[:, high:, :] = outer[:, low:, :]
    add_crossed(made, got, 1 - odd)
    pack_block(made, block, 0, which)
    end = jnp.logical_or(iy == 0, iy == lax.axis_size("by") - 1)

    @pl.when(end)
    def _():
        pay_w[0:8, :, :] = block[...]

    @pl.when(jnp.logical_not(end))
    def _():
        pay_w[0:3, :, :] = got[3:6, :, :]


def join_kernel(first, second, out):
    out[0 : first.shape[0], :, :] = first[...]
    out[first.shape[0] :, :, :] = second[...]


def moments_kernel(moves, part, got_b, got_w, rho_out, vel_out, pay_a, made):
    odd = lax.rem(lax.axis_index("by"), 2)
    nx = got_b.shape[1]
    which = number(moves[odd, :, :])
    made[...] = part[...]
    add_crossed(made, got_b, odd)
    for x in range(nx):
        rows = slice(ROWS * x, ROWS * x + ROWS)
        for h in (0, 1):
            rho = made[h, rows, :]
            inv = 1.0 / rho
            lanes = slice((2 * x + h) * LANES, (2 * x + h + 1) * LANES)
            rho_out[:, lanes] = rho
            for n in range(1, 4):
                tile = made[2 * n + h, rows, :] * inv
                made[2 * n + h, rows, :] = tile
                vel_out[n - 1, :, lanes] = tile
    pack_block(made, pay_a, 0, which)
    pay_a[8:11, :, :] = got_w[0:3, :, :]


def place_kernel(moves, rho, vel, away, got_a, got_b, got_w, rho_out, vel_out, block, crossed, made, sems):
    iy = lax.axis_index("by")
    odd = lax.rem(iy, 2)
    end = jnp.logical_or(iy == 0, iy == lax.axis_size("by") - 1)

    @pl.when(end)
    def _():
        block[...] = got_w[0:8, :, :]
        crossed[...] = got_a[8:11, :, :]

    @pl.when(jnp.logical_not(end))
    def _():
        block[...] = got_b[3:11, :, :]
        crossed[...] = away[...]

    row = sublane()
    width = LANES // ROWS
    top = 1 - odd
    sign = jnp.where(top == 1, -1.0, 1.0)
    mask = lane_block(width) == top * (ROWS - 1)
    spread = row * width + (lane_block(1) & (width - 1))
    theirs = jnp.maximum(moves[3 - odd, :, :], 0)
    for first in range(0, block.shape[1], ROWS):
        rows = slice(first, first + ROWS)
        extra = []
        for n in range(3):
            line = jnp.take_along_axis(crossed[n, rows, :], theirs, axis=0)
            extra.append(jnp.where(mask, jnp.take_along_axis(line, spread, axis=1), 0.0))
        total, cross, along = extra
        for n, more in enumerate((total, cross, sign * total, along)):
            block[2 * n + top, rows, :] += more
        for h in (0, 1):
            inv = 1.0 / block[h, rows, :]
            for n in range(1, 4):
                block[2 * n + h, rows, :] *= inv
    near = row == moves[odd, :, :]
    far = row == moves[1 - odd, :, :]
    copies = []
    for n in range(4):
        for x in range(block.shape[1]):
            for h in (0, 1):
                lanes = slice((2 * x + h) * LANES, (2 * x + h + 1) * LANES)
                k = 2 * n + h
                tile = rho[:, lanes] if n == 0 else vel[n - 1, :, lanes]
                tile = jnp.where(near, got_a[k, x : x + 1, :], tile)
                made[n, :, lanes] = jnp.where(far, block[k, x : x + 1, :], tile)
        target = rho_out if n == 0 else vel_out.at[n - 1]
        copies.append(pltpu.make_async_copy(made.at[n], target, sems.at[n]))
        copies[n].start()
    for copy in copies:
        copy.wait()


def swap(value, axis, odd):
    count_x, count_y = lax.axis_size("bx"), lax.axis_size("by")
    pairs = []
    if axis == "by":
        for x in range(count_x):
            for y in range(odd, count_y, 2):
                pairs.append((x * count_y + y, x * count_y + (y + 1) % count_y))
    else:
        for y in range(count_y):
            for x in range(odd, count_x, 2):
                pairs.append((x * count_y + y, (x + 1) % count_x * count_y + y))
    pairs = pairs + [(b, a) for a, b in pairs]
    return lax.ppermute(value, ("bx", "by"), pairs)


def swap_ends(value):
    count_x, count_y = lax.axis_size("bx"), lax.axis_size("by")
    pairs = []
    for x in range(count_x):
        here, after = x * count_y, (x + 1) * count_y
        if x + 1 < count_x:
            pairs += [(after - 1, after), (after, after - 1)]
            pairs += [(here + 1, after + 1), (after + count_y - 2, after - 2)]
        pairs += [(here + y, here + (y ^ 1)) for y in range(2, count_y - 2)]
    pairs += [(0, 1), (after - 1, after - 2)]
    pairs += [(after - count_y + 1, after - 1), (count_y - 2, 0)]
    return lax.ppermute(value, ("bx", "by"), pairs)


def call(kernel, outs, specs, scratch, name, work, limit, kept):
    space = {"v": pltpu.VMEM, "s": pltpu.SMEM, "h": pltpu.HBM, "a": pl.ANY}
    return pl.pallas_call(
        kernel,
        out_shape=outs,
        in_specs=[pl.BlockSpec(memory_space=space[k]) for k in specs],
        out_specs=[pl.BlockSpec(memory_space=pltpu.VMEM if kept else pl.ANY)] * len(outs),
        scratch_shapes=scratch,
        compiler_params=pltpu.CompilerParams(vmem_limit_bytes=limit),
        cost_estimate=pl.CostEstimate(
            flops=work * 2000000, bytes_accessed=work * 1000000, transcendentals=0
        ),
        name=name,
    )


def on_device(populations, block_level, new_slot):
    shape = (lax.axis_size("bx"), lax.axis_size("by"))
    blocks = new_slot.shape[0]
    _, nx, ny, nz = populations.shape
    yface, xface, yedge = (9, nx, nz), (24, ny, nz), (3, nx, nz)
    tile = (ROWS, nz)

    def real(*dims):
        return jax.ShapeDtypeStruct(dims, jnp.float32)

    def whole(*dims):
        return jax.ShapeDtypeStruct(dims, jnp.int32)

    def room(*shapes):
        return [pltpu.VMEM(dims, jnp.float32) for dims in shapes]

    def run(kernel, *args, outs, specs, scratch=(), work=1, limit=VMEM_BYTES, kept=True):
        def body(*refs):
            kernel(*refs)

        return call(body, outs, specs, scratch, kernel.func.__name__[:-7], work, limit, kept)(*args)

    high, low = run(
        functools.partial(fetch_kernel), populations,
        outs=[real(27, nx, nz)] * 2, specs="h", scratch=[pltpu.SemaphoreType.DMA((2,))],
        limit=FACE_BYTES,
    )
    marks, pay_a, pay_b = run(
        functools.partial(face_kernel, shape, blocks),
        block_level.reshape(block_level.shape[0] // nz, nz), high, low,
        outs=[whole(3, 3, *tile), real(*yface), real(*yface)],
        specs="vvv", scratch=room(yface, yface),
    )
    ya, yb = swap(pay_a, "by", 0), swap(pay_b, "by", 1)
    table, g, calm = run(
        functools.partial(first_kernel), marks, populations,
        outs=[real(5, 3, 3, ny, nz), real(*populations.shape), real(2, 9, ny, nz)],
        specs="vv", work=3,
    )
    pay_a, pay_b = run(
        functools.partial(side_kernel), marks, populations, g, calm, ya, yb,
        outs=[real(25, ny, nz), real(*xface)], specs="vvvvvv", scratch=room(yface, yface, xface, xface),
    )
    xa, xb = swap(pay_a, "bx", 0), swap(pay_b, "bx", 1)
    sums, inner, up, down, moves = run(
        functools.partial(inner_kernel, blocks),
        new_slot, marks, populations, g, table, ya, yb, pay_a,
        outs=[
            real(3, 3, 2, nx, ny, nz), real(8, nx * ROWS, nz), real(*yedge), real(*yedge),
            whole(4, *tile),
        ],
        specs="svvvvvva",
        scratch=room(yface, yface, (27, ny, nz)),
        work=10,
    )
    part, pay_a, away = run(
        functools.partial(outer_kernel),
        marks, populations, g, table, ya, yb, xa, xb, sums, up, down,
        outs=[real(8, 4 * ROWS, nz), real(6, nx, nz), real(*yedge)],
        specs="vvvvvvvvvvv",
        scratch=room(
            yface, yface, xface, xface, (27, ny, nz), (3, 3, 2, 4, ny, nz), yedge, yedge
        ),
    )
    got_a = swap(pay_a, "by", 0)
    (outer,) = run(
        functools.partial(turn_kernel), part, outs=[real(8, 4 * ROWS, nz)], specs="v"
    )
    part, block, pay_w = run(
        functools.partial(pack_kernel), moves, inner, outer, got_a,
        outs=[real(8, nx * ROWS, nz), real(8, nx, nz), real(12, nx, nz)], specs="vvvv",
    )
    got_w = swap_ends(pay_w)
    (pay_b,) = run(
        functools.partial(join_kernel), away, block, outs=[real(11, nx, nz)], specs="vv"
    )
    got_b = swap(pay_b, "by", 1)
    cells = nx * ny * nz // blocks
    results = [real(blocks, cells), real(3, blocks, cells)]
    rho, vel, pay_a = run(
        functools.partial(moments_kernel), moves, part, got_b, got_w,
        outs=results + [real(11, nx, nz)],
        specs="vvvv",
        scratch=room((8, nx * ROWS, nz)),
    )
    got_a = swap(pay_a, "by", 0)
    return tuple(
        run(
            functools.partial(place_kernel), moves, rho, vel, away, got_a, got_b, got_w,
            outs=results, specs="vvvvvvv", kept=False,
            scratch=room((8, nx, nz), yedge, (4, blocks, cells)) + [pltpu.SemaphoreType.DMA((4,))],
        )
    )


def solution(mesh):
    in_specs = (P(None, "bx", "by", None), P(), P(("bx", "by")))
    out_specs = (P(("bx", "by"), None), P(None, ("bx", "by"), None))
    return jax.shard_map(
        on_device, mesh=mesh, in_specs=in_specs, out_specs=out_specs, check_vma=False
    )
```

```python
import functools
import math

import jax
import jax.numpy as jnp
import numpy as np
from jax import lax
from jax.experimental import pallas as pl
from jax.experimental.pallas import tpu as pltpu
from jax.sharding import PartitionSpec as P

tau_coarse = 0.56
tau_fine = 0.62
scale_to_fine = tau_fine / (2.0 * tau_coarse)
scale_to_coarse = 2.0 * tau_coarse / tau_fine
smagorinsky = 18.0 * math.sqrt(2.0) * 0.17 * 0.17
weights = (8.0 / 27, 2.0 / 27, 1.0 / 54, 1.0 / 216)
ROWS = 8
LANES = 128
VMEM_BYTES = 16 * 1024 * 1024
FACE_BYTES = 53 * 1024 * 1024


def comp(a, b, e):
    return 9 * (a + 1) + 3 * (b + 1) + (e + 1)


def face(b, e):
    return 3 * (b + 1) + (e + 1)


DIRS = [(a, b, e) for a in (-1, 0, 1) for b in (-1, 0, 1) for e in (-1, 0, 1)]
HALF = [c for c in DIRS if c > (0, 0, 0)]


def lane_block(edge):
    return lax.broadcasted_iota(jnp.int32, (ROWS, LANES), 1) // edge


def sublane():
    return lax.broadcasted_iota(jnp.int32, (ROWS, LANES), 0)


def column_level(levels, shape, blocks, dx, dy):
    count_x, count_y = shape
    ix = lax.rem(lax.axis_index("bx") + (dx + count_x), count_x)
    iy = lax.rem(lax.axis_index("by") + (dy + count_y), count_y)
    base = (ix * count_y + iy) * blocks
    line = jnp.broadcast_to(levels[pl.ds(base // LANES, 1), :], (ROWS, LANES))
    line = pltpu.roll(line, lax.rem(LANES - lax.rem(base, LANES), LANES), 1)
    return jnp.take_along_axis(line, lane_block(LANES // blocks), axis=1)


def lane_roll(tile, by):
    return tile if by == 0 else pltpu.roll(tile, by % LANES, 1)


def group_sums(get):
    total, diff, quad = {}, {}, {}
    for b in (-1, 0, 1):
        low, mid, high = (get(b, e) for e in (-1, 0, 1))
        quad[b] = low + high
        total[b] = quad[b] + mid
        diff[b] = high - low
    both = total[-1] + total[1]
    return (
        both + total[0],
        total[1] - total[-1],
        both,
        diff[-1] + diff[0] + diff[1],
        diff[1] - diff[-1],
        quad[-1] + quad[0] + quad[1],
    )


def add_sums(first, second):
    return tuple(p + q for p, q in zip(first, second))


def collide(groups, get, fine, everywhere, factor, put, dirs=None):
    low, mid, high = (groups[a] for a in (-1, 0, 1))
    ends = add_sums(low, high)
    rho, jy, pyy, jz, pyz, pzz = add_sums(ends, mid)
    pxx = ends[0]
    jx, pxy, pxz = high[0] - low[0], high[1] - low[1], high[3] - low[3]
    inv = 1.0 / rho
    ux, uy, uz = jx * inv, jy * inv, jz * inv
    third = rho * (1.0 / 3.0)
    pxx = pxx - third - jx * ux
    pyy = pyy - third - jy * uy
    pzz = pzz - third - jz * uz
    pxy = pxy - jx * uy
    pxz = pxz - jx * uz
    pyz = pyz - jy * uz
    norm = jnp.sqrt(
        pxx * pxx + pyy * pyy + pzz * pzz + 2.0 * (pxy * pxy + pxz * pxz + pyz * pyz)
    )
    base_time = jnp.where(fine, tau_fine, tau_coarse)
    tau = 0.5 * (base_time + jnp.sqrt(base_time * base_time + smagorinsky * norm * inv))
    keep = 1.0 - 1.0 / tau
    if not everywhere:
        keep = jnp.where(fine, keep, 1.0)
    base = 1.0 - 1.5 * (ux * ux + uy * uy + uz * uz)
    scaled = [rho * w for w in weights]
    rest = [s * base for s in scaled]
    vx, vy, vz = 3.0 * ux, 3.0 * uy, 3.0 * uz
    vel = {(0, 0, 1): vz, (0, 1, 0): vy, (1, 0, 0): vx}
    vel[0, 1, 1], vel[0, 1, -1] = vy + vz, vy - vz
    vel[1, 0, 1], vel[1, 0, -1] = vx + vz, vx - vz
    vel[1, 1, 0], vel[1, -1, 0] = vx + vy, vx - vy
    for b in (-1, 1):
        for e in (-1, 1):
            vel[1, b, e] = vel[1, b, 0] + (vz if e > 0 else -vz)

    def emit(c, balance):
        if dirs is not None and c not in dirs:
            return
        gain = keep if c == (0, 0, 0) else keep * factor(c)
        put(c, balance + gain * (get(c) - balance))

    emit((0, 0, 0), rest[0])
    for c in HALF:
        n = sum(abs(k) for k in c)
        odd = scaled[n] * vel[c]
        even = rest[n] + 0.5 * odd * vel[c]
        emit(c, even + odd)
        emit(tuple(-k for k in c), even - odd)


def sums_of(get):
    return {a: group_sums(lambda b, e, a=a: get((a, b, e))) for a in (-1, 0, 1)}


def level_factor(here, there_rows, e):
    scale = jnp.where(here == 1, scale_to_coarse, scale_to_fine)
    return jnp.where(lane_roll(there_rows, -e) != here, scale, 1.0)


def fill_factors(marks, table):
    row = sublane()
    for k, (own, dx) in enumerate(((0, -1), (0, 0), (0, 1), (-1, 0), (1, 0))):
        here = marks[own + 1, 1, :, :]
        near = [marks[dx + 1, b, :, :] for b in range(3)]
        for e in (-1, 0, 1):
            plain = level_factor(here, near[1], e)
            for b in (-1, 0, 1):
                low, high = plain, plain
                if b == -1:
                    low = jnp.where(row == 0, level_factor(here, near[0], e), plain)
                if b == 1:
                    high = jnp.where(row == ROWS - 1, level_factor(here, near[2], e), plain)
                table[k, b + 1, e + 1, 0:8, :] = low
                table[k, b + 1, e + 1, 8:16, :] = high


def x_side(a, x, last):
    if a == 0:
        return 1
    return jnp.where(x == (0 if a < 0 else last), 1 + a, 1)


def store_by_parity(odd, first, second, up, down):
    @pl.when(odd == 0)
    def _():
        if first is not None:
            first[...] = up[...]
        second[...] = down[...]

    @pl.when(odd == 1)
    def _():
        if first is not None:
            first[...] = down[...]
        second[...] = up[...]


def fetch_kernel(f, high, low, sems):
    ny = f.shape[2]
    copies = [
        pltpu.make_async_copy(f.at[:, :, ny - 1, :], high, sems.at[0]),
        pltpu.make_async_copy(f.at[:, :, 0, :], low, sems.at[1]),
    ]
    for copy in copies:
        copy.start()
    for copy in copies:
        copy.wait()


def face_kernel(shape, blocks, levels, high, low, marks, pay_a, pay_b, up, down):
    nx = high.shape[1]
    for dx in (-1, 0, 1):
        for dy in (-1, 0, 1):
            marks[dx + 1, dy + 1, :, :] = column_level(levels, shape, blocks, dx, dy)
    here = marks[1, 1, :, :]
    row = sublane()
    for b, rows, pay in ((1, high, up), (-1, low, down)):
        near = [marks[dx, b + 1, :, :] for dx in range(3)]
        plain = {e: level_factor(here, near[1], e) for e in (-1, 0, 1)}
        for x in range(0, nx, ROWS):

            def get(c):
                return rows[comp(*c), x : x + ROWS, :]

            def factor(c):
                if c[0] == -1 and x == 0:
                    return jnp.where(row == 0, level_factor(here, near[0], c[2]), plain[c[2]])
                if c[0] == 1 and x + ROWS == nx:
                    return jnp.where(
                        row == ROWS - 1, level_factor(here, near[2], c[2]), plain[c[2]]
                    )
                return plain[c[2]]

            def put(c, value):
                pay[face(c[0], c[2]), x : x + ROWS, :] = value

            collide(
                sums_of(get), get, here == 1, False, factor, put, [c for c in DIRS if c[1] == b]
            )
    store_by_parity(lax.rem(lax.axis_index("by"), 2), pay_a, pay_b, up, down)


def first_collide(f, table, fine, x, near, put):
    for h in (0, 1):
        rows = slice(8 * h, 8 * h + 8)

        def get(c):
            return f[comp(*c), x, rows, :]

        def factor(c):
            return table[near(c[0]), c[1] + 1, c[2] + 1, rows, :]

        collide(sums_of(get), get, fine, False, factor, lambda c, value: put(c, rows, value))


def first_kernel(marks, f, table, out, calm):
    fill_factors(marks, table)
    fine = marks[1, 1, :, :] == 1
    nx = f.shape[1]
    for n, (x, a) in enumerate(((0, -1), (nx - 1, 1))):
        for h in (0, 1):
            rows = slice(8 * h, 8 * h + 8)

            def get(c):
                return f[comp(*c), x, rows, :]

            def put(c, value):
                calm[n, face(c[1], c[2]), rows, :] = value

            collide(
                sums_of(get), get, fine, True,
                lambda c: table[1 + c[0], c[1] + 1, c[2] + 1, rows, :],
                put, [c for c in DIRS if c[0] == a],
            )

    def layer(x, carry):
        def near(a):
            return 1 if a == 0 else jnp.where(x == (0 if a < 0 else nx - 1), 1 + a, 1)

        def put(c, rows, value):
            out[comp(*c), x, rows, :] = value

        first_collide(f, table, fine, x, near, put)
        return carry

    lax.fori_loop(0, nx, layer, 0)


def shifted_read(g, above, below, row, c, x, h):
    a, b, e = c
    i = comp(a, b, e)
    if b == 0:
        tile = g[i, x, 8 * h : 8 * h + 8, :]
    elif b == 1:
        if h == 1:
            tile = g[i, x, 7:15, :]
        else:
            tile = pltpu.roll(g[i, x, 0:8, :], 1, 0)
            tile = jnp.where(row == 0, below[face(a, e), pl.ds(x, 1), :], tile)
    else:
        if h == 0:
            tile = g[i, x, 1:9, :]
        else:
            tile = pltpu.roll(g[i, x, 8:16, :], 7, 0)
            tile = jnp.where(row == 7, above[face(a, e), pl.ds(x, 1), :], tile)
    return lane_roll(tile, e)


def load_by_parity(odd, first, second, above, below):
    @pl.when(odd == 0)
    def _():
        above[...] = first[...]
        below[...] = second[...]

    @pl.when(odd == 1)
    def _():
        above[...] = second[...]
        below[...] = first[...]


def side_kernel(marks, f, g, calm, got_a, got_b, pay_a, pay_b, above, below, up, down):
    load_by_parity(lax.rem(lax.axis_index("by"), 2), got_a, got_b, above, below)
    fine = marks[1, 1, :, :] == 1
    row = sublane()
    nx = f.shape[1]
    for n, (ad, x, pay) in enumerate(((-1, 0, down), (1, nx - 1, up))):
        for h in (0, 1):
            rows = slice(8 * h, 8 * h + 8)

            def flat(b, e):
                return shifted_read(g, above, below, row, (0, b, e), x, h)

            for b in (-1, 0, 1):
                for e in (-1, 0, 1):
                    c, j = (ad, b, e), face(b, e)
                    pay[j, rows, :] = shifted_read(g, above, below, row, c, x, h)
                    moved = shifted_read(g, above, below, row, c, x - ad, h)
                    pay[9 + j, rows, :] = jnp.where(fine, moved, calm[n, j, rows, :])
            for m, part in enumerate(group_sums(flat)):
                pay[18 + m, rows, :] = part
    store_by_parity(lax.rem(lax.axis_index("bx"), 2), pay_a.at[pl.ds(0, 24)], pay_b, up, down)


def second_collide(groups, get, fine, factor, put, dirs, known=None):
    made = {}

    def keep(c, value):
        made[c] = value if known is None else jnp.where(fine, value, known(c))

    collide(groups, get, fine, True, factor, keep, dirs)
    for a in (-1, 0, 1):
        if dirs is not None and (a, 0, 0) not in dirs:
            continue
        for b in (-1, 0, 1):
            plus = lane_roll(made[a, b, 1], 1)
            minus = lane_roll(made[a, b, -1], -1)
            put(a, b, made[a, b, 0] + (plus + minus), plus - minus)


def gather_layer(sums, row, put, up, down):
    total, cross, along = {}, {}, {}
    for b in (-1, 0, 1):
        for h in (0, 1):
            low, mid, high = (sums(a, b, 0, h) for a in (1, 0, -1))
            total[b, h] = low + mid + high
            cross[b, h] = low - high
            along[b, h] = sums(1, b, 1, h) + sums(0, b, 1, h) + sums(-1, b, 1, h)
    for n, part in enumerate((total, cross, along)):
        up(n, part[1, 1][7:8])
        down(n, part[-1, 0][0:1])
        rise = [pltpu.roll(part[1, h], 1, 0) for h in (0, 1)]
        fall = [pltpu.roll(part[-1, h], 7, 0) for h in (0, 1)]
        rise = [jnp.where(row == 0, 0.0, rise[0]), jnp.where(row == 0, rise[0], rise[1])]
        fall = [jnp.where(row == 7, fall[1], fall[0]), jnp.where(row == 7, 0.0, fall[1])]
        for h in (0, 1):
            put((0, 1, 3)[n], h, part[0, h] + rise[h] + fall[h])
            if n == 0:
                put(2, h, rise[h] - fall[h])


def turns():
    row = sublane()
    reflect = (lane_block(LANES // ROWS) - row) & (ROWS - 1)
    turn = (lane_block(1) + row * (LANES // ROWS)) & (LANES - 1)
    return reflect, turn


def block_rows(tile, reflect, turn):
    tile = pltpu.roll(tile, 0, 1, stride=LANES // ROWS, stride_axis=0)
    tile = jnp.take_along_axis(tile, reflect, axis=0)
    return jnp.take_along_axis(tile, turn, axis=1)


def leaving(slots, blocks, step):
    here = lax.axis_index("bx") * lax.axis_size("by") + lax.axis_index("by")
    which, theirs = jnp.int32(-1), jnp.int32(0)
    for k in range(blocks):
        goes = slots[k] // blocks == here + step
        which = jnp.where(goes, k, which)
        theirs = jnp.where(goes, lax.rem(slots[k], blocks), theirs)
    return which, theirs


def inner_kernel(
    blocks, slots, marks, f, g, table, ya, yb, tie, sums, made, up, down, moves,
    above, below, state,
):
    load_by_parity(lax.rem(lax.axis_index("by"), 2), ya, yb, above, below)
    for n, step in enumerate((1, -1)):
        which, theirs = leaving(slots, blocks, step)
        moves[n, :, :] = jnp.full((ROWS, LANES), which, jnp.int32)
        moves[2 + n, :, :] = jnp.full((ROWS, LANES), theirs, jnp.int32)
    fine = marks[1, 1, :, :] == 1
    row = sublane()
    reflect, turn = turns()
    nx = f.shape[1]

    def second(x, carry):
        for h in (0, 1):
            rows = slice(8 * h, 8 * h + 8)

            def moved(c):
                tile = shifted_read(g, above, below, row, c, x - c[0], h)
                tile = jnp.where(fine, tile, f[comp(*c), x, rows, :])
                state[comp(*c), rows, :] = tile
                return tile

            def put(a, b, total, along):
                sums[a + 1, b + 1, 0, x, rows, :] = total
                sums[a + 1, b + 1, 1, x, rows, :] = along

            second_collide(
                sums_of(moved),
                lambda c: state[comp(*c), rows, :],
                fine,
                lambda c: table[1, c[1] + 1, c[2] + 1, rows, :],
                put,
                None,
            )
        return carry

    lax.fori_loop(1, nx - 1, second, 0)

    def gather(x, carry):
        def put(n, h, tile):
            made[2 * n + h, pl.ds(x * ROWS, ROWS), :] = block_rows(tile, reflect, turn)

        def put_up(n, value):
            up[n, pl.ds(x, 1), :] = value

        def put_down(n, value):
            down[n, pl.ds(x, 1), :] = value

        gather_layer(
            lambda a, b, q, h: sums[a + 1, b + 1, q, x - a, 8 * h : 8 * h + 8, :],
            row, put, put_up, put_down,
        )
        return carry

    lax.fori_loop(2, nx - 2, gather, 0)


def outer_kernel(
    marks, f, g, table, ya, yb, xa, xb, sums, in_up, in_down,
    part, pay, away, above, below, right, left, state, ends, up, down,
):
    load_by_parity(lax.rem(lax.axis_index("by"), 2), ya, yb, above, below)
    load_by_parity(lax.rem(lax.axis_index("bx"), 2), xa.at[pl.ds(0, 24)], xb, right, left)
    fine = {dx: marks[dx + 1, 1, :, :] == 1 for dx in (-1, 0, 1)}
    row = sublane()
    reflect, turn = turns()
    nx = f.shape[1]
    hold = {-1: 0, 0: 1, nx - 1: 2, nx: 3}
    for side, x, k, got in ((-1, 0, 3, left), (1, nx - 1, 4, right)):
        for h in (0, 1):
            rows = slice(8 * h, 8 * h + 8)

            def keep(slot):
                def put(a, b, total, along):
                    ends[a + 1, b + 1, 0, slot, rows, :] = total
                    ends[a + 1, b + 1, 1, slot, rows, :] = along

                return put

            def read(c, x):
                return shifted_read(g, above, below, row, c, x, h)

            def moved(c):
                a, b, e = c
                if a == -side:
                    tile = got[face(b, e), rows, :]
                else:
                    tile = read(c, x - a)
                tile = jnp.where(fine[0], tile, f[comp(*c), x, rows, :])
                state[comp(*c), rows, :] = tile
                return tile

            second_collide(
                sums_of(moved),
                lambda c: state[comp(*c), rows, :],
                fine[0],
                lambda c: table[1, c[1] + 1, c[2] + 1, rows, :],
                keep(hold[x]),
                [c for c in DIRS if c[0] != side],
            )

            def toward(c):
                return got[9 + face(c[1], c[2]), rows, :]

            second_collide(
                {
                    side: group_sums(lambda b, e: read((side, b, e), x)),
                    0: tuple(got[18 + n, rows, :] for n in range(6)),
                    -side: group_sums(lambda b, e: toward((-side, b, e))),
                },
                toward,
                fine[side],
                lambda c: table[k, c[1] + 1, c[2] + 1, rows, :],
                keep(hold[x + side]),
                [c for c in DIRS if c[0] == -side],
                toward,
            )
    up[...] = in_up[...]
    down[...] = in_down[...]
    for m, x in enumerate((0, 1, nx - 2, nx - 1)):

        def fetch(a, b, q, h):
            rows = slice(8 * h, 8 * h + 8)
            if x - a in hold:
                return ends[a + 1, b + 1, q, hold[x - a], rows, :]
            return sums[a + 1, b + 1, q, x - a, rows, :]

        def put(n, h, tile):
            part[2 * n + h, ROWS * m : ROWS * m + ROWS, :] = tile

        def put_up(n, value):
            up[n, x : x + 1, :] = value

        def put_down(n, value):
            down[n, x : x + 1, :] = value

        gather_layer(fetch, row, put, put_up, put_down)
    for edge in (up, down):
        for n in range(3):
            for x in range(0, nx, ROWS):
                rows = slice(x, x + ROWS)
                edge[n, rows, :] = block_rows(edge[n, rows, :], reflect, turn)
    odd = lax.rem(lax.axis_index("by"), 2)
    store_by_parity(odd, pay.at[pl.ds(0, 3)], pay.at[pl.ds(3, 3)], up, down)
    store_by_parity(odd, None, away, up, down)


def turn_kernel(part, out):
    reflect, turn = turns()
    for n in range(part.shape[0]):
        for m in range(4):
            rows = slice(ROWS * m, ROWS * m + ROWS)
            out[n, rows, :] = block_rows(part[n, rows, :], reflect, turn)


def add_crossed(made, crossed, top):
    nx = crossed.shape[1]
    width = LANES // ROWS
    spot = top * (ROWS - 1)
    sign = jnp.where(top == 1, -1.0, 1.0)
    mask = lane_block(width) == spot
    for x in range(nx):
        rows = slice(ROWS * x, ROWS * x + ROWS)
        first = x // ROWS * ROWS
        shift = lax.rem(width * (spot - x % ROWS) + LANES, LANES)
        total, cross, along = (
            jnp.where(mask, pltpu.roll(crossed[n, first : first + ROWS, :], shift, 1), 0.0)
            for n in range(3)
        )
        for n, more in enumerate((total, cross, sign * total, along)):
            made[2 * n + top, rows, :] += more


def pack_block(made, pay, start, which):
    for n in range(8):
        pay[start + n, :, :] = made[n, pl.ds(which, pay.shape[1], stride=ROWS), :]


def number(tile):
    return jnp.maximum(jnp.max(tile), 0)


def pack_kernel(moves, inner, outer, got, made, block, pay_w):
    iy = lax.axis_index("by")
    odd = lax.rem(iy, 2)
    which = number(moves[1 - odd, :, :])
    nx = got.shape[1]
    low, high = ROWS * 2, ROWS * (nx - 2)
    made[:, 0:low, :] = outer[:, 0:low, :]
    made[:, low:high, :] = inner[:, low:high, :]
    made[:, high:, :] = outer[:, low:, :]
    add_crossed(made, got, 1 - odd)
    pack_block(made, block, 0, which)
    end = jnp.logical_or(iy == 0, iy == lax.axis_size("by") - 1)

    @pl.when(end)
    def _():
        pay_w[0:8, :, :] = block[...]

    @pl.when(jnp.logical_not(end))
    def _():
        pay_w[0:3, :, :] = got[3:6, :, :]


def join_kernel(first, second, out):
    out[0 : first.shape[0], :, :] = first[...]
    out[first.shape[0] :, :, :] = second[...]


def moments_kernel(moves, part, got_b, got_w, rho_out, vel_out, pay_a, made):
    odd = lax.rem(lax.axis_index("by"), 2)
    nx = got_b.shape[1]
    which = number(moves[odd, :, :])
    made[...] = part[...]
    add_crossed(made, got_b, odd)
    for x in range(nx):
        rows = slice(ROWS * x, ROWS * x + ROWS)
        for h in (0, 1):
            rho = made[h, rows, :]
            inv = 1.0 / rho
            lanes = slice((2 * x + h) * LANES, (2 * x + h + 1) * LANES)
            rho_out[:, lanes] = rho
            for n in range(1, 4):
                tile = made[2 * n + h, rows, :] * inv
                made[2 * n + h, rows, :] = tile
                vel_out[n - 1, :, lanes] = tile
    pack_block(made, pay_a, 0, which)
    pay_a[8:11, :, :] = got_w[0:3, :, :]


def place_kernel(moves, rho, vel, away, got_a, got_b, got_w, rho_out, vel_out, block, crossed, made, sems):
    iy = lax.axis_index("by")
    odd = lax.rem(iy, 2)
    end = jnp.logical_or(iy == 0, iy == lax.axis_size("by") - 1)

    @pl.when(end)
    def _():
        block[...] = got_w[0:8, :, :]
        crossed[...] = got_a[8:11, :, :]

    @pl.when(jnp.logical_not(end))
    def _():
        block[...] = got_b[3:11, :, :]
        crossed[...] = away[...]

    row = sublane()
    width = LANES // ROWS
    top = 1 - odd
    sign = jnp.where(top == 1, -1.0, 1.0)
    mask = lane_block(width) == top * (ROWS - 1)
    spread = row * width + (lane_block(1) & (width - 1))
    theirs = jnp.maximum(moves[3 - odd, :, :], 0)
    for first in range(0, block.shape[1], ROWS):
        rows = slice(first, first + ROWS)
        extra = []
        for n in range(3):
            line = jnp.take_along_axis(crossed[n, rows, :], theirs, axis=0)
            extra.append(jnp.where(mask, jnp.take_along_axis(line, spread, axis=1), 0.0))
        total, cross, along = extra
        for n, more in enumerate((total, cross, sign * total, along)):
            block[2 * n + top, rows, :] += more
        for h in (0, 1):
            inv = 1.0 / block[h, rows, :]
            for n in range(1, 4):
                block[2 * n + h, rows, :] *= inv
    near = row == moves[odd, :, :]
    far = row == moves[1 - odd, :, :]
    copies = []
    for n in range(4):
        for x in range(block.shape[1]):
            for h in (0, 1):
                lanes = slice((2 * x + h) * LANES, (2 * x + h + 1) * LANES)
                k = 2 * n + h
                tile = rho[:, lanes] if n == 0 else vel[n - 1, :, lanes]
                tile = jnp.where(near, got_a[k, x : x + 1, :], tile)
                made[n, :, lanes] = jnp.where(far, block[k, x : x + 1, :], tile)
        target = rho_out if n == 0 else vel_out.at[n - 1]
        copies.append(pltpu.make_async_copy(made.at[n], target, sems.at[n]))
        copies[n].start()
    for copy in copies:
        copy.wait()


def swap(value, axis, odd):
    count_x, count_y = lax.axis_size("bx"), lax.axis_size("by")
    pairs = []
    if axis == "by":
        for x in range(count_x):
            for y in range(odd, count_y, 2):
                pairs.append((x * count_y + y, x * count_y + (y + 1) % count_y))
    else:
        for y in range(count_y):
            for x in range(odd, count_x, 2):
                pairs.append((x * count_y + y, (x + 1) % count_x * count_y + y))
    pairs = pairs + [(b, a) for a, b in pairs]
    return lax.ppermute(value, ("bx", "by"), pairs)


def swap_ends(value):
    count_x, count_y = lax.axis_size("bx"), lax.axis_size("by")
    pairs = []
    for x in range(count_x):
        here, after = x * count_y, (x + 1) * count_y
        if x + 1 < count_x:
            pairs += [(after - 1, after), (after, after - 1)]
            pairs += [(here + 1, after + 1), (after + count_y - 2, after - 2)]
        pairs += [(here + y, here + (y ^ 1)) for y in range(2, count_y - 2)]
    pairs += [(0, 1), (after - 1, after - 2)]
    pairs += [(after - count_y + 1, after - 1), (count_y - 2, 0)]
    return lax.ppermute(value, ("bx", "by"), pairs)


def call(kernel, outs, specs, scratch, name, work, limit, kept):
    space = {"v": pltpu.VMEM, "s": pltpu.SMEM, "h": pltpu.HBM, "a": pl.ANY}
    return pl.pallas_call(
        kernel,
        out_shape=outs,
        in_specs=[pl.BlockSpec(memory_space=space[k]) for k in specs],
        out_specs=[pl.BlockSpec(memory_space=pltpu.VMEM if kept else pl.ANY)] * len(outs),
        scratch_shapes=scratch,
        compiler_params=pltpu.CompilerParams(vmem_limit_bytes=limit),
        cost_estimate=pl.CostEstimate(
            flops=work * 2000000, bytes_accessed=work * 1000000, transcendentals=0
        ),
        name=name,
    )


def on_device(populations, block_level, new_slot):
    shape = (lax.axis_size("bx"), lax.axis_size("by"))
    blocks = new_slot.shape[0]
    _, nx, ny, nz = populations.shape
    yface, xface, yedge = (9, nx, nz), (24, ny, nz), (3, nx, nz)
    tile = (ROWS, nz)

    def real(*dims):
        return jax.ShapeDtypeStruct(dims, jnp.float32)

    def whole(*dims):
        return jax.ShapeDtypeStruct(dims, jnp.int32)

    def room(*shapes):
        return [pltpu.VMEM(dims, jnp.float32) for dims in shapes]

    def run(kernel, *args, outs, specs, scratch=(), work=1, limit=VMEM_BYTES, kept=True):
        def body(*refs):
            kernel(*refs)

        return call(body, outs, specs, scratch, kernel.func.__name__[:-7], work, limit, kept)(*args)

    high, low = run(
        functools.partial(fetch_kernel), populations,
        outs=[real(27, nx, nz)] * 2, specs="h", scratch=[pltpu.SemaphoreType.DMA((2,))],
        limit=FACE_BYTES,
    )
    marks, pay_a, pay_b = run(
        functools.partial(face_kernel, shape, blocks),
        block_level.reshape(block_level.shape[0] // nz, nz), high, low,
        outs=[whole(3, 3, *tile), real(*yface), real(*yface)],
        specs="vvv", scratch=room(yface, yface),
    )
    ya, yb = swap(pay_a, "by", 0), swap(pay_b, "by", 1)
    table, g, calm = run(
        functools.partial(first_kernel), marks, populations,
        outs=[real(5, 3, 3, ny, nz), real(*populations.shape), real(2, 9, ny, nz)],
        specs="vv", work=3,
    )
    pay_a, pay_b = run(
        functools.partial(side_kernel), marks, populations, g, calm, ya, yb,
        outs=[real(25, ny, nz), real(*xface)], specs="vvvvvv", scratch=room(yface, yface, xface, xface),
    )
    xa, xb = swap(pay_a, "bx", 0), swap(pay_b, "bx", 1)
    sums, inner, up, down, moves = run(
        functools.partial(inner_kernel, blocks),
        new_slot, marks, populations, g, table, ya, yb, pay_a,
        outs=[
            real(3, 3, 2, nx, ny, nz), real(8, nx * ROWS, nz), real(*yedge), real(*yedge),
            whole(4, *tile),
        ],
        specs="svvvvvva",
        scratch=room(yface, yface, (27, ny, nz)),
        work=10,
    )
    part, pay_a, away = run(
        functools.partial(outer_kernel),
        marks, populations, g, table, ya, yb, xa, xb, sums, up, down,
        outs=[real(8, 4 * ROWS, nz), real(6, nx, nz), real(*yedge)],
        specs="vvvvvvvvvvv",
        scratch=room(
            yface, yface, xface, xface, (27, ny, nz), (3, 3, 2, 4, ny, nz), yedge, yedge
        ),
    )
    got_a = swap(pay_a, "by", 0)
    (outer,) = run(
        functools.partial(turn_kernel), part, outs=[real(8, 4 * ROWS, nz)], specs="v"
    )
    part, block, pay_w = run(
        functools.partial(pack_kernel), moves, inner, outer, got_a,
        outs=[real(8, nx * ROWS, nz), real(8, nx, nz), real(8, nx, nz)], specs="vvvv",
    )
    got_w = swap_ends(pay_w)
    (pay_b,) = run(
        functools.partial(join_kernel), away, block, outs=[real(11, nx, nz)], specs="vv"
    )
    got_b = swap(pay_b, "by", 1)
    cells = nx * ny * nz // blocks
    results = [real(blocks, cells), real(3, blocks, cells)]
    rho, vel, pay_a = run(
        functools.partial(moments_kernel), moves, part, got_b, got_w,
        outs=results + [real(11, nx, nz)],
        specs="vvvv",
        scratch=room((8, nx * ROWS, nz)),
    )
    got_a = swap(pay_a, "by", 0)
    return tuple(
        run(
            functools.partial(place_kernel), moves, rho, vel, away, got_a, got_b, got_w,
            outs=results, specs="vvvvvvv", kept=False,
            scratch=room((8, nx, nz), yedge, (4, blocks, cells)) + [pltpu.SemaphoreType.DMA((4,))],
        )
    )


def solution(mesh):
    in_specs = (P(None, "bx", "by", None), P(), P(("bx", "by")))
    out_specs = (P(("bx", "by"), None), P(None, ("bx", "by"), None))
    return jax.shard_map(
        on_device, mesh=mesh, in_specs=in_specs, out_specs=out_specs, check_vma=False
    )
```
